256 devices in a mesh: gx: 16 (over x, y), gy: 4 (over z_lo, core), gz: 4 (over z_hi).
Axes of the slice: x: 4, y: 4, z: 8 (z_hi: 4, z_lo: 2; z = z_hi * 2 + z_lo), core: 2. Of those that a mesh axis runs over, the one named last changes fastest.
Arguments:
- iterate: float32 [4194304], P(('gx', 'gy', 'gz')), may hold values from -6 to 6
- residual: float32 [4194304], P(('gx', 'gy', 'gz'))
- direction: float32 [4194304], P(('gx', 'gy', 'gz'))
- noise: float32 [4194304], P(('gx', 'gy', 'gz')), may hold values from 0.1 to 1
- stencil_base: int32 [3, 32768], P(None, ('gx', 'gy', 'gz')), may hold values from 0 to 508, as said below
- interp_weights: float32 [12, 4194304], P(None, ('gx', 'gy', 'gz')), may hold values from -0.25 to 1
- tile_counts: int32 [32768], P(('gx', 'gy', 'gz')), may hold values from 42 to 128, as said below
- reach: float32 [3], replicated, may hold values from 1.5 to 6
Outputs:
- new_iterate: float32 [4194304], P(('gx', 'gy', 'gz'))
- new_residual: float32 [4194304], P(('gx', 'gy', 'gz'))
- new_direction: float32 [4194304], P(('gx', 'gy', 'gz'))
The draws below stay inside these ranges and needn't reach their ends.
Inputs may be any that keep to these rules, and one draw needn't show every extreme that they name: Along each dimension the four stencil cells lie inside the grid, and stencil_base + 1 lies in the block of 32 x 64 x 128 cells of the device that holds the tile (devices taken in the order of the tiles' shards, blocks in the grid's order). `tile_counts`: every device has a tile with all 128 slots live.
All inputs are finite; a program needn't handle non-finite values.
Results may differ from the reference program's by a relative error of at most 0.000059.
Values sent between devices are 32-bit elements; how exact they have to be, the bound alone decides.
A program may use at most 192 MiB of HBM per device.

```python
import math
import jax
import jax.numpy as jnp
from jax import lax

NX = 512
NY = 256
NZ = 512
SLOT = 128
TILES = 128
CX = 32
CY = 64
CZ = 128
TILE_ROWS = 32768
READINGS = 4194304
N_GY = 4
N_GZ = 4
DEVICES = 256


def device_scale():
    owner = jnp.arange(READINGS, dtype=jnp.int32) // (TILES * SLOT)
    return jnp.exp(jnp.log(3.0) * owner.astype(jnp.float32) / max(DEVICES - 1, 1))


def draw_residual(key, part):
    key = jax.random.fold_in(key, 3)
    values = jax.random.normal(key, (READINGS,), jnp.float32)
    return values * device_scale()


def draw_direction(key, part):
    key = jax.random.fold_in(key, 5)
    values = jax.random.normal(key, (READINGS,), jnp.float32)
    return values * device_scale()


def draw_stencil_base(key, part):
    key = jax.random.fold_in(key, 11)
    owner = jnp.arange(TILE_ROWS, dtype=jnp.int32) // TILES
    block_x = owner // (N_GY * N_GZ)
    block_y = owner // N_GZ % N_GY
    block_z = owner % N_GZ
    keys = jax.random.split(key, 3)
    base_x = block_x * CX - 1 + jax.random.randint(keys[0], (TILE_ROWS,), 0, CX)
    base_y = block_y * CY - 1 + jax.random.randint(keys[1], (TILE_ROWS,), 0, CY)
    base_z = block_z * CZ - 1 + jax.random.randint(keys[2], (TILE_ROWS,), 0, CZ)
    base_x = jnp.clip(base_x, 0, NX - 4)
    base_y = jnp.clip(base_y, 0, NY - 4)
    base_z = jnp.clip(base_z, 0, NZ - 4)
    return jnp.stack([base_x, base_y, base_z]).astype(jnp.int32)


def draw_tile_counts(key, part):
    key = jax.random.fold_in(key, 17)
    keys = jax.random.split(key, 2)
    counts = jax.random.randint(keys[0], (TILE_ROWS,), SLOT // 3, SLOT + 1)
    chosen = jax.random.randint(keys[1], (DEVICES,), 0, TILES)
    full_tile = jnp.arange(TILE_ROWS, dtype=jnp.int32) % TILES == jnp.repeat(chosen, TILES)
    return jnp.where(full_tile, SLOT, counts).astype(jnp.int32)


def steps_of(rng, dims, cuts, smallest, largest):
    gain, own = 1.0, jax.random.fold_in(rng, 6)
    for position, blocks in cuts:
        steps = jnp.exp(jax.random.uniform(jax.random.fold_in(own, position), (blocks,), jnp.float32, smallest / len(cuts), largest / len(cuts)))
        gain = gain * jnp.repeat(steps, dims[position] // blocks).reshape([-1 if axis == position else 1 for axis in range(len(dims))])
    return gain


def gaussian(rng, extent, spread, limit, cuts=(), kind=jnp.bfloat16):
    result = spread * jax.random.normal(rng, extent, jnp.float32)
    if cuts:
        result = result * steps_of(rng, extent, cuts, -0.22, 0.18)
    return jnp.clip(result, -limit, limit).astype(kind)


def setup_inputs(seed: int = 0) -> dict:
    streams_of = jax.random.split(jax.random.key(seed), 9)
    return {
        "iterate": gaussian(streams_of[0], (READINGS,), 1.0, 6.0, ((0, 256),), jnp.float32),
        "residual": draw_residual(jax.random.fold_in(streams_of[8], 71), 0),
        "direction": draw_direction(jax.random.fold_in(streams_of[8], 71), 0),
        "noise": jnp.clip(jnp.exp(math.log(1.0) - 2.3025851 * jax.random.uniform(streams_of[3], (READINGS,), jnp.float32) ** steps_of(streams_of[3], (READINGS,), ((0, 256),), -0.2, 0.2)), 0.1, 1.0),
        "stencil_base": draw_stencil_base(jax.random.fold_in(streams_of[8], 71), 0),
        "interp_weights": jnp.clip(-0.25 + 1.25 * jax.random.uniform(streams_of[5], (12, READINGS), jnp.float32) ** steps_of(streams_of[5], (12, READINGS), ((1, 256),), -0.2, 0.2), -0.25, 1.0),
        "tile_counts": draw_tile_counts(jax.random.fold_in(streams_of[8], 71), 0),
        "reach": jnp.clip(jnp.exp(jax.random.uniform(streams_of[7], (3,), jnp.float32, math.log(1.5), math.log(6.0))), 1.5, 6.0),
    }


HIGHEST = lax.Precision.HIGHEST

def toeplitz_factor(count, length):
    place = jnp.arange(count, dtype=jnp.float32)
    distance = jnp.abs(place[:, None] - place[None, :])
    return jnp.exp(-distance / length) / jnp.sqrt(length)

def spread_values(values, reading_base, interp_weights):
    flat_grid = jnp.zeros((NX * NY * NZ,), jnp.float32)
    for first in range(4):
        for second in range(4):
            for third in range(4):
                index = ((reading_base[0] + first) * NY + reading_base[1] + second) * NZ + reading_base[2] + third
                weight = interp_weights[first] * interp_weights[4 + second] * interp_weights[8 + third]
                flat_grid = flat_grid.at[index.astype(jnp.int32)].add(weight * values)
    return flat_grid.reshape(NX, NY, NZ)

def sample_grid(flat_grid, reading_base, interp_weights):
    total = jnp.zeros(reading_base.shape[1:], jnp.float32)
    for first in range(4):
        for second in range(4):
            for third in range(4):
                index = ((reading_base[0] + first) * NY + reading_base[1] + second) * NZ + reading_base[2] + third
                weight = interp_weights[first] * interp_weights[4 + second] * interp_weights[8 + third]
                total = total + weight * flat_grid[index.astype(jnp.int32)]
    return total

def reference(iterate, residual, direction, noise, stencil_base, interp_weights, tile_counts, reach):
    slot = jnp.arange(READINGS, dtype=jnp.int32) % SLOT
    live_mask = (slot < jnp.repeat(tile_counts, SLOT)).astype(jnp.float32)
    live_dir = live_mask * direction
    live_res = live_mask * residual
    reading_base = jnp.repeat(stencil_base, SLOT, axis=1).astype(jnp.int32)
    grid = spread_values(live_dir, reading_base, interp_weights)
    factor_x = toeplitz_factor(NX, reach[0] * CX)
    factor_y = toeplitz_factor(NY, reach[1] * CY)
    factor_z = toeplitz_factor(NZ, reach[2] * CZ)
    grid = jnp.einsum('ij,jkl->ikl', factor_x, grid, precision=HIGHEST)
    grid = jnp.einsum('ij,ajl->ail', factor_y, grid, precision=HIGHEST)
    grid = jnp.einsum('ij,abj->abi', factor_z, grid, precision=HIGHEST)
    sampled = sample_grid(grid.reshape(-1), reading_base, interp_weights)
    image = live_mask * (sampled + noise * live_dir)
    norm_old = jnp.sum(live_res * live_res)
    curvature = jnp.sum(live_dir * image)
    step_size = norm_old / curvature
    new_iterate = live_mask * iterate + step_size * live_dir
    new_residual = live_res - step_size * image
    norm_new = jnp.sum(new_residual * new_residual)
    new_direction = new_residual + norm_new / norm_old * live_dir
    return (new_iterate, new_residual, new_direction)
```

```python
import functools

import jax
import jax.numpy as jnp
from jax import lax
from jax.experimental import pallas as pl
from jax.experimental.pallas import tpu as pltpu
from jax.sharding import PartitionSpec as P

F32 = jnp.float32
BF16 = jnp.bfloat16
LANES = 128
TILES = 128
NX, NY, NZ = 32, 64, 128
WX = NX + 3
TOP = 4
ROWS = 80
LIVE = 72
YT = LIVE // 8
SPARE, COPIES = 8, 20
STACKS = -(-WX * YT // COPIES)
MOMENT_STACKS, FIX_STACKS = -(-STACKS // 6), -(-STACKS // 3)
XROWS = 40
MESH = pl.DeviceIdType.MESH


def iota(shape, dim):
    return lax.broadcasted_iota(jnp.int32, shape, dim)


def full(value):
    return jnp.full((1, LANES), value, F32)


def decay(distance, length):
    return jnp.exp(-distance.astype(F32) / length)


def outgoing(kind, source, size, length):
    one = decay(full(1), length) - jnp.exp(full(1.0) / length)
    two = decay(full(2), length) - jnp.exp(full(2.0) / length)
    one, two = one[:, :1], two[:, :1]
    zero = jnp.zeros(source.shape, F32)
    if kind == 0:
        return decay(size + 1 - source, length)
    if kind == 1:
        return decay(source + 1, length)
    if kind == 2:
        return jnp.where(source == size, one, jnp.where(source == size + 1, two, zero))
    if kind == 3:
        return jnp.where(source == size + 1, one, zero)
    if kind == 4:
        return jnp.where(source == -1, two, jnp.where(source == 0, one, zero))
    return jnp.where(source == -1, one, zero)


def incoming(kind, cell, size, length):
    if kind == 0:
        return decay(cell - 1, length)
    if kind == 1:
        return decay(size - 1 - cell, length)
    target = (-1, 0, size + 1, size)[kind - 2]
    return jnp.where(cell == target, 1.0, 0.0).astype(F32)


def tile_weights(w8, low):
    along_y = jnp.where(low, pltpu.roll(w8, 4, 0), w8)
    first = jnp.where(low, w8[0:1], w8[1:2]) * along_y
    second = jnp.where(low, w8[2:3], w8[3:4]) * along_y
    return first, second, along_y


def spread_kernel(count, base, reach, w, direction, residual, grid, live_dir, live_res, live, table):
    anchor_x = lax.axis_index("gx") * NX
    anchor_y = lax.axis_index("gy") * NY
    anchor_z = lax.axis_index("gz") * NZ
    length = reach[2] * float(NZ)
    scale = 1.0 / (
        jnp.sqrt(full(reach[0] * float(NX))) * jnp.sqrt(full(reach[1] * float(NY))) * jnp.sqrt(full(length))
    )
    source = iota((136, LANES), 0) - 1
    lane = iota((136, LANES), 1)
    table[0] = decay(jnp.abs(lane - 1 - source), length) * scale
    second = jnp.where(lane < 3, decay(jnp.abs(lane + NZ - 1 - source), length), 0.0)
    for kind in range(6):
        start = SPARE + COPIES * kind
        inside = (lane >= start) & (lane < start + COPIES)
        second = jnp.where(inside, outgoing(kind, source, NZ, length), second)
    table[1] = second * scale

    def clear(x, carry):
        for half in range(2):
            grid[x, half] = jnp.zeros((ROWS, LANES), F32)
        return carry

    lax.fori_loop(0, WX, clear, 0)
    low = iota((8, LANES), 0) < 4
    slot = iota((1, LANES), 1)

    def tile(t, carry):
        at = pl.ds(pl.multiple_of(t * LANES, LANES), LANES)
        w8 = w[0:8, at]
        mask = slot < count[t]
        values = jnp.where(mask, direction[pl.ds(t, 1), :], 0.0)
        live_dir[pl.ds(t, 1), :] = values
        live_res[pl.ds(t, 1), :] = jnp.where(mask, residual[pl.ds(t, 1), :], 0.0)
        live[pl.ds(t, 1), :] = jnp.where(mask, 1.0, 0.0)
        first, second, _ = tile_weights(w8, low)
        x0 = base[0, t] - anchor_x + 1
        y0 = base[1, t] - anchor_y + 1 + TOP
        z0 = base[2, t] - anchor_z + 1
        parts = [[None, None], [None, None]]
        for e in range(4):
            along_z = w[8 + e : 9 + e, at] * values
            row = [table[half, pl.ds(z0 + e, 1), :] for half in range(2)]
            for pair, product in enumerate((first, second)):
                taps = jnp.sum(product * along_z, axis=1, keepdims=True)
                for half in range(2):
                    term = taps * row[half]
                    parts[pair][half] = term if e == 0 else parts[pair][half] + term
        for a in range(4):
            start = y0 if a % 2 == 0 else y0 - 4
            keep = low if a % 2 == 0 else jnp.logical_not(low)
            for half in range(2):
                spot = (x0 + a, half, pl.ds(start, 8), slice(None))
                grid[spot] = grid[spot] + jnp.where(keep, parts[a // 2][half], 0.0)
        return carry

    lax.fori_loop(0, TILES, tile, 0, unroll=2)


def partner(axis, me, offset, count):
    return {axis: lax.rem(me + offset, count)}


def solve_kernel(
    sizes,
    base,
    reach,
    grid,
    live_dir,
    live_res,
    live,
    noise,
    w_hbm,
    image,
    sums,
    w,
    forward,
    smooth,
    basis,
    pick_z,
    pick_x,
    z_moment,
    z_fix,
    z_moment_in,
    z_fix_in,
    y_out,
    y_moment_in,
    y_fix_in,
    x_moment,
    x_fix,
    x_fix_in,
    x_chunk_in,
    x_prefix,
    x_far,
    sampled,
    sum_out,
    sum_in_x,
    sum_mid,
    sum_in_yz,
    w_sem,
    z_sem,
    z_fix_sem,
    y_sem,
    y_fix_sem,
    x_fix_sem,
    x1_send,
    x1_recv,
    x2_send,
    x2_recv,
    sx_sem,
    syz_sem,
):
    n_gx, n_gy, n_gz = sizes
    n_yz = n_gy * n_gz
    px, py, pz = lax.axis_index("gx"), lax.axis_index("gy"), lax.axis_index("gz")
    pyz = py * n_gz + pz
    length_x, length_y, length_z = reach[0] * float(NX), reach[1] * float(NY), reach[2] * float(NZ)

    def yz_partner(offset):
        other = lax.rem(pyz + offset, n_yz)
        return {"gy": other // n_gz, "gz": lax.rem(other, n_gz)}

    barrier = pltpu.get_barrier_semaphore()
    for k in range(1, n_gx):
        pl.semaphore_signal(barrier, inc=1, device_id=partner("gx", px, k, n_gx), device_id_type=MESH)
    for k in range(1, n_yz):
        pl.semaphore_signal(barrier, inc=1, device_id=yz_partner(k), device_id_type=MESH)

    w_copy = pltpu.make_async_copy(w_hbm, w, w_sem)
    w_copy.start()

    def remote(src, dst, send, recv, device):
        return pltpu.make_async_remote_copy(
            src_ref=src, dst_ref=dst, send_sem=send, recv_sem=recv, device_id=device, device_id_type=MESH
        )

    sub = iota((8, LANES), 0)
    lane = iota((8, LANES), 1)
    low = sub < 4
    copy_of = jnp.where(lane < SPARE, -1, lax.rem(lane - SPARE + COPIES, COPIES))

    row = iota((96, 3 * ROWS), 0)
    col = iota((96, 3 * ROWS), 1)
    part = col // ROWS
    source = col - part * ROWS - TOP - 1
    cell = row - TOP - 1
    entry = jnp.where((cell >= -1) & (cell <= NY + 1), decay(jnp.abs(cell - source), length_y), 0.0)
    for kind in range(6):
        entry = jnp.where(row == ROWS + kind, outgoing(kind, source, NY, length_y), entry)
    entry = jnp.where((source >= -1) & (source <= NY + 1), entry, 0.0)
    entry_high = entry.astype(BF16).astype(F32)
    basis[...] = jnp.where(part == 1, entry - entry_high, entry_high).astype(BF16)
    cell = iota((136, LANES), 0) - 1
    wide = iota((136, LANES), 1)
    pick_z[0] = jnp.where(wide == cell + 1, 1.0, 0.0).astype(F32)
    picked = jnp.where((wide < 3) & (wide + NZ - 1 == cell), 1.0, 0.0).astype(F32)
    for kind in range(6):
        start = SPARE + COPIES * kind
        picked = jnp.where((wide >= start) & (wide < start + COPIES), incoming(kind, cell, NZ, length_z), picked)
    pick_z[1] = picked
    cell = iota((XROWS, LANES), 0) - 1
    for kind in range(2):
        pick_x[kind] = incoming(kind, cell, NX, length_x)
    for side in range(2):
        for half in range(2):
            x_far[side, half, LIVE:ROWS, :] = jnp.zeros((ROWS - LIVE, LANES), F32)

    def mix(pos, count, size, length, k):
        from_left = pos >= k
        left = jnp.where(from_left, jnp.exp(full(-float(size * (k - 1))) / length), 0.0)
        right = jnp.where(from_left, 0.0, jnp.exp(full(-float(size * (count - k - 1))) / length))
        return left, right

    stacks = [None] * STACKS
    for j in range(WX * YT):
        x, yt = divmod(j, YT)
        stack, copy = divmod(j, COPIES)
        value = grid[x, 1, 8 * yt : 8 * yt + 8, :]
        stacks[stack] = value if copy == 0 else jnp.where(copy_of == copy, value, stacks[stack])
    for kind in range(2):
        for group in range(MOMENT_STACKS):
            total = jnp.zeros((8, LANES), F32)
            for i, stack in enumerate(range(6 * group, min(6 * group + 6, STACKS))):
                shift = (COPIES * i - SPARE - COPIES * kind) % LANES
                moved = pltpu.roll(stacks[stack], shift, 1) if shift else stacks[stack]
                total = jnp.where((lane >= COPIES * i) & (lane < COPIES * (i + 1)), moved, total)
            z_moment[kind, group] = total
        for group in range(FIX_STACKS):
            total = jnp.zeros((8, LANES), F32)
            for i, stack in enumerate(range(3 * group, min(3 * group + 3, STACKS))):
                shift = (2 * COPIES * i - SPARE - 2 * COPIES * (kind + 1)) % LANES
                moved = pltpu.roll(stacks[stack], shift, 1) if shift else stacks[stack]
                total = jnp.where((lane >= 2 * COPIES * i) & (lane < 2 * COPIES * (i + 1)), moved, total)
            z_fix[kind, group] = total

    pl.semaphore_wait(barrier, n_gx - 1 + n_yz - 1)

    def exchange(axis, pos, count, moment, moment_in, fix, fix_in, sem, fix_sem):
        copies = []
        for k in range(1, count):
            way = jnp.where(pos + k < count, 0, 1)
            copy = remote(
                moment.at[way], moment_in.at[k - 1], sem.at[0, k - 1], sem.at[1, k - 1], partner(axis, pos, k, count)
            )
            copy.start()
            copies.append(copy)
        if count > 1:
            right = remote(
                fix.at[0], fix_in.at[0], fix_sem.at[0, 0], fix_sem.at[1, 0], partner(axis, pos, 1, count)
            )
            left = remote(
                fix.at[1], fix_in.at[1], fix_sem.at[0, 1], fix_sem.at[1, 1], partner(axis, pos, count - 1, count)
            )
            pl.when(pos + 1 < count)(right.start)
            pl.when(pos > 0)(left.start)

        def wait_fix():
            if count > 1:
                pl.when(pos > 0)(right.wait_recv)
                pl.when(pos + 1 < count)(left.wait_recv)

        def wait_moment():
            for copy in copies:
                copy.wait_recv()

        def wait_send():
            for copy in copies:
                copy.wait_send()
            if count > 1:
                pl.when(pos + 1 < count)(right.wait_send)
                pl.when(pos > 0)(left.wait_send)

        return wait_moment, wait_fix, wait_send

    z_wait, z_wait_fix, z_done = exchange(
        "gz", pz, n_gz, z_moment, z_moment_in, z_fix, z_fix_in, z_sem, z_fix_sem
    )
    z_wait()
    z_wait_fix()
    mixed = [[jnp.zeros((8, LANES), F32) for _ in range(MOMENT_STACKS)] for _ in range(2)]
    for k in range(1, n_gz):
        weights = mix(pz, n_gz, NZ, length_z, k)
        for group in range(MOMENT_STACKS):
            got = z_moment_in[k - 1, group]
            for side in range(2):
                mixed[side][group] = mixed[side][group] + weights[side] * got
    fixes = [[jnp.where(pz > 0, z_fix_in[0, group], 0.0) for group in range(FIX_STACKS)]]
    fixes.append([jnp.where(pz + 1 < n_gz, z_fix_in[1, group], 0.0) for group in range(FIX_STACKS)])
    for stack in range(STACKS):
        total = jnp.zeros((8, LANES), F32)
        for kind in range(2):
            group, i = divmod(stack, 6)
            start = SPARE + COPIES * kind
            shift = (start - COPIES * i) % LANES
            moved = pltpu.roll(mixed[kind][group], shift, 1) if shift else mixed[kind][group]
            total = jnp.where((lane >= start) & (lane < start + COPIES), moved, total)
            group, i = divmod(stack, 3)
            start = SPARE + 2 * COPIES * (kind + 1)
            shift = (start - 2 * COPIES * i) % LANES
            moved = pltpu.roll(fixes[kind][group], shift, 1) if shift else fixes[kind][group]
            total = jnp.where((lane >= start) & (lane < start + 2 * COPIES), moved, total)
        for copy in range(COPIES):
            j = stack * COPIES + copy
            if j < WX * YT:
                x, yt = divmod(j, YT)
                spot = slice(8 * yt, 8 * yt + 8)
                value = jnp.where(copy_of == copy, total, 0.0)
                forward[x, 1, spot, :] = jnp.where(lane < SPARE, grid[x, 1, spot, :], value)
    for x in range(WX):
        forward[x, 1, LIVE:ROWS, :] = jnp.zeros((ROWS - LIVE, LANES), F32)

    def contract(x, carry):
        for half in range(2):
            values = (grid, forward)[half][x, half]
            high = values.astype(BF16)
            rest = (values - high.astype(F32)).astype(BF16)
            stacked = jnp.concatenate([high, high, rest], axis=0)
            result = jnp.dot(basis[...], stacked, preferred_element_type=F32)
            smooth[x, half] = result[:ROWS]
            for kind in range(6):
                y_out[kind // 2, kind % 2, half, pl.ds(x, 1), :] = result[ROWS + kind : ROWS + kind + 1]
        return carry

    lax.fori_loop(0, WX, contract, 0)
    y_wait, y_wait_fix, y_done = exchange(
        "gy", py, n_gy, y_out.at[0], y_moment_in, y_out.at[pl.ds(1, 2)], y_fix_in, y_sem, y_fix_sem
    )
    y_wait()
    y_wait_fix()
    far_y = []
    for half in range(2):
        totals = [jnp.zeros((XROWS, LANES), F32) for _ in range(2)]
        for k in range(1, n_gy):
            weights = mix(py, n_gy, NY, length_y, k)
            got = y_moment_in[k - 1, half]
            totals = [total + weight * got for total, weight in zip(totals, weights)]
        far_y.append(totals)
    for half in range(2):
        for side in range(2):
            y_moment_in[side, half] = far_y[half][side]
    has_left, has_right = py > 0, py + 1 < n_gy

    step_x = jnp.exp(full(-1.0) / length_x)
    fix_one = step_x - jnp.exp(full(1.0) / length_x)
    fix_two = jnp.exp(full(-2.0) / length_x) - jnp.exp(full(2.0) / length_x)

    def scan(yt, carry):
        rows = pl.ds(pl.multiple_of(yt * 8, 8), 8)
        cell = iota((8, LANES), 0) + yt * 8 - TOP - 1
        from_left = incoming(0, cell, NY, length_y)
        from_right = incoming(1, cell, NY, length_y)
        for half in range(2):
            state = None
            ends = {}
            for x in range(WX):
                value = smooth[x, half, rows, :]
                value = value + from_left * y_moment_in[0, half, x : x + 1, :]
                value = value + from_right * y_moment_in[1, half, x : x + 1, :]
                left = jnp.where(has_left, y_fix_in[0, :, half, x : x + 1, :], 0.0)
                right = jnp.where(has_right, y_fix_in[1, :, half, x : x + 1, :], 0.0)
                value = value + jnp.where(cell == -1, left[0], jnp.where(cell == 0, left[1], 0.0))
                value = value + jnp.where(cell == NY + 1, right[0], jnp.where(cell == NY, right[1], 0.0))
                smooth[x, half, rows, :] = value
                state = value if x == 0 else value + step_x * state
                forward[x, half, rows, :] = state
                if x < 2 or x >= WX - 2:
                    ends[x] = value
            x_moment[0, half, rows, :] = state
            x_fix[0, 0, half, rows, :] = ends[WX - 2] * fix_one + ends[WX - 1] * fix_two
            x_fix[0, 1, half, rows, :] = ends[WX - 1] * fix_one
            x_fix[1, 0, half, rows, :] = ends[0] * fix_two + ends[1] * fix_one
            x_fix[1, 1, half, rows, :] = ends[0] * fix_one
            state = jnp.zeros((8, LANES), F32)
            for x in reversed(range(WX)):
                value = smooth[x, half, rows, :]
                smooth[x, half, rows, :] = forward[x, half, rows, :] + state
                if x == 0:
                    x_moment[1, half, rows, :] = state + value
                state = step_x * (state + value)
        return carry

    lax.fori_loop(0, YT, scan, 0)

    right = left = None
    if n_gx > 1:
        right = remote(x_fix.at[0], x_fix_in.at[0], x_fix_sem.at[0, 0], x_fix_sem.at[1, 0], partner("gx", px, 1, n_gx))
        left = remote(
            x_fix.at[1], x_fix_in.at[1], x_fix_sem.at[0, 1], x_fix_sem.at[1, 1], partner("gx", px, n_gx - 1, n_gx)
        )

    def chunk(index):
        return pl.ds(pl.multiple_of(index * 8, 8), 8)

    first_sends = []
    for c in range(YT):
        copy = remote(x_moment.at[:, :, chunk(c), :], x_chunk_in.at[px], x1_send.at[c], x1_recv.at[px], {"gx": c})
        first_sends.append((px != c, copy))
        pl.when(px != c)(copy.start)
    if n_gx > 1:
        pl.when(px + 1 < n_gx)(right.start)
        pl.when(px > 0)(left.start)

    @pl.when(px < YT)
    def _():
        x_chunk_in[px] = x_moment[:, :, chunk(px), :]
        for p in range(n_gx):
            copy = remote(
                x_moment.at[:, :, chunk(0), :], x_chunk_in.at[p], x1_send.at[0], x1_recv.at[p], {"gx": p}
            )
            pl.when(px != p)(copy.wait_recv)
        ratio = jnp.exp(full(-float(NX)) / length_x)
        for side, order in enumerate((range(n_gx), reversed(range(n_gx)))):
            total = [jnp.zeros((8, LANES), F32) for _ in range(2)]
            for q in order:
                for half in range(2):
                    x_prefix[q, side, half] = total[half]
                    total[half] = total[half] * ratio + x_chunk_in[q, side, half]
        for q in range(n_gx):
            copy = remote(x_prefix.at[q], x_far.at[:, :, chunk(px), :], x2_send.at[q], x2_recv.at[px], {"gx": q})
            pl.when(px != q)(copy.start)
        x_far[:, :, chunk(px), :] = x_prefix[px]

    if n_gx > 1:
        pl.when(px > 0)(right.wait_recv)
        pl.when(px + 1 < n_gx)(left.wait_recv)
    for half in range(2):
        for kind, x in enumerate((0, 1)):
            smooth[x, half, 0:LIVE, :] += jnp.where(px > 0, x_fix_in[0, kind, half], 0.0)
        for kind, x in enumerate((WX - 1, WX - 2)):
            smooth[x, half, 0:LIVE, :] += jnp.where(px + 1 < n_gx, x_fix_in[1, kind, half], 0.0)
    w_copy.wait()

    def tile_spot(t):
        at = pl.ds(pl.multiple_of(t * LANES, LANES), LANES)
        x0 = jnp.clip(base[0, t] - px * NX + 1, 0, NX - 1)
        y0 = jnp.clip(base[1, t] - py * NY + 1, 0, NY - 1) + TOP
        z0 = jnp.clip(base[2, t] - pz * NZ + 1, 0, NZ - 1)
        return at, x0, y0, z0

    def gather(rows, weights, at, z0):
        total = None
        for e in range(4):
            pick = [pick_z[half, pl.ds(z0 + e, 1), :] for half in range(2)]
            inner = None
            for cells, weight in zip(rows, weights):
                taps = jnp.sum(cells[0] * pick[0] + cells[1] * pick[1], axis=1, keepdims=True)
                inner = weight * taps if inner is None else inner + weight * taps
            inner = inner * w[8 + e : 9 + e, at]
            total = inner if e == 0 else total + inner
        return jnp.sum(total, axis=0, keepdims=True)

    def near(t, carry):
        at, x0, y0, z0 = tile_spot(t)
        first, second, _ = tile_weights(w[0:8, at], low)
        rows = [
            [
                jnp.where(
                    low, smooth[x0 + a, half, pl.ds(y0, 8), :], smooth[x0 + a + 1, half, pl.ds(y0 - 4, 8), :]
                )
                for half in range(2)
            ]
            for a in (0, 2)
        ]
        sampled[pl.ds(t, 1), :] = gather(rows, (first, second), at, z0)
        return carry

    lax.fori_loop(0, TILES, near, 0, unroll=2)

    for c in range(YT):
        copy = remote(x_prefix.at[0], x_far.at[:, :, chunk(c), :], x2_send.at[0], x2_recv.at[c], {"gx": c})
        pl.when(px != c)(copy.wait_recv)

    def far(t, carry):
        at, x0, y0, z0 = tile_spot(t)
        w8 = w[0:8, at]
        _, _, along_y = tile_weights(w8, low)
        along_x = []
        for side in range(2):
            total = None
            for a in range(4):
                term = w8[a : a + 1] * pick_x[side, pl.ds(x0 + a, 1), :]
                total = term if a == 0 else total + term
            along_x.append(total)
        weight = jnp.where(low, along_x[0], along_x[1]) * along_y
        rows = [jnp.where(low, x_far[0, half, pl.ds(y0, 8), :], x_far[1, half, pl.ds(y0 - 4, 8), :]) for half in range(2)]
        sampled[pl.ds(t, 1), :] += gather([rows], [weight], at, z0)
        return carry

    lax.fori_loop(0, TILES, far, 0, unroll=2)

    value = live[...] * (sampled[...] + noise[...] * live_dir[...])
    image[...] = value
    pairs = (
        (live_res[...], live_res[...]),
        (live_dir[...], value),
        (live_res[...], value),
        (value, value),
    )
    sum_out[...] = jnp.concatenate(
        [jnp.sum(a * b, axis=0, keepdims=True) for a, b in pairs] + [jnp.zeros((4, LANES), F32)], axis=0
    )
    last = []
    for k in range(1, n_gx):
        copy = remote(sum_out, sum_in_x.at[k - 1], sx_sem.at[0, k - 1], sx_sem.at[1, k - 1], partner("gx", px, k, n_gx))
        copy.start()
        last.append(copy)
    total = sum_out[...]
    for k in range(1, n_gx):
        last[k - 1].wait_recv()
        total = total + sum_in_x[k - 1]
    sum_mid[...] = total
    more = []
    for k in range(1, n_yz):
        copy = remote(sum_mid, sum_in_yz.at[k - 1], syz_sem.at[0, k - 1], syz_sem.at[1, k - 1], yz_partner(k))
        copy.start()
        more.append(copy)
    for k in range(1, n_yz):
        more[k - 1].wait_recv()
        total = total + sum_in_yz[k - 1]
    sums[...] = total

    for copy in last + more:
        copy.wait_send()
    z_done()
    y_done()
    if n_gx > 1:
        pl.when(px + 1 < n_gx)(right.wait_send)
        pl.when(px > 0)(left.wait_send)
    for sent, copy in first_sends:
        pl.when(sent)(copy.wait_send)

    @pl.when(px < YT)
    def _():
        for q in range(n_gx):
            copy = remote(x_prefix.at[q], x_far.at[:, :, chunk(px), :], x2_send.at[q], x2_recv.at[px], {"gx": q})
            pl.when(px != q)(copy.wait_send)


def update_kernel(sums, iterate, live, live_dir, live_res, image, new_iterate, new_residual, new_direction):
    def total(row):
        return jnp.sum(sums[row : row + 1, :], axis=1, keepdims=True)

    norm_old, curvature, cross, square = total(0), total(1), total(2), total(3)
    step = norm_old / curvature
    norm_new = norm_old + step * (step * square - 2.0 * cross)
    held = live_res[...] - step * image[...]
    new_iterate[...] = live[...] * iterate[...] + step * live_dir[...]
    new_residual[...] = held
    new_direction[...] = held + norm_new / norm_old * live_dir[...]


def body(sizes, iterate, residual, direction, noise, stencil_base, interp_weights, tile_counts, reach):
    n_gx, n_gy, n_gz = sizes
    n_yz = n_gy * n_gz
    square = (TILES, LANES)
    in_vmem = pl.BlockSpec(memory_space=pltpu.VMEM)
    in_smem = pl.BlockSpec(memory_space=pltpu.SMEM)

    def keep(x):
        return pltpu.with_memory_space_constraint(x, pltpu.VMEM)

    grid, live_dir, live_res, live = pl.pallas_call(
        spread_kernel,
        out_shape=[pltpu.VMEM((WX, 2, ROWS, LANES), F32)] + [pltpu.VMEM(square, F32)] * 3,
        in_specs=[in_smem] * 3 + [in_vmem] * 3,
        out_specs=[in_vmem] * 4,
        scratch_shapes=[pltpu.VMEM((2, 136, LANES), F32)],
        compiler_params=pltpu.CompilerParams(vmem_limit_bytes=16 << 20),
        name="spread",
    )(tile_counts, stencil_base, reach, interp_weights, direction.reshape(square), residual.reshape(square))

    dma = pltpu.SemaphoreType.DMA
    image, sums = pl.pallas_call(
        functools.partial(solve_kernel, sizes),
        out_shape=[pltpu.VMEM(square, F32), pltpu.VMEM((8, LANES), F32)],
        in_specs=[in_smem] * 2 + [in_vmem] * 5 + [pl.BlockSpec(memory_space=pl.ANY)],
        out_specs=[in_vmem] * 2,
        scratch_shapes=[
            pltpu.VMEM((12, TILES * LANES), F32),
            pltpu.VMEM((WX, 2, ROWS, LANES), F32),
            pltpu.VMEM((WX, 2, ROWS, LANES), F32),
            pltpu.VMEM((96, 3 * ROWS), BF16),
            pltpu.VMEM((2, 136, LANES), F32),
            pltpu.VMEM((2, XROWS, LANES), F32),
            pltpu.VMEM((2, MOMENT_STACKS, 8, LANES), F32),
            pltpu.VMEM((2, FIX_STACKS, 8, LANES), F32),
            pltpu.VMEM((3, MOMENT_STACKS, 8, LANES), F32),
            pltpu.VMEM((2, FIX_STACKS, 8, LANES), F32),
            pltpu.VMEM((3, 2, 2, XROWS, LANES), F32),
            pltpu.VMEM((3, 2, XROWS, LANES), F32),
            pltpu.VMEM((2, 2, 2, XROWS, LANES), F32),
            pltpu.VMEM((2, 2, LIVE, LANES), F32),
            pltpu.VMEM((2, 2, 2, LIVE, LANES), F32),
            pltpu.VMEM((2, 2, 2, LIVE, LANES), F32),
            pltpu.VMEM((n_gx, 2, 2, 8, LANES), F32),
            pltpu.VMEM((n_gx, 2, 2, 8, LANES), F32),
            pltpu.VMEM((2, 2, ROWS, LANES), F32),
            pltpu.VMEM(square, F32),
            pltpu.VMEM((8, LANES), F32),
            pltpu.VMEM((15, 8, LANES), F32),
            pltpu.VMEM((8, LANES), F32),
            pltpu.VMEM((15, 8, LANES), F32),
            dma,
            dma((2, 3)),
            dma((2, 2)),
            dma((2, 3)),
            dma((2, 2)),
            dma((2, 2)),
            dma((YT,)),
            dma((n_gx,)),
            dma((n_gx,)),
            dma((YT,)),
            dma((2, 15)),
            dma((2, 15)),
        ],
        compiler_params=pltpu.CompilerParams(
            collective_id=0, has_side_effects=True, vmem_limit_bytes=24 << 20
        ),
        name="solve",
    )(
        stencil_base,
        reach,
        keep(grid),
        keep(live_dir),
        keep(live_res),
        keep(live),
        noise.reshape(square),
        interp_weights,
    )

    outs = pl.pallas_call(
        update_kernel,
        out_shape=[jax.ShapeDtypeStruct(square, F32)] * 3,
        in_specs=[in_vmem] * 6,
        out_specs=[in_vmem] * 3,
        name="update",
    )(keep(sums), iterate.reshape(square), keep(live), keep(live_dir), keep(live_res), keep(image))
    return tuple(out.reshape(-1) for out in outs)


def solution(mesh):
    sizes = tuple(mesh.shape[axis] for axis in ("gx", "gy", "gz"))
    lines = P(("gx", "gy", "gz"))
    return jax.shard_map(
        functools.partial(body, sizes),
        mesh=mesh,
        in_specs=(lines, lines, lines, lines, P(None, ("gx", "gy", "gz")), P(None, ("gx", "gy", "gz")), lines, P()),
        out_specs=(lines, lines, lines),
        check_vma=False,
    )
```

```python
import functools

import jax
import jax.numpy as jnp
from jax import lax
from jax.experimental import pallas as pl
from jax.experimental.pallas import tpu as pltpu
from jax.sharding import PartitionSpec as P

F32 = jnp.float32
BF16 = jnp.bfloat16
LANES = 128
TILES = 128
NX, NY, NZ = 32, 64, 128
WX = NX + 3
TOP = 4
ROWS = 80
LIVE = 72
YT = LIVE // 8
SPARE, COPIES = 8, 20
STACKS = -(-WX * YT // COPIES)
MOMENT_STACKS, FIX_STACKS = -(-STACKS // 6), -(-STACKS // 3)
XROWS = 40
MESH = pl.DeviceIdType.MESH


def iota(shape, dim):
    return lax.broadcasted_iota(jnp.int32, shape, dim)


def full(value):
    return jnp.full((1, LANES), value, F32)


def decay(distance, length):
    return jnp.exp(-distance.astype(F32) / length)


def outgoing(kind, source, size, length):
    one = decay(full(1), length) - jnp.exp(full(1.0) / length)
    two = decay(full(2), length) - jnp.exp(full(2.0) / length)
    one, two = one[:, :1], two[:, :1]
    zero = jnp.zeros(source.shape, F32)
    if kind == 0:
        return decay(size + 1 - source, length)
    if kind == 1:
        return decay(source + 1, length)
    if kind == 2:
        return jnp.where(source == size, one, jnp.where(source == size + 1, two, zero))
    if kind == 3:
        return jnp.where(source == size + 1, one, zero)
    if kind == 4:
        return jnp.where(source == -1, two, jnp.where(source == 0, one, zero))
    return jnp.where(source == -1, one, zero)


def incoming(kind, cell, size, length):
    if kind == 0:
        return decay(cell - 1, length)
    if kind == 1:
        return decay(size - 1 - cell, length)
    target = (-1, 0, size + 1, size)[kind - 2]
    return jnp.where(cell == target, 1.0, 0.0).astype(F32)


def tile_weights(w8, low):
    along_y = jnp.where(low, pltpu.roll(w8, 4, 0), w8)
    first = jnp.where(low, w8[0:1], w8[1:2]) * along_y
    second = jnp.where(low, w8[2:3], w8[3:4]) * along_y
    return first, second, along_y


def fetch(pairs, sem):
    copies = [pltpu.make_async_copy(src, dst, sem.at[i]) for i, (src, dst) in enumerate(pairs)]
    for copy in copies:
        copy.start()
    return copies


def spread_kernel(
    count_hbm,
    base_hbm,
    reach_hbm,
    w_hbm,
    direction_hbm,
    residual_hbm,
    grid,
    live_dir,
    live_res,
    live,
    table,
    count,
    base,
    reach,
    w,
    direction,
    residual,
    sem,
):
    copies = fetch(
        (
            (reach_hbm, reach),
            (w_hbm, w),
            (count_hbm, count),
            (base_hbm, base),
            (direction_hbm, direction),
            (residual_hbm, residual),
        ),
        sem,
    )

    def clear(x, carry):
        for half in range(2):
            grid[x, half] = jnp.zeros((ROWS, LANES), F32)
        return carry

    lax.fori_loop(0, WX, clear, 0)
    copies[0].wait()
    anchor_x = lax.axis_index("gx") * NX
    anchor_y = lax.axis_index("gy") * NY
    anchor_z = lax.axis_index("gz") * NZ
    length = reach[2] * float(NZ)
    scale = 1.0 / (
        jnp.sqrt(full(reach[0] * float(NX))) * jnp.sqrt(full(reach[1] * float(NY))) * jnp.sqrt(full(length))
    )
    source = iota((136, LANES), 0) - 1
    lane = iota((136, LANES), 1)
    table[0] = decay(jnp.abs(lane - 1 - source), length) * scale
    second = jnp.where(lane < 3, decay(jnp.abs(lane + NZ - 1 - source), length), 0.0)
    for kind in range(6):
        start = SPARE + COPIES * kind
        inside = (lane >= start) & (lane < start + COPIES)
        second = jnp.where(inside, outgoing(kind, source, NZ, length), second)
    table[1] = second * scale
    for copy in copies[1:]:
        copy.wait()
    low = iota((8, LANES), 0) < 4
    slot = iota((1, LANES), 1)

    def tile(t, carry):
        at = pl.ds(pl.multiple_of(t * LANES, LANES), LANES)
        w8 = w[0:8, at]
        mask = slot < count[t]
        values = jnp.where(mask, direction[pl.ds(t, 1), :], 0.0)
        live_dir[pl.ds(t, 1), :] = values
        live_res[pl.ds(t, 1), :] = jnp.where(mask, residual[pl.ds(t, 1), :], 0.0)
        live[pl.ds(t, 1), :] = jnp.where(mask, 1.0, 0.0)
        first, second, _ = tile_weights(w8, low)
        x0 = base[0, t] - anchor_x + 1
        y0 = base[1, t] - anchor_y + 1 + TOP
        z0 = base[2, t] - anchor_z + 1
        parts = [[None, None], [None, None]]
        for e in range(4):
            along_z = w[8 + e : 9 + e, at] * values
            row = [table[half, pl.ds(z0 + e, 1), :] for half in range(2)]
            for pair, product in enumerate((first, second)):
                taps = jnp.sum(product * along_z, axis=1, keepdims=True)
                for half in range(2):
                    term = taps * row[half]
                    parts[pair][half] = term if e == 0 else parts[pair][half] + term
        for a in range(4):
            start = y0 if a % 2 == 0 else y0 - 4
            keep = low if a % 2 == 0 else jnp.logical_not(low)
            for half in range(2):
                spot = (x0 + a, half, pl.ds(start, 8), slice(None))
                grid[spot] = grid[spot] + jnp.where(keep, parts[a // 2][half], 0.0)
        return carry

    lax.fori_loop(0, TILES, tile, 0, unroll=8)


def partner(axis, me, offset, count):
    return {axis: lax.rem(me + offset, count)}


def solve_kernel(
    sizes,
    base_hbm,
    reach_hbm,
    noise_hbm,
    w_hbm,
    grid,
    live_dir,
    live_res,
    live,
    image,
    sums,
    base,
    reach,
    noise,
    w,
    forward,
    smooth,
    basis,
    pick_z,
    pick_x,
    z_moment,
    z_fix,
    z_moment_in,
    z_fix_in,
    y_out,
    y_moment_in,
    y_fix_in,
    x_moment,
    x_fix,
    x_fix_in,
    x_chunk_in,
    x_prefix,
    x_far,
    sampled,
    sum_out,
    sum_in_x,
    sum_mid,
    sum_in_yz,
    in_sem,
    z_sem,
    z_fix_sem,
    y_sem,
    y_fix_sem,
    x_fix_sem,
    x1_send,
    x1_recv,
    x2_send,
    x2_recv,
    sx_sem,
    syz_sem,
):
    n_gx, n_gy, n_gz = sizes
    n_yz = n_gy * n_gz
    px, py, pz = lax.axis_index("gx"), lax.axis_index("gy"), lax.axis_index("gz")
    pyz = py * n_gz + pz
    def yz_partner(offset):
        other = lax.rem(pyz + offset, n_yz)
        return {"gy": other // n_gz, "gz": lax.rem(other, n_gz)}

    barrier = pltpu.get_barrier_semaphore()
    for k in range(1, n_gx):
        pl.semaphore_signal(barrier, inc=1, device_id=partner("gx", px, k, n_gx), device_id_type=MESH)
    for k in range(1, n_yz):
        pl.semaphore_signal(barrier, inc=1, device_id=yz_partner(k), device_id_type=MESH)

    copies_in = fetch(((reach_hbm, reach), (base_hbm, base), (noise_hbm, noise), (w_hbm, w)), in_sem)
    copies_in[0].wait()
    length_x, length_y, length_z = reach[0] * float(NX), reach[1] * float(NY), reach[2] * float(NZ)

    def remote(src, dst, send, recv, device):
        return pltpu.make_async_remote_copy(
            src_ref=src, dst_ref=dst, send_sem=send, recv_sem=recv, device_id=device, device_id_type=MESH
        )

    sub = iota((8, LANES), 0)
    lane = iota((8, LANES), 1)
    low = sub < 4
    copy_of = jnp.where(lane < SPARE, -1, lax.rem(lane - SPARE + COPIES, COPIES))

    row = iota((96, 3 * ROWS), 0)
    col = iota((96, 3 * ROWS), 1)
    part = col // ROWS
    source = col - part * ROWS - TOP - 1
    cell = row - TOP - 1
    entry = jnp.where((cell >= -1) & (cell <= NY + 1), decay(jnp.abs(cell - source), length_y), 0.0)
    for kind in range(6):
        entry = jnp.where(row == ROWS + kind, outgoing(kind, source, NY, length_y), entry)
    entry = jnp.where((source >= -1) & (source <= NY + 1), entry, 0.0)
    entry_high = entry.astype(BF16).astype(F32)
    basis[...] = jnp.where(part == 1, entry - entry_high, entry_high).astype(BF16)
    cell = iota((136, LANES), 0) - 1
    wide = iota((136, LANES), 1)
    pick_z[0] = jnp.where(wide == cell + 1, 1.0, 0.0).astype(F32)
    picked = jnp.where((wide < 3) & (wide + NZ - 1 == cell), 1.0, 0.0).astype(F32)
    for kind in range(6):
        start = SPARE + COPIES * kind
        picked = jnp.where((wide >= start) & (wide < start + COPIES), incoming(kind, cell, NZ, length_z), picked)
    pick_z[1] = picked
    cell = iota((XROWS, LANES), 0) - 1
    for kind in range(2):
        pick_x[kind] = incoming(kind, cell, NX, length_x)
    for side in range(2):
        for half in range(2):
            x_far[side, half, LIVE:ROWS, :] = jnp.zeros((ROWS - LIVE, LANES), F32)

    def mix(pos, count, size, length, k):
        from_left = pos >= k
        left = jnp.where(from_left, jnp.exp(full(-float(size * (k - 1))) / length), 0.0)
        right = jnp.where(from_left, 0.0, jnp.exp(full(-float(size * (count - k - 1))) / length))
        return left, right

    stacks = [None] * STACKS
    for j in range(WX * YT):
        x, yt = divmod(j, YT)
        stack, copy = divmod(j, COPIES)
        value = grid[x, 1, 8 * yt : 8 * yt + 8, :]
        stacks[stack] = value if copy == 0 else jnp.where(copy_of == copy, value, stacks[stack])
    for kind in range(2):
        for group in range(MOMENT_STACKS):
            total = jnp.zeros((8, LANES), F32)
            for i, stack in enumerate(range(6 * group, min(6 * group + 6, STACKS))):
                shift = (COPIES * i - SPARE - COPIES * kind) % LANES
                moved = pltpu.roll(stacks[stack], shift, 1) if shift else stacks[stack]
                total = jnp.where((lane >= COPIES * i) & (lane < COPIES * (i + 1)), moved, total)
            z_moment[kind, group] = total
        for group in range(FIX_STACKS):
            total = jnp.zeros((8, LANES), F32)
            for i, stack in enumerate(range(3 * group, min(3 * group + 3, STACKS))):
                shift = (2 * COPIES * i - SPARE - 2 * COPIES * (kind + 1)) % LANES
                moved = pltpu.roll(stacks[stack], shift, 1) if shift else stacks[stack]
                total = jnp.where((lane >= 2 * COPIES * i) & (lane < 2 * COPIES * (i + 1)), moved, total)
            z_fix[kind, group] = total

    pl.semaphore_wait(barrier, n_gx - 1 + n_yz - 1)

    def exchange(axis, pos, count, moment, moment_in, fix, fix_in, sem, fix_sem):
        copies = []
        for k in range(1, count):
            way = jnp.where(pos + k < count, 0, 1)
            copy = remote(
                moment.at[way], moment_in.at[k - 1], sem.at[0, k - 1], sem.at[1, k - 1], partner(axis, pos, k, count)
            )
            copy.start()
            copies.append(copy)
        if count > 1:
            right = remote(
                fix.at[0], fix_in.at[0], fix_sem.at[0, 0], fix_sem.at[1, 0], partner(axis, pos, 1, count)
            )
            left = remote(
                fix.at[1], fix_in.at[1], fix_sem.at[0, 1], fix_sem.at[1, 1], partner(axis, pos, count - 1, count)
            )
            pl.when(pos + 1 < count)(right.start)
            pl.when(pos > 0)(left.start)

        def wait_fix():
            if count > 1:
                pl.when(pos > 0)(right.wait_recv)
                pl.when(pos + 1 < count)(left.wait_recv)

        def wait_moment():
            for copy in copies:
                copy.wait_recv()

        def wait_send():
            for copy in copies:
                copy.wait_send()
            if count > 1:
                pl.when(pos + 1 < count)(right.wait_send)
                pl.when(pos > 0)(left.wait_send)

        return wait_moment, wait_fix, wait_send

    z_wait, z_wait_fix, z_done = exchange(
        "gz", pz, n_gz, z_moment, z_moment_in, z_fix, z_fix_in, z_sem, z_fix_sem
    )
    z_wait()
    z_wait_fix()
    mixed = [[jnp.zeros((8, LANES), F32) for _ in range(MOMENT_STACKS)] for _ in range(2)]
    for k in range(1, n_gz):
        weights = mix(pz, n_gz, NZ, length_z, k)
        for group in range(MOMENT_STACKS):
            got = z_moment_in[k - 1, group]
            for side in range(2):
                mixed[side][group] = mixed[side][group] + weights[side] * got
    fixes = [[jnp.where(pz > 0, z_fix_in[0, group], 0.0) for group in range(FIX_STACKS)]]
    fixes.append([jnp.where(pz + 1 < n_gz, z_fix_in[1, group], 0.0) for group in range(FIX_STACKS)])
    for stack in range(STACKS):
        total = jnp.zeros((8, LANES), F32)
        for kind in range(2):
            group, i = divmod(stack, 6)
            start = SPARE + COPIES * kind
            shift = (start - COPIES * i) % LANES
            moved = pltpu.roll(mixed[kind][group], shift, 1) if shift else mixed[kind][group]
            total = jnp.where((lane >= start) & (lane < start + COPIES), moved, total)
            group, i = divmod(stack, 3)
            start = SPARE + 2 * COPIES * (kind + 1)
            shift = (start - 2 * COPIES * i) % LANES
            moved = pltpu.roll(fixes[kind][group], shift, 1) if shift else fixes[kind][group]
            total = jnp.where((lane >= start) & (lane < start + 2 * COPIES), moved, total)
        for copy in range(COPIES):
            j = stack * COPIES + copy
            if j < WX * YT:
                x, yt = divmod(j, YT)
                spot = slice(8 * yt, 8 * yt + 8)
                value = jnp.where(copy_of == copy, total, 0.0)
                forward[x, 1, spot, :] = jnp.where(lane < SPARE, grid[x, 1, spot, :], value)
    for x in range(WX):
        forward[x, 1, LIVE:ROWS, :] = jnp.zeros((ROWS - LIVE, LANES), F32)

    def contract(x, carry):
        for half in range(2):
            values = (grid, forward)[half][x, half]
            high = values.astype(BF16)
            rest = (values - high.astype(F32)).astype(BF16)
            stacked = jnp.concatenate([high, high, rest], axis=0)
            result = jnp.dot(basis[...], stacked, preferred_element_type=F32)
            smooth[x, half] = result[:ROWS]
            for kind in range(6):
                y_out[kind // 2, kind % 2, half, pl.ds(x, 1), :] = result[ROWS + kind : ROWS + kind + 1]
        return carry

    lax.fori_loop(0, WX, contract, 0)
    y_wait, y_wait_fix, y_done = exchange(
        "gy", py, n_gy, y_out.at[0], y_moment_in, y_out.at[pl.ds(1, 2)], y_fix_in, y_sem, y_fix_sem
    )
    y_wait()
    y_wait_fix()
    far_y = []
    for half in range(2):
        totals = [jnp.zeros((XROWS, LANES), F32) for _ in range(2)]
        for k in range(1, n_gy):
            weights = mix(py, n_gy, NY, length_y, k)
            got = y_moment_in[k - 1, half]
            totals = [total + weight * got for total, weight in zip(totals, weights)]
        far_y.append(totals)
    for half in range(2):
        for side in range(2):
            y_moment_in[side, half] = far_y[half][side]
    has_left, has_right = py > 0, py + 1 < n_gy

    step_x = jnp.exp(full(-1.0) / length_x)
    fix_one = step_x - jnp.exp(full(1.0) / length_x)
    fix_two = jnp.exp(full(-2.0) / length_x) - jnp.exp(full(2.0) / length_x)

    def scan(yt, carry):
        rows = pl.ds(pl.multiple_of(yt * 8, 8), 8)
        cell = iota((8, LANES), 0) + yt * 8 - TOP - 1
        from_left = incoming(0, cell, NY, length_y)
        from_right = incoming(1, cell, NY, length_y)
        for half in range(2):
            state = None
            ends = {}
            for x in range(WX):
                value = smooth[x, half, rows, :]
                value = value + from_left * y_moment_in[0, half, x : x + 1, :]
                value = value + from_right * y_moment_in[1, half, x : x + 1, :]
                left = jnp.where(has_left, y_fix_in[0, :, half, x : x + 1, :], 0.0)
                right = jnp.where(has_right, y_fix_in[1, :, half, x : x + 1, :], 0.0)
                value = value + jnp.where(cell == -1, left[0], jnp.where(cell == 0, left[1], 0.0))
                value = value + jnp.where(cell == NY + 1, right[0], jnp.where(cell == NY, right[1], 0.0))
                smooth[x, half, rows, :] = value
                state = value if x == 0 else value + step_x * state
                forward[x, half, rows, :] = state
                if x < 2 or x >= WX - 2:
                    ends[x] = value
            x_moment[0, half, rows, :] = state
            x_fix[0, 0, half, rows, :] = ends[WX - 2] * fix_one + ends[WX - 1] * fix_two
            x_fix[0, 1, half, rows, :] = ends[WX - 1] * fix_one
            x_fix[1, 0, half, rows, :] = ends[0] * fix_two + ends[1] * fix_one
            x_fix[1, 1, half, rows, :] = ends[0] * fix_one
            state = jnp.zeros((8, LANES), F32)
            for x in reversed(range(WX)):
                value = smooth[x, half, rows, :]
                smooth[x, half, rows, :] = forward[x, half, rows, :] + state
                if x == 0:
                    x_moment[1, half, rows, :] = state + value
                state = step_x * (state + value)
        return carry

    lax.fori_loop(0, YT, scan, 0)

    right = left = None
    if n_gx > 1:
        right = remote(x_fix.at[0], x_fix_in.at[0], x_fix_sem.at[0, 0], x_fix_sem.at[1, 0], partner("gx", px, 1, n_gx))
        left = remote(
            x_fix.at[1], x_fix_in.at[1], x_fix_sem.at[0, 1], x_fix_sem.at[1, 1], partner("gx", px, n_gx - 1, n_gx)
        )

    def chunk(index):
        return pl.ds(pl.multiple_of(index * 8, 8), 8)

    first_sends = []
    for c in range(YT):
        copy = remote(x_moment.at[:, :, chunk(c), :], x_chunk_in.at[px], x1_send.at[c], x1_recv.at[px], {"gx": c})
        first_sends.append((px != c, copy))
        pl.when(px != c)(copy.start)
    if n_gx > 1:
        pl.when(px + 1 < n_gx)(right.start)
        pl.when(px > 0)(left.start)

    @pl.when(px < YT)
    def _():
        x_chunk_in[px] = x_moment[:, :, chunk(px), :]
        for p in range(n_gx):
            copy = remote(
                x_moment.at[:, :, chunk(0), :], x_chunk_in.at[p], x1_send.at[0], x1_recv.at[p], {"gx": p}
            )
            pl.when(px != p)(copy.wait_recv)
        ratio = jnp.exp(full(-float(NX)) / length_x)
        for side, order in enumerate((range(n_gx), reversed(range(n_gx)))):
            total = [jnp.zeros((8, LANES), F32) for _ in range(2)]
            for q in order:
                for half in range(2):
                    x_prefix[q, side, half] = total[half]
                    total[half] = total[half] * ratio + x_chunk_in[q, side, half]
        for q in range(n_gx):
            copy = remote(x_prefix.at[q], x_far.at[:, :, chunk(px), :], x2_send.at[q], x2_recv.at[px], {"gx": q})
            pl.when(px != q)(copy.start)
        x_far[:, :, chunk(px), :] = x_prefix[px]

    if n_gx > 1:
        pl.when(px > 0)(right.wait_recv)
        pl.when(px + 1 < n_gx)(left.wait_recv)
    for half in range(2):
        for kind, x in enumerate((0, 1)):
            smooth[x, half, 0:LIVE, :] += jnp.where(px > 0, x_fix_in[0, kind, half], 0.0)
        for kind, x in enumerate((WX - 1, WX - 2)):
            smooth[x, half, 0:LIVE, :] += jnp.where(px + 1 < n_gx, x_fix_in[1, kind, half], 0.0)
    for copy in copies_in[1:]:
        copy.wait()

    def tile_spot(t):
        at = pl.ds(pl.multiple_of(t * LANES, LANES), LANES)
        x0 = jnp.clip(base[0, t] - px * NX + 1, 0, NX - 1)
        y0 = jnp.clip(base[1, t] - py * NY + 1, 0, NY - 1) + TOP
        z0 = jnp.clip(base[2, t] - pz * NZ + 1, 0, NZ - 1)
        return at, x0, y0, z0

    def gather(rows, weights, at, z0):
        total = None
        for e in range(4):
            pick = [pick_z[half, pl.ds(z0 + e, 1), :] for half in range(2)]
            inner = None
            for cells, weight in zip(rows, weights):
                taps = jnp.sum(cells[0] * pick[0] + cells[1] * pick[1], axis=1, keepdims=True)
                inner = weight * taps if inner is None else inner + weight * taps
            inner = inner * w[8 + e : 9 + e, at]
            total = inner if e == 0 else total + inner
        return jnp.sum(total, axis=0, keepdims=True)

    def near(t, carry):
        at, x0, y0, z0 = tile_spot(t)
        first, second, _ = tile_weights(w[0:8, at], low)
        rows = [
            [
                jnp.where(
                    low, smooth[x0 + a, half, pl.ds(y0, 8), :], smooth[x0 + a + 1, half, pl.ds(y0 - 4, 8), :]
                )
                for half in range(2)
            ]
            for a in (0, 2)
        ]
        sampled[pl.ds(t, 1), :] = gather(rows, (first, second), at, z0)
        return carry

    lax.fori_loop(0, TILES, near, 0, unroll=8)

    for c in range(YT):
        copy = remote(x_prefix.at[0], x_far.at[:, :, chunk(c), :], x2_send.at[0], x2_recv.at[c], {"gx": c})
        pl.when(px != c)(copy.wait_recv)

    def far(t, carry):
        at, x0, y0, z0 = tile_spot(t)
        w8 = w[0:8, at]
        _, _, along_y = tile_weights(w8, low)
        along_x = []
        for side in range(2):
            total = None
            for a in range(4):
                term = w8[a : a + 1] * pick_x[side, pl.ds(x0 + a, 1), :]
                total = term if a == 0 else total + term
            along_x.append(total)
        weight = jnp.where(low, along_x[0], along_x[1]) * along_y
        rows = [jnp.where(low, x_far[0, half, pl.ds(y0, 8), :], x_far[1, half, pl.ds(y0 - 4, 8), :]) for half in range(2)]
        sampled[pl.ds(t, 1), :] += gather([rows], [weight], at, z0)
        return carry

    lax.fori_loop(0, TILES, far, 0, unroll=8)

    value = live[...] * (sampled[...] + noise[...] * live_dir[...])
    image[...] = value
    pairs = (
        (live_res[...], live_res[...]),
        (live_dir[...], value),
        (live_res[...], value),
        (value, value),
    )
    sum_out[...] = jnp.concatenate(
        [jnp.sum(a * b, axis=0, keepdims=True) for a, b in pairs] + [jnp.zeros((4, LANES), F32)], axis=0
    )
    last = []
    for k in range(1, n_gx):
        copy = remote(sum_out, sum_in_x.at[k - 1], sx_sem.at[0, k - 1], sx_sem.at[1, k - 1], partner("gx", px, k, n_gx))
        copy.start()
        last.append(copy)
    total = sum_out[...]
    for k in range(1, n_gx):
        last[k - 1].wait_recv()
        total = total + sum_in_x[k - 1]
    sum_mid[...] = total
    more = []
    for k in range(1, n_yz):
        copy = remote(sum_mid, sum_in_yz.at[k - 1], syz_sem.at[0, k - 1], syz_sem.at[1, k - 1], yz_partner(k))
        copy.start()
        more.append(copy)
    for k in range(1, n_yz):
        more[k - 1].wait_recv()
        total = total + sum_in_yz[k - 1]
    sums[...] = total

    for copy in last + more:
        copy.wait_send()
    z_done()
    y_done()
    if n_gx > 1:
        pl.when(px + 1 < n_gx)(right.wait_send)
        pl.when(px > 0)(left.wait_send)
    for sent, copy in first_sends:
        pl.when(sent)(copy.wait_send)

    @pl.when(px < YT)
    def _():
        for q in range(n_gx):
            copy = remote(x_prefix.at[q], x_far.at[:, :, chunk(px), :], x2_send.at[q], x2_recv.at[px], {"gx": q})
            pl.when(px != q)(copy.wait_send)


def update_kernel(
    iterate_hbm, sums, live, live_dir, live_res, image, new_iterate, new_residual, new_direction, iterate, sem
):
    copies = fetch(((iterate_hbm, iterate),), sem)
    def total(row):
        return jnp.sum(sums[row : row + 1, :], axis=1, keepdims=True)

    norm_old, curvature, cross, square = total(0), total(1), total(2), total(3)
    step = norm_old / curvature
    norm_new = norm_old + step * (step * square - 2.0 * cross)
    held = live_res[...] - step * image[...]
    copies[0].wait()
    new_iterate[...] = live[...] * iterate[...] + step * live_dir[...]
    new_residual[...] = held
    new_direction[...] = held + norm_new / norm_old * live_dir[...]


def body(sizes, iterate, residual, direction, noise, stencil_base, interp_weights, tile_counts, reach):
    n_gx, n_gy, n_gz = sizes
    n_yz = n_gy * n_gz
    square = (TILES, LANES)
    in_vmem = pl.BlockSpec(memory_space=pltpu.VMEM)
    in_hbm = pl.BlockSpec(memory_space=pltpu.HBM)
    dma = pltpu.SemaphoreType.DMA

    def away(x):
        return pltpu.with_memory_space_constraint(x, pltpu.HBM)

    def keep(x):
        return pltpu.with_memory_space_constraint(x, pltpu.VMEM)

    grid, live_dir, live_res, live = pl.pallas_call(
        spread_kernel,
        out_shape=[pltpu.VMEM((WX, 2, ROWS, LANES), F32)] + [pltpu.VMEM(square, F32)] * 3,
        in_specs=[in_hbm] * 6,
        out_specs=[in_vmem] * 4,
        scratch_shapes=[
            pltpu.VMEM((2, 136, LANES), F32),
            pltpu.SMEM((TILES,), jnp.int32),
            pltpu.SMEM((3, TILES), jnp.int32),
            pltpu.SMEM((3,), F32),
            pltpu.VMEM((12, TILES * LANES), F32),
            pltpu.VMEM(square, F32),
            pltpu.VMEM(square, F32),
            dma((6,)),
        ],
        compiler_params=pltpu.CompilerParams(vmem_limit_bytes=16 << 20),
        name="spread",
    )(
        away(tile_counts),
        away(stencil_base),
        away(reach),
        away(interp_weights),
        away(direction.reshape(square)),
        away(residual.reshape(square)),
    )

    image, sums = pl.pallas_call(
        functools.partial(solve_kernel, sizes),
        out_shape=[pltpu.VMEM(square, F32), pltpu.VMEM((8, LANES), F32)],
        in_specs=[in_hbm] * 4 + [in_vmem] * 4,
        out_specs=[in_vmem] * 2,
        scratch_shapes=[
            pltpu.SMEM((3, TILES), jnp.int32),
            pltpu.SMEM((3,), F32),
            pltpu.VMEM(square, F32),
            pltpu.VMEM((12, TILES * LANES), F32),
            pltpu.VMEM((WX, 2, ROWS, LANES), F32),
            pltpu.VMEM((WX, 2, ROWS, LANES), F32),
            pltpu.VMEM((96, 3 * ROWS), BF16),
            pltpu.VMEM((2, 136, LANES), F32),
            pltpu.VMEM((2, XROWS, LANES), F32),
            pltpu.VMEM((2, MOMENT_STACKS, 8, LANES), F32),
            pltpu.VMEM((2, FIX_STACKS, 8, LANES), F32),
            pltpu.VMEM((3, MOMENT_STACKS, 8, LANES), F32),
            pltpu.VMEM((2, FIX_STACKS, 8, LANES), F32),
            pltpu.VMEM((3, 2, 2, XROWS, LANES), F32),
            pltpu.VMEM((3, 2, XROWS, LANES), F32),
            pltpu.VMEM((2, 2, 2, XROWS, LANES), F32),
            pltpu.VMEM((2, 2, LIVE, LANES), F32),
            pltpu.VMEM((2, 2, 2, LIVE, LANES), F32),
            pltpu.VMEM((2, 2, 2, LIVE, LANES), F32),
            pltpu.VMEM((n_gx, 2, 2, 8, LANES), F32),
            pltpu.VMEM((n_gx, 2, 2, 8, LANES), F32),
            pltpu.VMEM((2, 2, ROWS, LANES), F32),
            pltpu.VMEM(square, F32),
            pltpu.VMEM((8, LANES), F32),
            pltpu.VMEM((15, 8, LANES), F32),
            pltpu.VMEM((8, LANES), F32),
            pltpu.VMEM((15, 8, LANES), F32),
            dma((4,)),
            dma((2, 3)),
            dma((2, 2)),
            dma((2, 3)),
            dma((2, 2)),
            dma((2, 2)),
            dma((YT,)),
            dma((n_gx,)),
            dma((n_gx,)),
            dma((YT,)),
            dma((2, 15)),
            dma((2, 15)),
        ],
        compiler_params=pltpu.CompilerParams(
            collective_id=0, has_side_effects=True, vmem_limit_bytes=24 << 20
        ),
        name="solve",
    )(
        away(stencil_base),
        away(reach),
        away(noise.reshape(square)),
        away(interp_weights),
        keep(grid),
        keep(live_dir),
        keep(live_res),
        keep(live),
    )

    outs = pl.pallas_call(
        update_kernel,
        out_shape=[jax.ShapeDtypeStruct(square, F32)] * 3,
        in_specs=[in_hbm] + [in_vmem] * 5,
        out_specs=[in_vmem] * 3,
        scratch_shapes=[pltpu.VMEM(square, F32), dma((1,))],
        name="update",
    )(away(iterate.reshape(square)), keep(sums), keep(live), keep(live_dir), keep(live_res), keep(image))
    return tuple(out.reshape(-1) for out in outs)


def solution(mesh):
    sizes = tuple(mesh.shape[axis] for axis in ("gx", "gy", "gz"))
    lines = P(("gx", "gy", "gz"))
    return jax.shard_map(
        functools.partial(body, sizes),
        mesh=mesh,
        in_specs=(lines, lines, lines, lines, P(None, ("gx", "gy", "gz")), P(None, ("gx", "gy", "gz")), lines, P()),
        out_specs=(lines, lines, lines),
        check_vma=False,
    )
```

```python
import functools

import jax
import jax.numpy as jnp
from jax import lax
from jax.experimental import pallas as pl
from jax.experimental.pallas import tpu as pltpu
from jax.sharding import PartitionSpec as P

F32 = jnp.float32
BF16 = jnp.bfloat16
LANES = 128
TILES = 128
NX, NY, NZ = 32, 64, 128
WX = NX + 3
TOP = 4
ROWS = 80
LIVE = 72
YT = LIVE // 8
OWN, SPARE, CHANNELS, COPIES = 5, 8, 6, 20
STACKS = -(-WX * YT // COPIES)
PAIRS = STACKS // 2
XROWS = 40
SIDE, FIX = XROWS, XROWS + 8
YMSG = FIX + 2 * XROWS
PACK = SPARE + CHANNELS - OWN
OWNERS = ROWS // 8
MESH = pl.DeviceIdType.MESH


def iota(shape, dim):
    return lax.broadcasted_iota(jnp.int32, shape, dim)


def full(value):
    return jnp.full((1, LANES), value, F32)


def decay(distance, length):
    return jnp.exp(-distance.astype(F32) / length)


def outgoing(kind, source, size, length):
    one = decay(full(1), length) - jnp.exp(full(1.0) / length)
    two = decay(full(2), length) - jnp.exp(full(2.0) / length)
    one, two = one[:, :1], two[:, :1]
    zero = jnp.zeros(source.shape, F32)
    if kind == 0:
        return decay(size + 1 - source, length)
    if kind == 1:
        return jnp.where(source == size, one, jnp.where(source == size + 1, two, zero))
    if kind == 2:
        return jnp.where(source == size + 1, one, zero)
    if kind == 3:
        return decay(source + 1, length)
    if kind == 4:
        return jnp.where(source == -1, two, jnp.where(source == 0, one, zero))
    return jnp.where(source == -1, one, zero)


def incoming(kind, cell, size, length):
    if kind == 0:
        return decay(cell - 1, length)
    if kind == 3:
        return decay(size - 1 - cell, length)
    target = {1: -1, 2: 0, 4: size + 1, 5: size}[kind]
    return jnp.where(cell == target, 1.0, 0.0).astype(F32)


def lane_roles(lane):
    spare = lane >= SPARE
    place = jnp.maximum(lane - SPARE, 0)
    copy = place // CHANNELS
    return jnp.where(spare, place - copy * CHANNELS, -1), jnp.where(spare, copy, -1)


def tile_weights(w8, low):
    along_y = jnp.where(low, pltpu.roll(w8, 4, 0), w8)
    first = jnp.where(low, w8[0:1], w8[1:2]) * along_y
    second = jnp.where(low, w8[2:3], w8[3:4]) * along_y
    return first, second, along_y


def fetch(pairs, sem):
    copies = [pltpu.make_async_copy(src, dst, sem.at[i]) for i, (src, dst) in enumerate(pairs)]
    for copy in copies:
        copy.start()
    return copies


def spread_kernel(
    count_hbm,
    base_hbm,
    reach_hbm,
    w_hbm,
    direction_hbm,
    residual_hbm,
    grid,
    live_dir,
    live_res,
    live,
    table,
    count,
    base,
    reach,
    w,
    direction,
    residual,
    sem,
):
    copies = fetch(
        (
            (reach_hbm, reach),
            (w_hbm, w),
            (count_hbm, count),
            (base_hbm, base),
            (direction_hbm, direction),
            (residual_hbm, residual),
        ),
        sem,
    )

    def clear(x, carry):
        for half in range(2):
            grid[x, half] = jnp.zeros((ROWS, LANES), F32)
        return carry

    lax.fori_loop(0, WX, clear, 0)
    copies[0].wait()
    anchor_x = lax.axis_index("gx") * NX
    anchor_y = lax.axis_index("gy") * NY
    anchor_z = lax.axis_index("gz") * NZ
    length = reach[2] * float(NZ)
    scale = 1.0 / (
        jnp.sqrt(full(reach[0] * float(NX))) * jnp.sqrt(full(reach[1] * float(NY))) * jnp.sqrt(full(length))
    )
    source = iota((136, LANES), 0) - 1
    lane = iota((136, LANES), 1)
    table[0] = decay(jnp.abs(lane - 1 - source), length) * scale
    own = (lane >= OWN) & (lane < SPARE)
    second = jnp.where(own, decay(jnp.abs(lane - OWN + NZ - 1 - source), length), 0.0)
    channel, _ = lane_roles(lane)
    for kind in range(CHANNELS):
        second = jnp.where(channel == kind, outgoing(kind, source, NZ, length), second)
    table[1] = second * scale
    for copy in copies[1:]:
        copy.wait()
    low = iota((8, LANES), 0) < 4
    slot = iota((1, LANES), 1)

    def tile(t, carry):
        at = pl.ds(pl.multiple_of(t * LANES, LANES), LANES)
        w8 = w[0:8, at]
        mask = slot < count[t]
        values = jnp.where(mask, direction[pl.ds(t, 1), :], 0.0)
        live_dir[pl.ds(t, 1), :] = values
        live_res[pl.ds(t, 1), :] = jnp.where(mask, residual[pl.ds(t, 1), :], 0.0)
        live[pl.ds(t, 1), :] = jnp.where(mask, 1.0, 0.0)
        first, second, _ = tile_weights(w8, low)
        x0 = base[0, t] - anchor_x + 1
        y0 = base[1, t] - anchor_y + 1 + TOP
        z0 = base[2, t] - anchor_z + 1
        parts = [[None, None], [None, None]]
        for e in range(4):
            along_z = w[8 + e : 9 + e, at] * values
            row = [table[half, pl.ds(z0 + e, 1), :] for half in range(2)]
            for pair, product in enumerate((first, second)):
                taps = jnp.sum(product * along_z, axis=1, keepdims=True)
                for half in range(2):
                    term = taps * row[half]
                    parts[pair][half] = term if e == 0 else parts[pair][half] + term
        for a in range(4):
            start = y0 if a % 2 == 0 else y0 - 4
            keep = low if a % 2 == 0 else jnp.logical_not(low)
            for half in range(2):
                spot = (x0 + a, half, pl.ds(start, 8), slice(None))
                grid[spot] = grid[spot] + jnp.where(keep, parts[a // 2][half], 0.0)
        return carry

    lax.fori_loop(0, TILES, tile, 0, unroll=16)


def solve_kernel(
    sizes,
    base_hbm,
    reach_hbm,
    noise_hbm,
    w_hbm,
    grid,
    live_dir,
    live_res,
    live,
    image,
    sums,
    base,
    reach,
    noise,
    w,
    smooth,
    basis,
    pick_z,
    pick_x,
    pick_y,
    x_side,
    x_out,
    x_in,
    x_prefix,
    x_far,
    x_fix_in,
    y_msg,
    y_side,
    diagonal,
    z_out,
    z_in,
    y_in,
    y_fix_in,
    diagonal_in,
    z_mixed,
    y_mixed,
    far,
    far_z,
    far_y,
    far_z_in,
    far_y_in,
    sampled,
    sum_out,
    sum_in_x,
    sum_mid,
    sum_in_yz,
    in_sem,
    x_sem,
    x_back_sem,
    x_fix_sem,
    z_sem,
    y_sem,
    y_fix_sem,
    d_sem,
    fz_sem,
    fy_sem,
    sx_sem,
    syz_sem,
):
    n_gx, n_gy, n_gz = sizes
    n_yz = n_gy * n_gz
    px, py, pz = lax.axis_index("gx"), lax.axis_index("gy"), lax.axis_index("gz")
    pyz = py * n_gz + pz

    def at_x(k):
        return {"gx": lax.rem(px + k, n_gx)}

    def at_yz(ky, kz):
        return {"gy": lax.rem(py + ky, n_gy), "gz": lax.rem(pz + kz, n_gz)}

    def around_yz(k):
        other = lax.rem(pyz + k, n_yz)
        return {"gy": other // n_gz, "gz": lax.rem(other, n_gz)}

    barrier = pltpu.get_barrier_semaphore()
    for k in range(1, n_gx):
        pl.semaphore_signal(barrier, inc=1, device_id=at_x(k), device_id_type=MESH)
    for k in range(1, n_yz):
        pl.semaphore_signal(barrier, inc=1, device_id=around_yz(k), device_id_type=MESH)
    copies_in = fetch(((reach_hbm, reach), (base_hbm, base), (noise_hbm, noise), (w_hbm, w)), in_sem)
    copies_in[0].wait()
    length_x, length_y, length_z = reach[0] * float(NX), reach[1] * float(NY), reach[2] * float(NZ)
    sent = []

    def chunk(c):
        return pl.ds(pl.multiple_of(c * 8, 8), 8)

    def send(src, dst, sems, index, device, when=None, slot=None):
        copy = pltpu.make_async_remote_copy(
            src_ref=src,
            dst_ref=dst,
            send_sem=sems.at[0, index],
            recv_sem=sems.at[1, index if slot is None else slot],
            device_id=device,
            device_id_type=MESH,
        )
        if when is None:
            copy.start()
            sent.append(copy.wait_send)
        else:
            pl.when(when)(copy.start)
            sent.append(lambda: pl.when(when)(copy.wait_send))
        return copy

    def way(pos, k, count):
        return jnp.where(pos + k < count, 0, 1)

    def mix(pos, count, size, length, k):
        from_left = pos >= k
        left = jnp.where(from_left, jnp.exp(full(-float(size * (k - 1))) / length), 0.0)
        right = jnp.where(from_left, 0.0, jnp.exp(full(-float(size * (count - k - 1))) / length))
        next_left = jnp.where(from_left, full(1.0), 0.0) if k == 1 else full(0.0)
        next_right = jnp.where(from_left, 0.0, full(1.0)) if count - k == 1 else full(0.0)
        return (left, next_left), (right, next_right)

    sub = iota((8, LANES), 0)
    lane = iota((8, LANES), 1)
    low = sub < 4
    channel, copy_of = lane_roles(lane)
    first_kinds = (channel >= 0) & (channel < 3)
    is_moment = (channel == 0) | (channel == 3)

    step_x = jnp.exp(full(-1.0) / length_x)
    fix_one = step_x - jnp.exp(full(1.0) / length_x)
    fix_two = jnp.exp(full(-2.0) / length_x) - jnp.exp(full(2.0) / length_x)

    def scan(yt, carry):
        rows = pl.ds(pl.multiple_of(yt * 8, 8), 8)
        for half, out in enumerate((x_out, x_side)):
            state = grid[0, half, rows, :]
            smooth[0, half, rows, :] = state
            for x in range(1, WX):
                state = grid[x, half, rows, :] + step_x * state
                smooth[x, half, rows, :] = state
            out[0, rows, :] = state
            edge = [grid[x, half, rows, :] for x in (0, 1, WX - 2, WX - 1)]
            out[2, rows, :] = edge[2] * fix_one + edge[3] * fix_two
            out[3, rows, :] = edge[3] * fix_one
            out[4, rows, :] = edge[0] * fix_two + edge[1] * fix_one
            out[5, rows, :] = edge[0] * fix_one
            state = step_x * edge[3]
            for x in reversed(range(WX - 1)):
                smooth[x, half, rows, :] = smooth[x, half, rows, :] + state
                if x == 0:
                    out[1, rows, :] = state + edge[0]
                else:
                    state = step_x * (state + grid[x, half, rows, :])
        return carry

    lax.fori_loop(0, YT, scan, 0)
    for x in range(WX):
        for half in range(2):
            smooth[x, half, LIVE:ROWS, :] = jnp.zeros((ROWS - LIVE, LANES), F32)
    for plane in range(6):
        total = jnp.zeros((8, LANES), F32)
        for yt in range(YT):
            moved = pltpu.roll(x_side[plane, 8 * yt : 8 * yt + 8, :], (PACK * yt - OWN) % LANES, 1)
            total = jnp.where((lane >= PACK * yt) & (lane < PACK * (yt + 1)), moved, total)
        x_out[plane, LIVE:ROWS, :] = total

    def unpack(packed, yt):
        place = PACK * yt + jnp.where(lane < SPARE, jnp.maximum(lane - OWN, 0), channel + SPARE - OWN)
        return jnp.where(lane < OWN, 0.0, jnp.take_along_axis(packed, place, axis=1))

    pl.semaphore_wait(barrier, n_gx - 1 + n_yz - 1)
    x_right = send(x_out.at[pl.ds(2, 2)], x_fix_in.at[0], x_fix_sem, 0, at_x(1), px + 1 < n_gx)
    x_left = send(x_out.at[pl.ds(4, 2)], x_fix_in.at[1], x_fix_sem, 1, at_x(n_gx - 1), px > 0)
    for c in range(OWNERS):
        send(x_out.at[pl.ds(0, 2), chunk(c), :], x_in.at[px], x_sem, c, {"gx": c}, px != c, px)

    row = iota((96, 3 * ROWS), 0)
    col = iota((96, 3 * ROWS), 1)
    part = col // ROWS
    source = col - part * ROWS - TOP - 1
    cell = row - TOP - 1
    entry = jnp.where((cell >= -1) & (cell <= NY + 1), decay(jnp.abs(cell - source), length_y), 0.0)
    for kind in range(CHANNELS):
        entry = jnp.where(row == ROWS + kind + kind // 3, outgoing(kind, source, NY, length_y), entry)
    entry = jnp.where((source >= -1) & (source <= NY + 1), entry, 0.0)
    entry_high = entry.astype(BF16).astype(F32)
    basis[...] = jnp.where(part == 1, entry - entry_high, entry_high).astype(BF16)

    def contract(planes):
        values = jnp.concatenate(planes, axis=1)
        high = values.astype(BF16)
        rest = (values - high.astype(F32)).astype(BF16)
        stacked = jnp.concatenate([high, high, rest], axis=0)
        return jnp.dot(basis[...], stacked, preferred_element_type=F32)

    def back(q):
        return pltpu.make_async_remote_copy(
            src_ref=x_prefix.at[q],
            dst_ref=x_far.at[:, chunk(px), :],
            send_sem=x_back_sem.at[0, q],
            recv_sem=x_back_sem.at[1, px],
            device_id={"gx": q},
            device_id_type=MESH,
        )

    def contract_own(x):
        result = contract([smooth[x, 0], smooth[x, 1]])
        for half in range(2):
            smooth[x, half] = result[:ROWS, LANES * half : LANES * (half + 1)]
        for side in range(2):
            for kind in range(3):
                line = result[ROWS + 4 * side + kind : ROWS + 4 * side + kind + 1]
                start = 0 if kind == 0 else FIX + XROWS * (kind - 1)
                y_msg[side, pl.ds(start + x, 1), :] = line[:, :LANES]
                y_side[side, kind, pl.ds(x, 1), :] = line[:, LANES:]

    def contract_step(x, carry):
        contract_own(x)
        return carry

    lax.fori_loop(2, WX - 3, contract_step, 0, unroll=5)

    def received(dst, sems, slot):
        pltpu.make_async_remote_copy(
            src_ref=dst,
            dst_ref=dst,
            send_sem=sems.at[0, slot],
            recv_sem=sems.at[1, slot],
            device_id={"gx": slot},
            device_id_type=MESH,
        ).wait_recv()

    ratio = jnp.exp(full(-float(NX)) / length_x)

    @pl.when(px < OWNERS)
    def _():
        x_in[px] = x_out[0:2, chunk(px), :]
        for p in range(n_gx):
            pl.when(px != p)(lambda: received(x_in.at[p], x_sem, p))
        for side, order in enumerate((range(n_gx), reversed(range(n_gx)))):
            total = jnp.zeros((8, LANES), F32)
            for q in order:
                x_prefix[q, side] = total
                total = total * ratio + x_in[q, side]
        x_far[:, chunk(px), :] = x_prefix[px]
        for q in range(n_gx):
            pl.when(px != q)(back(q).start)

    if n_gx > 1:
        pl.when(px > 0)(x_right.wait_recv)
        pl.when(px + 1 < n_gx)(x_left.wait_recv)
    for side, valid, places in ((0, px > 0, (0, 1)), (1, px + 1 < n_gx, (WX - 1, WX - 2))):
        for kind, x in enumerate(places):
            smooth[x, 0, 0:LIVE, :] += jnp.where(valid, x_fix_in[side, kind, 0:LIVE, :], 0.0)
            packed = jnp.where(valid, x_fix_in[side, kind, LIVE:ROWS, :], 0.0)
            for yt in range(YT):
                smooth[x, 1, 8 * yt : 8 * yt + 8, :] += unpack(packed, yt)
    for x in (0, 1, WX - 3, WX - 2, WX - 1):
        contract_own(x)

    stacks = [jnp.zeros((8, LANES), F32) for _ in range(STACKS)]
    for j in range(WX * YT):
        x, yt = divmod(j, YT)
        stack, copy = divmod(j, COPIES)
        stacks[stack] = jnp.where(copy_of == copy, smooth[x, 1, 8 * yt : 8 * yt + 8, :], stacks[stack])
    for pair in range(PAIRS):
        one, two = stacks[2 * pair], stacks[2 * pair + 1]
        z_out[0, pair] = jnp.where(first_kinds, one, pltpu.roll(two, 3, 1))
        z_out[1, pair] = jnp.where(first_kinds, pltpu.roll(one, LANES - 3, 1), two)
    for side in range(2):
        beside = jnp.zeros((8, LANES), F32)
        both = jnp.zeros((8, LANES), F32)
        for j in range(15):
            kind, xt = divmod(j, 5)
            value = y_side[side, kind, 8 * xt : 8 * xt + 8, :]
            moved = pltpu.roll(value, 8 * j, 1) if j else value
            beside = jnp.where((lane >= 8 * j) & (lane < 8 * j + 8), moved, beside)
            both = jnp.where(copy_of == j, value, both)
        y_msg[side, SIDE : SIDE + 8, :] = beside
        diagonal[side] = both
    z_copies = [
        send(z_out.at[way(pz, k, n_gz)], z_in.at[k - 1], z_sem, k - 1, at_yz(0, k)) for k in range(1, n_gz)
    ]
    y_copies = [
        send(y_msg.at[way(py, k, n_gy), pl.ds(0, FIX), :], y_in.at[k - 1], y_sem, k - 1, at_yz(k, 0))
        for k in range(1, n_gy)
    ]
    y_right = y_left = None
    if n_gy > 1:
        fixes = pl.ds(FIX, 2 * XROWS)
        y_right = send(y_msg.at[0, fixes, :], y_fix_in.at[0], y_fix_sem, 0, at_yz(1, 0), py + 1 < n_gy)
        y_left = send(y_msg.at[1, fixes, :], y_fix_in.at[1], y_fix_sem, 1, at_yz(n_gy - 1, 0), py > 0)
    d_copies = {}
    for ky in range(1, n_gy):
        for kz in range(1, n_gz):
            index = (ky - 1) * (n_gz - 1) + kz - 1
            d_copies[ky, kz] = send(
                diagonal.at[way(py, ky, n_gy)], diagonal_in.at[index], d_sem, index, at_yz(ky, kz)
            )

    cell = iota((136, LANES), 0) - 1
    wide = iota((136, LANES), 1)
    pick_z[0] = jnp.where(wide == cell + 1, 1.0, 0.0).astype(F32)
    picked = jnp.where((wide >= OWN) & (wide < SPARE) & (wide - OWN + NZ - 1 == cell), 1.0, 0.0).astype(F32)
    wide_channel, _ = lane_roles(wide)
    for kind in range(CHANNELS):
        picked = jnp.where(wide_channel == kind, incoming(kind, cell, NZ, length_z), picked)
    pick_z[1] = picked
    cell = iota((XROWS, LANES), 0) - 1
    for side in range(2):
        pick_x[side] = incoming(3 * side, cell, NX, length_x)
    cell = iota((ROWS, LANES), 0) - TOP - 1
    for side in range(2):
        pick_y[side] = incoming(3 * side, cell, NY, length_y)

    for c in range(OWNERS):
        pl.when(px != c)(lambda: received(x_far.at[:, chunk(c), :], x_back_sem, c))
    for side in range(2):
        far[side, 0, 0:LIVE, :] = x_far[side, 0:LIVE, :]
        for yt in range(YT):
            far[side, 1, 8 * yt : 8 * yt + 8, :] = unpack(x_far[side, LIVE:ROWS, :], yt)
        for half in range(2):
            far[side, half, LIVE:ROWS, :] = jnp.zeros((ROWS - LIVE, LANES), F32)
    total = jnp.zeros((8, LANES), F32)
    for side in range(2):
        result = contract([far[side, 0], far[side, 1]])
        for half in range(2):
            values = result[:, LANES * half : LANES * (half + 1)]
            far[side, half] = values[:ROWS]
            for to in range(2):
                far_y[to, half, 4 * side : 4 * side + 4, :] = values[ROWS + 4 * to : ROWS + 4 * to + 4]
        for yt in range(YT):
            j = side * YT + yt
            total = jnp.where(copy_of == j, result[8 * yt : 8 * yt + 8, LANES:], total)
    far_z[...] = total
    far_z_copies = [send(far_z, far_z_in.at[k - 1], fz_sem, k - 1, at_yz(0, k)) for k in range(1, n_gz)]
    far_y_copies = {}
    for ky in range(1, n_gy):
        for kz in range(n_gz):
            index = (ky - 1) * n_gz + kz
            far_y_copies[ky, kz] = send(
                far_y.at[way(py, ky, n_gy)], far_y_in.at[index], fy_sem, index, at_yz(ky, kz)
            )

    def channel_weights(k):
        (left, next_left), (right, next_right) = mix(pz, n_gz, NZ, length_z, k)
        return jnp.where(
            first_kinds,
            jnp.where(is_moment, left, next_left),
            jnp.where(channel >= 3, jnp.where(is_moment, right, next_right), 0.0),
        )

    from_z = [[jnp.zeros((8, LANES), F32) for _ in range(PAIRS)] for _ in range(2)]
    for k in range(1, n_gz):
        z_copies[k - 1].wait_recv()
        weights = [jnp.where(is_moment, moment, fix) for moment, fix in mix(pz, n_gz, NZ, length_z, k)]
        for pair in range(PAIRS):
            got = z_in[k - 1, pair]
            for side in range(2):
                from_z[side][pair] = from_z[side][pair] + weights[side] * got
    for pair in range(PAIRS):
        one, two = from_z[0][pair], from_z[1][pair]
        z_mixed[2 * pair] = jnp.where(first_kinds, one, pltpu.roll(two, 3, 1))
        z_mixed[2 * pair + 1] = jnp.where(first_kinds, pltpu.roll(one, LANES - 3, 1), two)
    beside = [jnp.zeros((8, LANES), F32) for _ in range(2)]
    both = [jnp.zeros((8, LANES), F32) for _ in range(2)]
    lines = [[jnp.zeros((8, LANES), F32) for _ in range(XROWS // 8)] for _ in range(2)]
    for ky in range(1, n_gy):
        y_copies[ky - 1].wait_recv()
        weights = mix(py, n_gy, NY, length_y, ky)
        for side in range(2):
            moment, fix = weights[side]
            for tile in range(XROWS // 8):
                lines[side][tile] = lines[side][tile] + moment * y_in[ky - 1, 8 * tile : 8 * tile + 8, :]
            beside[side] = beside[side] + jnp.where(lane < 40, moment, fix) * y_in[ky - 1, SIDE : SIDE + 8, :]
        for kz in range(1, n_gz):
            d_copies[ky, kz].wait_recv()
            got = channel_weights(kz) * diagonal_in[(ky - 1) * (n_gz - 1) + kz - 1]
            for side in range(2):
                moment, fix = weights[side]
                both[side] = both[side] + jnp.where(copy_of < 5, moment, fix) * got
    if n_gy > 1:
        pl.when(py > 0)(y_right.wait_recv)
        pl.when(py + 1 < n_gy)(y_left.wait_recv)
    for side, valid in enumerate((py > 0, py + 1 < n_gy)):
        for tile in range(XROWS // 8):
            y_mixed[side, 0, 0, 8 * tile : 8 * tile + 8, :] = lines[side][tile]
        for kind in range(1, 3):
            start = XROWS * (kind - 1)
            y_mixed[side, kind, 0] = jnp.where(valid, y_fix_in[side, start : start + XROWS, :], 0.0)
        for j in range(15):
            kind, xt = divmod(j, 5)
            moved = pltpu.roll(beside[side], LANES - 8 * j, 1) if j else beside[side]
            y_mixed[side, kind, 1, 8 * xt : 8 * xt + 8, :] = jnp.where(
                lane < SPARE, moved, jnp.where(copy_of == j, both[side], 0.0)
            )

    def expand(x, carry):
        for half in range(2):
            line = [
                [y_mixed[side, kind, half, pl.ds(x, 1), :] for kind in range(3)] for side in range(2)
            ]
            for yt in range(YT):
                rows = slice(8 * yt, 8 * yt + 8)
                value = smooth[x, half, rows, :]
                if half == 1:
                    j = x * YT + yt
                    stack = j // COPIES
                    value = jnp.where(
                        lane < SPARE, value, jnp.where(copy_of == j - stack * COPIES, z_mixed[stack], 0.0)
                    )
                for side in range(2):
                    value = value + pick_y[side, rows, :] * line[side][0]
                if yt == 0:
                    value = value + jnp.where(sub == 4, line[0][1], jnp.where(sub == 5, line[0][2], 0.0))
                if yt == YT - 1:
                    value = value + jnp.where(sub == 6, line[1][1], jnp.where(sub == 5, line[1][2], 0.0))
                smooth[x, half, rows, :] = value
        return carry

    lax.fori_loop(0, WX, expand, 0)
    for copy in copies_in[1:]:
        copy.wait()

    def tile_spot(t):
        at = pl.ds(pl.multiple_of(t * LANES, LANES), LANES)
        x0 = jnp.clip(base[0, t] - px * NX + 1, 0, NX - 1)
        y0 = jnp.clip(base[1, t] - py * NY + 1, 0, NY - 1) + TOP
        z0 = jnp.clip(base[2, t] - pz * NZ + 1, 0, NZ - 1)
        return at, x0, y0, z0

    def gather(rows, weights, at, z0):
        total = None
        for e in range(4):
            pick = [pick_z[half, pl.ds(z0 + e, 1), :] for half in range(2)]
            inner = None
            for cells, weight in zip(rows, weights):
                taps = jnp.sum(cells[0] * pick[0] + cells[1] * pick[1], axis=1, keepdims=True)
                inner = weight * taps if inner is None else inner + weight * taps
            inner = inner * w[8 + e : 9 + e, at]
            total = inner if e == 0 else total + inner
        return jnp.sum(total, axis=0, keepdims=True)

    def near(t, carry):
        at, x0, y0, z0 = tile_spot(t)
        first, second, _ = tile_weights(w[0:8, at], low)
        rows = [
            [
                jnp.where(
                    low, smooth[x0 + a, half, pl.ds(y0, 8), :], smooth[x0 + a + 1, half, pl.ds(y0 - 4, 8), :]
                )
                for half in range(2)
            ]
            for a in (0, 2)
        ]
        sampled[pl.ds(t, 1), :] = gather(rows, (first, second), at, z0)
        return carry

    lax.fori_loop(0, TILES, near, 0, unroll=16)

    from_z = jnp.zeros((8, LANES), F32)
    for k in range(1, n_gz):
        far_z_copies[k - 1].wait_recv()
        from_z = from_z + channel_weights(k) * far_z_in[k - 1]
    lines = [[jnp.zeros((8, LANES), F32) for _ in range(2)] for _ in range(2)]
    for ky in range(1, n_gy):
        weights = mix(py, n_gy, NY, length_y, ky)
        weights = [jnp.where((sub == 0) | (sub == 4), moment, fix) for moment, fix in weights]
        for kz in range(n_gz):
            far_y_copies[ky, kz].wait_recv()
            index = (ky - 1) * n_gz + kz
            got = [far_y_in[index, half] for half in range(2)]
            if kz == 0:
                got[1] = jnp.where(lane < SPARE, got[1], 0.0)
            else:
                got = [None, jnp.where(copy_of == 0, channel_weights(kz) * got[1], 0.0)]
            for side in range(2):
                for half in range(2):
                    if got[half] is not None:
                        lines[side][half] = lines[side][half] + weights[side] * got[half]
    for x in range(2):
        for half in range(2):
            line = [[lines[side][half][4 * x + kind : 4 * x + kind + 1] for kind in range(3)] for side in range(2)]
            for yt in range(YT):
                rows = slice(8 * yt, 8 * yt + 8)
                value = far[x, half, rows, :]
                if half == 1:
                    value = jnp.where(lane < SPARE, value, jnp.where(copy_of == x * YT + yt, from_z, 0.0))
                for side in range(2):
                    value = value + pick_y[side, rows, :] * line[side][0]
                if yt == 0:
                    value = value + jnp.where(sub == 4, line[0][1], jnp.where(sub == 5, line[0][2], 0.0))
                if yt == YT - 1:
                    value = value + jnp.where(sub == 6, line[1][1], jnp.where(sub == 5, line[1][2], 0.0))
                far[x, half, rows, :] = value

    def distant(t, carry):
        at, x0, y0, z0 = tile_spot(t)
        w8 = w[0:8, at]
        _, _, along_y = tile_weights(w8, low)
        along_x = []
        for side in range(2):
            total = None
            for a in range(4):
                term = w8[a : a + 1] * pick_x[side, pl.ds(x0 + a, 1), :]
                total = term if a == 0 else total + term
            along_x.append(total)
        weight = jnp.where(low, along_x[0], along_x[1]) * along_y
        rows = [jnp.where(low, far[0, half, pl.ds(y0, 8), :], far[1, half, pl.ds(y0 - 4, 8), :]) for half in range(2)]
        sampled[pl.ds(t, 1), :] += gather([rows], [weight], at, z0)
        return carry

    lax.fori_loop(0, TILES, distant, 0, unroll=16)

    value = live[...] * (sampled[...] + noise[...] * live_dir[...])
    image[...] = value
    pairs = (
        (live_res[...], live_res[...]),
        (live_dir[...], value),
        (live_res[...], value),
        (value, value),
    )
    sum_out[...] = jnp.concatenate(
        [jnp.sum(a * b, axis=0, keepdims=True) for a, b in pairs] + [jnp.zeros((4, LANES), F32)], axis=0
    )
    copies = [send(sum_out, sum_in_x.at[k - 1], sx_sem, k - 1, at_x(k)) for k in range(1, n_gx)]
    total = sum_out[...]
    for k in range(1, n_gx):
        copies[k - 1].wait_recv()
        total = total + sum_in_x[k - 1]
    sum_mid[...] = total
    copies = [send(sum_mid, sum_in_yz.at[k - 1], syz_sem, k - 1, around_yz(k)) for k in range(1, n_yz)]
    for k in range(1, n_yz):
        copies[k - 1].wait_recv()
        total = total + sum_in_yz[k - 1]
    sums[...] = total
    for wait in sent:
        wait()

    @pl.when(px < OWNERS)
    def _():
        for q in range(n_gx):
            pl.when(px != q)(back(q).wait_send)


def update_kernel(
    iterate_hbm, sums, live, live_dir, live_res, image, new_iterate, new_residual, new_direction, iterate, sem
):
    copies = fetch(((iterate_hbm, iterate),), sem)
    def total(row):
        return jnp.sum(sums[row : row + 1, :], axis=1, keepdims=True)

    norm_old, curvature, cross, square = total(0), total(1), total(2), total(3)
    step = norm_old / curvature
    norm_new = norm_old + step * (step * square - 2.0 * cross)
    held = live_res[...] - step * image[...]
    copies[0].wait()
    new_iterate[...] = live[...] * iterate[...] + step * live_dir[...]
    new_residual[...] = held
    new_direction[...] = held + norm_new / norm_old * live_dir[...]


def body(sizes, iterate, residual, direction, noise, stencil_base, interp_weights, tile_counts, reach):
    n_gx, n_gy, n_gz = sizes
    n_yz = n_gy * n_gz
    square = (TILES, LANES)
    in_vmem = pl.BlockSpec(memory_space=pltpu.VMEM)
    in_hbm = pl.BlockSpec(memory_space=pltpu.HBM)
    dma = pltpu.SemaphoreType.DMA

    def away(x):
        return pltpu.with_memory_space_constraint(x, pltpu.HBM)

    def keep(x):
        return pltpu.with_memory_space_constraint(x, pltpu.VMEM)

    grid, live_dir, live_res, live = pl.pallas_call(
        spread_kernel,
        out_shape=[pltpu.VMEM((WX, 2, ROWS, LANES), F32)] + [pltpu.VMEM(square, F32)] * 3,
        in_specs=[in_hbm] * 6,
        out_specs=[in_vmem] * 4,
        scratch_shapes=[
            pltpu.VMEM((2, 136, LANES), F32),
            pltpu.SMEM((TILES,), jnp.int32),
            pltpu.SMEM((3, TILES), jnp.int32),
            pltpu.SMEM((3,), F32),
            pltpu.VMEM((12, TILES * LANES), F32),
            pltpu.VMEM(square, F32),
            pltpu.VMEM(square, F32),
            dma((6,)),
        ],
        compiler_params=pltpu.CompilerParams(vmem_limit_bytes=16 << 20),
        name="spread",
    )(
        away(tile_counts),
        away(stencil_base),
        away(reach),
        away(interp_weights),
        away(direction.reshape(square)),
        away(residual.reshape(square)),
    )

    image, sums = pl.pallas_call(
        functools.partial(solve_kernel, sizes),
        out_shape=[pltpu.VMEM(square, F32), pltpu.VMEM((8, LANES), F32)],
        in_specs=[in_hbm] * 4 + [in_vmem] * 4,
        out_specs=[in_vmem] * 2,
        scratch_shapes=[
            pltpu.SMEM((3, TILES), jnp.int32),
            pltpu.SMEM((3,), F32),
            pltpu.VMEM(square, F32),
            pltpu.VMEM((12, TILES * LANES), F32),
            pltpu.VMEM((WX, 2, ROWS, LANES), F32),
            pltpu.VMEM((96, 3 * ROWS), BF16),
            pltpu.VMEM((2, 136, LANES), F32),
            pltpu.VMEM((2, XROWS, LANES), F32),
            pltpu.VMEM((2, ROWS, LANES), F32),
            pltpu.VMEM((6, LIVE, LANES), F32),
            pltpu.VMEM((6, ROWS, LANES), F32),
            pltpu.VMEM((n_gx, 2, 8, LANES), F32),
            pltpu.VMEM((n_gx, 2, 8, LANES), F32),
            pltpu.VMEM((2, ROWS, LANES), F32),
            pltpu.VMEM((2, 2, ROWS, LANES), F32),
            pltpu.VMEM((2, YMSG, LANES), F32),
            pltpu.VMEM((2, 3, XROWS, LANES), F32),
            pltpu.VMEM((2, 8, LANES), F32),
            pltpu.VMEM((2, PAIRS, 8, LANES), F32),
            pltpu.VMEM((3, PAIRS, 8, LANES), F32),
            pltpu.VMEM((3, FIX, LANES), F32),
            pltpu.VMEM((2, 2 * XROWS, LANES), F32),
            pltpu.VMEM((9, 8, LANES), F32),
            pltpu.VMEM((STACKS, 8, LANES), F32),
            pltpu.VMEM((2, 3, 2, XROWS, LANES), F32),
            pltpu.VMEM((2, 2, ROWS, LANES), F32),
            pltpu.VMEM((8, LANES), F32),
            pltpu.VMEM((2, 2, 8, LANES), F32),
            pltpu.VMEM((3, 8, LANES), F32),
            pltpu.VMEM((12, 2, 8, LANES), F32),
            pltpu.VMEM(square, F32),
            pltpu.VMEM((8, LANES), F32),
            pltpu.VMEM((15, 8, LANES), F32),
            pltpu.VMEM((8, LANES), F32),
            pltpu.VMEM((15, 8, LANES), F32),
            dma((4,)),
            dma((2, n_gx)),
            dma((2, n_gx)),
            dma((2, 2)),
            dma((2, 3)),
            dma((2, 3)),
            dma((2, 2)),
            dma((2, 9)),
            dma((2, 3)),
            dma((2, 12)),
            dma((2, 15)),
            dma((2, 15)),
        ],
        compiler_params=pltpu.CompilerParams(
            collective_id=0, has_side_effects=True, vmem_limit_bytes=24 << 20
        ),
        name="solve",
    )(
        away(stencil_base),
        away(reach),
        away(noise.reshape(square)),
        away(interp_weights),
        keep(grid),
        keep(live_dir),
        keep(live_res),
        keep(live),
    )

    outs = pl.pallas_call(
        update_kernel,
        out_shape=[jax.ShapeDtypeStruct(square, F32)] * 3,
        in_specs=[in_hbm] + [in_vmem] * 5,
        out_specs=[in_vmem] * 3,
        scratch_shapes=[pltpu.VMEM(square, F32), dma((1,))],
        name="update",
    )(away(iterate.reshape(square)), keep(sums), keep(live), keep(live_dir), keep(live_res), keep(image))
    return tuple(out.reshape(-1) for out in outs)


def solution(mesh):
    sizes = tuple(mesh.shape[axis] for axis in ("gx", "gy", "gz"))
    lines = P(("gx", "gy", "gz"))
    return jax.shard_map(
        functools.partial(body, sizes),
        mesh=mesh,
        in_specs=(lines, lines, lines, lines, P(None, ("gx", "gy", "gz")), P(None, ("gx", "gy", "gz")), lines, P()),
        out_specs=(lines, lines, lines),
        check_vma=False,
    )
```

```python
import functools

import jax
import jax.numpy as jnp
from jax import lax
from jax.experimental import pallas as pl
from jax.experimental.pallas import tpu as pltpu
from jax.sharding import PartitionSpec as P

F32 = jnp.float32
BF16 = jnp.bfloat16
LANES = 128
TILES = 128
NX, NY, NZ = 32, 64, 128
WX = NX + 3
TOP = 4
ROWS = 80
LIVE = 72
YT = LIVE // 8
OWN, SPARE, CHANNELS, COPIES = 5, 8, 6, 20
STACKS = -(-WX * YT // COPIES)
PAIRS = STACKS // 2
XROWS = 40
SIDE, FIX = XROWS, XROWS + 8
YMSG = FIX + 2 * XROWS
PACK = SPARE + CHANNELS - OWN
OWNERS = ROWS // 8
MESH = pl.DeviceIdType.MESH


def iota(shape, dim):
    return lax.broadcasted_iota(jnp.int32, shape, dim)


def full(value):
    return jnp.full((1, LANES), value, F32)


def decay(distance, length):
    return jnp.exp(-distance.astype(F32) / length)


def outgoing(kind, source, size, length):
    one = decay(full(1), length) - jnp.exp(full(1.0) / length)
    two = decay(full(2), length) - jnp.exp(full(2.0) / length)
    one, two = one[:, :1], two[:, :1]
    zero = jnp.zeros(source.shape, F32)
    if kind == 0:
        return decay(size + 1 - source, length)
    if kind == 1:
        return jnp.where(source == size, one, jnp.where(source == size + 1, two, zero))
    if kind == 2:
        return jnp.where(source == size + 1, one, zero)
    if kind == 3:
        return decay(source + 1, length)
    if kind == 4:
        return jnp.where(source == -1, two, jnp.where(source == 0, one, zero))
    return jnp.where(source == -1, one, zero)


def incoming(kind, cell, size, length):
    if kind == 0:
        return decay(cell - 1, length)
    if kind == 3:
        return decay(size - 1 - cell, length)
    target = {1: -1, 2: 0, 4: size + 1, 5: size}[kind]
    return jnp.where(cell == target, 1.0, 0.0).astype(F32)


def lane_roles(lane):
    spare = lane >= SPARE
    place = jnp.maximum(lane - SPARE, 0)
    copy = place // CHANNELS
    return jnp.where(spare, place - copy * CHANNELS, -1), jnp.where(spare, copy, -1)


def tile_weights(w8, low):
    along_y = jnp.where(low, pltpu.roll(w8, 4, 0), w8)
    first = jnp.where(low, w8[0:1], w8[1:2]) * along_y
    second = jnp.where(low, w8[2:3], w8[3:4]) * along_y
    return first, second, along_y


def fetch(pairs, sem):
    copies = [pltpu.make_async_copy(src, dst, sem.at[i]) for i, (src, dst) in enumerate(pairs)]
    for copy in copies:
        copy.start()
    return copies


def spread_kernel(
    count_hbm,
    base_hbm,
    reach_hbm,
    w_hbm,
    direction_hbm,
    residual_hbm,
    grid,
    live_dir,
    live_res,
    live,
    lengths,
    table,
    count,
    base,
    reach,
    w,
    direction,
    residual,
    sem,
):
    copies = fetch(
        (
            (reach_hbm, reach),
            (w_hbm, w),
            (count_hbm, count),
            (base_hbm, base),
            (direction_hbm, direction),
            (residual_hbm, residual),
        ),
        sem,
    )

    def clear(x, carry):
        for half in range(2):
            grid[x, half] = jnp.zeros((ROWS, LANES), F32)
        return carry

    lax.fori_loop(0, WX, clear, 0)
    copies[0].wait()
    anchor_x = lax.axis_index("gx") * NX
    anchor_y = lax.axis_index("gy") * NY
    anchor_z = lax.axis_index("gz") * NZ
    length = reach[2] * float(NZ)
    scale = 1.0 / (
        jnp.sqrt(full(reach[0] * float(NX))) * jnp.sqrt(full(reach[1] * float(NY))) * jnp.sqrt(full(length))
    )
    source = iota((136, LANES), 0) - 1
    lane = iota((136, LANES), 1)
    for i, size in enumerate((NX, NY, NZ)):
        lengths[i : i + 1, :] = full(reach[i] * float(size))
    table[0] = decay(jnp.abs(lane - 1 - source), length) * scale
    own = (lane >= OWN) & (lane < SPARE)
    second = jnp.where(own, decay(jnp.abs(lane - OWN + NZ - 1 - source), length), 0.0)
    channel, _ = lane_roles(lane)
    for kind in range(CHANNELS):
        second = jnp.where(channel == kind, outgoing(kind, source, NZ, length), second)
    table[1] = second * scale
    for copy in copies[1:]:
        copy.wait()
    low = iota((8, LANES), 0) < 4
    slot = iota((1, LANES), 1)

    def tile(t, carry):
        at = pl.ds(pl.multiple_of(t * LANES, LANES), LANES)
        w8 = w[0:8, at]
        mask = slot < count[t]
        values = jnp.where(mask, direction[pl.ds(t, 1), :], 0.0)
        live_dir[pl.ds(t, 1), :] = values
        live_res[pl.ds(t, 1), :] = jnp.where(mask, residual[pl.ds(t, 1), :], 0.0)
        live[pl.ds(t, 1), :] = jnp.where(mask, 1.0, 0.0)
        first, second, _ = tile_weights(w8, low)
        x0 = base[0, t] - anchor_x + 1
        y0 = base[1, t] - anchor_y + 1 + TOP
        z0 = base[2, t] - anchor_z + 1
        parts = [[None, None], [None, None]]
        for e in range(4):
            along_z = w[8 + e : 9 + e, at] * values
            row = [table[half, pl.ds(z0 + e, 1), :] for half in range(2)]
            for pair, product in enumerate((first, second)):
                taps = jnp.sum(product * along_z, axis=1, keepdims=True)
                for half in range(2):
                    term = taps * row[half]
                    parts[pair][half] = term if e == 0 else parts[pair][half] + term
        for a in range(4):
            start = y0 if a % 2 == 0 else y0 - 4
            keep = low if a % 2 == 0 else jnp.logical_not(low)
            for half in range(2):
                spot = (x0 + a, half, pl.ds(start, 8), slice(None))
                grid[spot] = grid[spot] + jnp.where(keep, parts[a // 2][half], 0.0)
        return carry

    lax.fori_loop(0, TILES, tile, 0, unroll=16)


def solve_kernel(
    sizes,
    base_hbm,
    iterate_hbm,
    noise_hbm,
    w_hbm,
    lengths,
    grid,
    live_dir,
    live_res,
    live,
    image,
    sums,
    iterate,
    base,
    spot,
    noise,
    w,
    smooth,
    basis,
    pick_z,
    pick_x,
    pick_y,
    x_side,
    x_out,
    x_in,
    x_prefix,
    x_far,
    x_fix_in,
    y_msg,
    y_side,
    diagonal,
    z_out,
    z_in,
    y_in,
    y_fix_in,
    diagonal_in,
    z_mixed,
    y_mixed,
    far,
    far_z,
    far_y,
    far_z_in,
    far_y_in,
    sampled,
    sum_out,
    sum_in_x,
    sum_mid,
    sum_in_yz,
    in_sem,
    x_sem,
    x_back_sem,
    x_fix_sem,
    z_sem,
    y_sem,
    y_fix_sem,
    d_sem,
    fz_sem,
    fy_sem,
    sx_sem,
    syz_sem,
):
    n_gx, n_gy, n_gz = sizes
    n_yz = n_gy * n_gz
    px, py, pz = lax.axis_index("gx"), lax.axis_index("gy"), lax.axis_index("gz")
    pyz = py * n_gz + pz

    def at_x(k):
        return {"gx": lax.rem(px + k, n_gx)}

    def at_yz(ky, kz):
        return {"gy": lax.rem(py + ky, n_gy), "gz": lax.rem(pz + kz, n_gz)}

    def around_yz(k):
        other = lax.rem(pyz + k, n_yz)
        return {"gy": other // n_gz, "gz": lax.rem(other, n_gz)}

    barrier = pltpu.get_barrier_semaphore()
    for k in range(1, n_gx):
        pl.semaphore_signal(barrier, inc=1, device_id=at_x(k), device_id_type=MESH)
    for k in range(1, n_yz):
        pl.semaphore_signal(barrier, inc=1, device_id=around_yz(k), device_id_type=MESH)
    copies_in = fetch(((base_hbm, base), (noise_hbm, noise), (w_hbm, w), (iterate_hbm, iterate)), in_sem)
    length_x, length_y, length_z = (lengths[i : i + 1, 0:1] for i in range(3))
    sent = []

    def chunk(c):
        return pl.ds(pl.multiple_of(c * 8, 8), 8)

    def send(src, dst, sems, index, device, when=None, slot=None):
        copy = pltpu.make_async_remote_copy(
            src_ref=src,
            dst_ref=dst,
            send_sem=sems.at[0, index],
            recv_sem=sems.at[1, index if slot is None else slot],
            device_id=device,
            device_id_type=MESH,
        )
        if when is None:
            copy.start()
            sent.append(copy.wait_send)
        else:
            pl.when(when)(copy.start)
            sent.append(lambda: pl.when(when)(copy.wait_send))
        return copy

    def way(pos, k, count):
        return jnp.where(pos + k < count, 0, 1)

    def mix(pos, count, size, length, k):
        from_left = pos >= k
        left = jnp.where(from_left, jnp.exp(full(-float(size * (k - 1))) / length), 0.0)
        right = jnp.where(from_left, 0.0, jnp.exp(full(-float(size * (count - k - 1))) / length))
        next_left = jnp.where(from_left, full(1.0), 0.0) if k == 1 else full(0.0)
        next_right = jnp.where(from_left, 0.0, full(1.0)) if count - k == 1 else full(0.0)
        return (left, next_left), (right, next_right)

    sub = iota((8, LANES), 0)
    lane = iota((8, LANES), 1)
    low = sub < 4
    channel, copy_of = lane_roles(lane)
    first_kinds = (channel >= 0) & (channel < 3)
    is_moment = (channel == 0) | (channel == 3)

    step_x = jnp.exp(full(-1.0) / length_x)
    fix_one = step_x - jnp.exp(full(1.0) / length_x)
    fix_two = jnp.exp(full(-2.0) / length_x) - jnp.exp(full(2.0) / length_x)

    def scan(yt, carry):
        rows = pl.ds(pl.multiple_of(yt * 8, 8), 8)
        for half, out in enumerate((x_out, x_side)):
            state = grid[0, half, rows, :]
            smooth[0, half, rows, :] = state
            for x in range(1, WX):
                state = grid[x, half, rows, :] + step_x * state
                smooth[x, half, rows, :] = state
            out[0, rows, :] = state
            edge = [grid[x, half, rows, :] for x in (0, 1, WX - 2, WX - 1)]
            out[2, rows, :] = edge[2] * fix_one + edge[3] * fix_two
            out[3, rows, :] = edge[3] * fix_one
            out[4, rows, :] = edge[0] * fix_two + edge[1] * fix_one
            out[5, rows, :] = edge[0] * fix_one
            state = step_x * edge[3]
            for x in reversed(range(WX - 1)):
                smooth[x, half, rows, :] = smooth[x, half, rows, :] + state
                if x == 0:
                    out[1, rows, :] = state + edge[0]
                else:
                    state = step_x * (state + grid[x, half, rows, :])
        return carry

    lax.fori_loop(0, YT, scan, 0, unroll=3)
    for x in range(WX):
        for half in range(2):
            smooth[x, half, LIVE:ROWS, :] = jnp.zeros((ROWS - LIVE, LANES), F32)
    for plane in range(6):
        total = jnp.zeros((8, LANES), F32)
        for yt in range(YT):
            moved = pltpu.roll(x_side[plane, 8 * yt : 8 * yt + 8, :], (PACK * yt - OWN) % LANES, 1)
            total = jnp.where((lane >= PACK * yt) & (lane < PACK * (yt + 1)), moved, total)
        x_out[plane, LIVE:ROWS, :] = total

    def unpack(packed, yt):
        place = PACK * yt + jnp.where(lane < SPARE, jnp.maximum(lane - OWN, 0), channel + SPARE - OWN)
        return jnp.where(lane < OWN, 0.0, jnp.take_along_axis(packed, place, axis=1))

    pl.semaphore_wait(barrier, n_gx - 1 + n_yz - 1)
    x_right = send(x_out.at[pl.ds(2, 2)], x_fix_in.at[0], x_fix_sem, 0, at_x(1), px + 1 < n_gx)
    x_left = send(x_out.at[pl.ds(4, 2)], x_fix_in.at[1], x_fix_sem, 1, at_x(n_gx - 1), px > 0)
    for c in range(OWNERS):
        send(x_out.at[pl.ds(0, 2), chunk(c), :], x_in.at[px], x_sem, c, {"gx": c}, px != c, px)

    row = iota((96, 3 * ROWS), 0)
    col = iota((96, 3 * ROWS), 1)
    part = col // ROWS
    source = col - part * ROWS - TOP - 1
    cell = row - TOP - 1
    entry = jnp.where((cell >= -1) & (cell <= NY + 1), decay(jnp.abs(cell - source), length_y), 0.0)
    for kind in range(CHANNELS):
        entry = jnp.where(row == ROWS + kind + kind // 3, outgoing(kind, source, NY, length_y), entry)
    entry = jnp.where((source >= -1) & (source <= NY + 1), entry, 0.0)
    entry_high = entry.astype(BF16).astype(F32)
    basis[...] = jnp.where(part == 1, entry - entry_high, entry_high).astype(BF16)

    def contract(planes):
        values = jnp.concatenate(planes, axis=1)
        high = values.astype(BF16)
        rest = (values - high.astype(F32)).astype(BF16)
        stacked = jnp.concatenate([high, high, rest], axis=0)
        return jnp.dot(basis[...], stacked, preferred_element_type=F32)

    def back(q):
        return pltpu.make_async_remote_copy(
            src_ref=x_prefix.at[q],
            dst_ref=x_far.at[:, chunk(px), :],
            send_sem=x_back_sem.at[0, q],
            recv_sem=x_back_sem.at[1, px],
            device_id={"gx": q},
            device_id_type=MESH,
        )

    def contract_own(x):
        result = contract([smooth[x, 0], smooth[x, 1]])
        for half in range(2):
            smooth[x, half] = result[:ROWS, LANES * half : LANES * (half + 1)]
        for side in range(2):
            for kind in range(3):
                line = result[ROWS + 4 * side + kind : ROWS + 4 * side + kind + 1]
                start = 0 if kind == 0 else FIX + XROWS * (kind - 1)
                y_msg[side, pl.ds(start + x, 1), :] = line[:, :LANES]
                y_side[side, kind, pl.ds(x, 1), :] = line[:, LANES:]

    def contract_step(x, carry):
        contract_own(x)
        return carry

    lax.fori_loop(2, WX - 3, contract_step, 0, unroll=5)

    contract_own(WX - 3)
    stacks = [jnp.zeros((8, LANES), F32) for _ in range(STACKS)]

    def stacked_planes(planes):
        for x in planes:
            for yt in range(YT):
                stack, copy = divmod(x * YT + yt, COPIES)
                stacks[stack] = jnp.where(copy_of == copy, smooth[x, 1, 8 * yt : 8 * yt + 8, :], stacks[stack])

    stacked_planes(range(2, WX - 2))
    copies_in[0].wait()

    def locate(t, carry):
        spot[0, t] = jnp.clip(base[0, t] - px * NX + 1, 0, NX - 1)
        spot[1, t] = jnp.clip(base[1, t] - py * NY + 1, 0, NY - 1) + TOP
        spot[2, t] = jnp.clip(base[2, t] - pz * NZ + 1, 0, NZ - 1)
        return carry

    lax.fori_loop(0, TILES, locate, 0, unroll=8)
    if n_gx > 1:
        pl.when(px > 0)(x_right.wait_recv)
        pl.when(px + 1 < n_gx)(x_left.wait_recv)
    for side, valid, places in ((0, px > 0, (0, 1)), (1, px + 1 < n_gx, (WX - 1, WX - 2))):
        for kind, x in enumerate(places):
            smooth[x, 0, 0:LIVE, :] += jnp.where(valid, x_fix_in[side, kind, 0:LIVE, :], 0.0)
            packed = jnp.where(valid, x_fix_in[side, kind, LIVE:ROWS, :], 0.0)
            for yt in range(YT):
                smooth[x, 1, 8 * yt : 8 * yt + 8, :] += unpack(packed, yt)
    for x in (0, 1, WX - 2, WX - 1):
        contract_own(x)

    stacked_planes((0, 1, WX - 2, WX - 1))
    for pair in range(PAIRS):
        one, two = stacks[2 * pair], stacks[2 * pair + 1]
        z_out[0, pair] = jnp.where(first_kinds, one, pltpu.roll(two, 3, 1))
        z_out[1, pair] = jnp.where(first_kinds, pltpu.roll(one, LANES - 3, 1), two)
    for side in range(2):
        beside = jnp.zeros((8, LANES), F32)
        both = jnp.zeros((8, LANES), F32)
        for j in range(15):
            kind, xt = divmod(j, 5)
            value = y_side[side, kind, 8 * xt : 8 * xt + 8, :]
            moved = pltpu.roll(value, 8 * j, 1) if j else value
            beside = jnp.where((lane >= 8 * j) & (lane < 8 * j + 8), moved, beside)
            both = jnp.where(copy_of == j, value, both)
        y_msg[side, SIDE : SIDE + 8, :] = beside
        diagonal[side] = both
    z_copies = [
        send(z_out.at[way(pz, k, n_gz)], z_in.at[k - 1], z_sem, k - 1, at_yz(0, k)) for k in range(1, n_gz)
    ]
    y_copies = [
        send(y_msg.at[way(py, k, n_gy), pl.ds(0, FIX), :], y_in.at[k - 1], y_sem, k - 1, at_yz(k, 0))
        for k in range(1, n_gy)
    ]
    y_right = y_left = None
    if n_gy > 1:
        fixes = pl.ds(FIX, 2 * XROWS)
        y_right = send(y_msg.at[0, fixes, :], y_fix_in.at[0], y_fix_sem, 0, at_yz(1, 0), py + 1 < n_gy)
        y_left = send(y_msg.at[1, fixes, :], y_fix_in.at[1], y_fix_sem, 1, at_yz(n_gy - 1, 0), py > 0)
    d_copies = {}
    for ky in range(1, n_gy):
        for kz in range(1, n_gz):
            index = (ky - 1) * (n_gz - 1) + kz - 1
            d_copies[ky, kz] = send(
                diagonal.at[way(py, ky, n_gy)], diagonal_in.at[index], d_sem, index, at_yz(ky, kz)
            )

    def received(dst, sems, slot):
        pltpu.make_async_remote_copy(
            src_ref=dst,
            dst_ref=dst,
            send_sem=sems.at[0, slot],
            recv_sem=sems.at[1, slot],
            device_id={"gx": slot},
            device_id_type=MESH,
        ).wait_recv()

    ratio = jnp.exp(full(-float(NX)) / length_x)

    @pl.when(px < OWNERS)
    def _():
        x_in[px] = x_out[0:2, chunk(px), :]
        for p in range(n_gx):
            pl.when(px != p)(lambda: received(x_in.at[p], x_sem, p))
        for side, order in enumerate((range(n_gx), reversed(range(n_gx)))):
            total = jnp.zeros((8, LANES), F32)
            for q in order:
                x_prefix[q, side] = total
                total = total * ratio + x_in[q, side]
        x_far[:, chunk(px), :] = x_prefix[px]
        for q in range(n_gx):
            pl.when(px != q)(back(q).start)

    cell = iota((136, LANES), 0) - 1
    wide = iota((136, LANES), 1)
    pick_z[0] = jnp.where(wide == cell + 1, 1.0, 0.0).astype(F32)
    picked = jnp.where((wide >= OWN) & (wide < SPARE) & (wide - OWN + NZ - 1 == cell), 1.0, 0.0).astype(F32)
    wide_channel, _ = lane_roles(wide)
    for kind in range(CHANNELS):
        picked = jnp.where(wide_channel == kind, incoming(kind, cell, NZ, length_z), picked)
    pick_z[1] = picked
    cell = iota((XROWS, LANES), 0) - 1
    for side in range(2):
        pick_x[side] = incoming(3 * side, cell, NX, length_x)
    cell = iota((ROWS, LANES), 0) - TOP - 1
    for side in range(2):
        pick_y[side] = incoming(3 * side, cell, NY, length_y)

    for c in range(OWNERS):
        pl.when(px != c)(lambda: received(x_far.at[:, chunk(c), :], x_back_sem, c))
    for side in range(2):
        far[side, 0, 0:LIVE, :] = x_far[side, 0:LIVE, :]
        for yt in range(YT):
            far[side, 1, 8 * yt : 8 * yt + 8, :] = unpack(x_far[side, LIVE:ROWS, :], yt)
        for half in range(2):
            far[side, half, LIVE:ROWS, :] = jnp.zeros((ROWS - LIVE, LANES), F32)
    total = jnp.zeros((8, LANES), F32)
    for side in range(2):
        result = contract([far[side, 0], far[side, 1]])
        for half in range(2):
            values = result[:, LANES * half : LANES * (half + 1)]
            far[side, half] = values[:ROWS]
            for to in range(2):
                far_y[to, half, 4 * side : 4 * side + 4, :] = values[ROWS + 4 * to : ROWS + 4 * to + 4]
        for yt in range(YT):
            j = side * YT + yt
            total = jnp.where(copy_of == j, result[8 * yt : 8 * yt + 8, LANES:], total)
    far_z[...] = total
    far_z_copies = [send(far_z, far_z_in.at[k - 1], fz_sem, k - 1, at_yz(0, k)) for k in range(1, n_gz)]
    far_y_copies = {}
    for ky in range(1, n_gy):
        for kz in range(n_gz):
            index = (ky - 1) * n_gz + kz
            far_y_copies[ky, kz] = send(
                far_y.at[way(py, ky, n_gy)], far_y_in.at[index], fy_sem, index, at_yz(ky, kz)
            )

    def channel_weights(k):
        (left, next_left), (right, next_right) = mix(pz, n_gz, NZ, length_z, k)
        return jnp.where(
            first_kinds,
            jnp.where(is_moment, left, next_left),
            jnp.where(channel >= 3, jnp.where(is_moment, right, next_right), 0.0),
        )

    from_z = [[jnp.zeros((8, LANES), F32) for _ in range(PAIRS)] for _ in range(2)]
    for k in range(1, n_gz):
        z_copies[k - 1].wait_recv()
        weights = [jnp.where(is_moment, moment, fix) for moment, fix in mix(pz, n_gz, NZ, length_z, k)]
        for pair in range(PAIRS):
            got = z_in[k - 1, pair]
            for side in range(2):
                from_z[side][pair] = from_z[side][pair] + weights[side] * got
    for pair in range(PAIRS):
        one, two = from_z[0][pair], from_z[1][pair]
        z_mixed[2 * pair] = jnp.where(first_kinds, one, pltpu.roll(two, 3, 1))
        z_mixed[2 * pair + 1] = jnp.where(first_kinds, pltpu.roll(one, LANES - 3, 1), two)
    beside = [jnp.zeros((8, LANES), F32) for _ in range(2)]
    both = [jnp.zeros((8, LANES), F32) for _ in range(2)]
    lines = [[jnp.zeros((8, LANES), F32) for _ in range(XROWS // 8)] for _ in range(2)]
    for ky in range(1, n_gy):
        y_copies[ky - 1].wait_recv()
        weights = mix(py, n_gy, NY, length_y, ky)
        for side in range(2):
            moment, fix = weights[side]
            for tile in range(XROWS // 8):
                lines[side][tile] = lines[side][tile] + moment * y_in[ky - 1, 8 * tile : 8 * tile + 8, :]
            beside[side] = beside[side] + jnp.where(lane < 40, moment, fix) * y_in[ky - 1, SIDE : SIDE + 8, :]
        for kz in range(1, n_gz):
            d_copies[ky, kz].wait_recv()
            got = channel_weights(kz) * diagonal_in[(ky - 1) * (n_gz - 1) + kz - 1]
            for side in range(2):
                moment, fix = weights[side]
                both[side] = both[side] + jnp.where(copy_of < 5, moment, fix) * got
    if n_gy > 1:
        pl.when(py > 0)(y_right.wait_recv)
        pl.when(py + 1 < n_gy)(y_left.wait_recv)
    for side, valid in enumerate((py > 0, py + 1 < n_gy)):
        for tile in range(XROWS // 8):
            y_mixed[side, 0, 0, 8 * tile : 8 * tile + 8, :] = lines[side][tile]
        for kind in range(1, 3):
            start = XROWS * (kind - 1)
            y_mixed[side, kind, 0] = jnp.where(valid, y_fix_in[side, start : start + XROWS, :], 0.0)
        for j in range(15):
            kind, xt = divmod(j, 5)
            moved = pltpu.roll(beside[side], LANES - 8 * j, 1) if j else beside[side]
            y_mixed[side, kind, 1, 8 * xt : 8 * xt + 8, :] = jnp.where(
                lane < SPARE, moved, jnp.where(copy_of == j, both[side], 0.0)
            )

    def expand(x, carry):
        for half in range(2):
            line = [
                [y_mixed[side, kind, half, pl.ds(x, 1), :] for kind in range(3)] for side in range(2)
            ]
            for yt in range(YT):
                rows = slice(8 * yt, 8 * yt + 8)
                value = smooth[x, half, rows, :]
                if half == 1:
                    j = x * YT + yt
                    stack = j // COPIES
                    value = jnp.where(
                        lane < SPARE, value, jnp.where(copy_of == j - stack * COPIES, z_mixed[stack], 0.0)
                    )
                for side in range(2):
                    value = value + pick_y[side, rows, :] * line[side][0]
                if yt == 0:
                    value = value + jnp.where(sub == 4, line[0][1], jnp.where(sub == 5, line[0][2], 0.0))
                if yt == YT - 1:
                    value = value + jnp.where(sub == 6, line[1][1], jnp.where(sub == 5, line[1][2], 0.0))
                smooth[x, half, rows, :] = value
        return carry

    lax.fori_loop(0, WX, expand, 0, unroll=5)
    for copy in copies_in[1:]:
        copy.wait()

    def tile_spot(t):
        at = pl.ds(pl.multiple_of(t * LANES, LANES), LANES)
        return at, spot[0, t], spot[1, t], spot[2, t]

    def gather(rows, weights, at, z0):
        total = None
        for e in range(4):
            pick = [pick_z[half, pl.ds(z0 + e, 1), :] for half in range(2)]
            inner = None
            for cells, weight in zip(rows, weights):
                taps = jnp.sum(cells[0] * pick[0] + cells[1] * pick[1], axis=1, keepdims=True)
                inner = weight * taps if inner is None else inner + weight * taps
            inner = inner * w[8 + e : 9 + e, at]
            total = inner if e == 0 else total + inner
        return jnp.sum(total, axis=0, keepdims=True)

    def near(t, carry):
        at, x0, y0, z0 = tile_spot(t)
        first, second, _ = tile_weights(w[0:8, at], low)
        rows = [
            [
                jnp.where(
                    low, smooth[x0 + a, half, pl.ds(y0, 8), :], smooth[x0 + a + 1, half, pl.ds(y0 - 4, 8), :]
                )
                for half in range(2)
            ]
            for a in (0, 2)
        ]
        sampled[pl.ds(t, 1), :] = gather(rows, (first, second), at, z0)
        return carry

    lax.fori_loop(0, TILES, near, 0, unroll=16)

    from_z = jnp.zeros((8, LANES), F32)
    for k in range(1, n_gz):
        far_z_copies[k - 1].wait_recv()
        from_z = from_z + channel_weights(k) * far_z_in[k - 1]
    lines = [[jnp.zeros((8, LANES), F32) for _ in range(2)] for _ in range(2)]
    for ky in range(1, n_gy):
        weights = mix(py, n_gy, NY, length_y, ky)
        weights = [jnp.where((sub == 0) | (sub == 4), moment, fix) for moment, fix in weights]
        for kz in range(n_gz):
            far_y_copies[ky, kz].wait_recv()
            index = (ky - 1) * n_gz + kz
            got = [far_y_in[index, half] for half in range(2)]
            if kz == 0:
                got[1] = jnp.where(lane < SPARE, got[1], 0.0)
            else:
                got = [None, jnp.where(copy_of == 0, channel_weights(kz) * got[1], 0.0)]
            for side in range(2):
                for half in range(2):
                    if got[half] is not None:
                        lines[side][half] = lines[side][half] + weights[side] * got[half]
    for x in range(2):
        for half in range(2):
            line = [[lines[side][half][4 * x + kind : 4 * x + kind + 1] for kind in range(3)] for side in range(2)]
            for yt in range(YT):
                rows = slice(8 * yt, 8 * yt + 8)
                value = far[x, half, rows, :]
                if half == 1:
                    value = jnp.where(lane < SPARE, value, jnp.where(copy_of == x * YT + yt, from_z, 0.0))
                for side in range(2):
                    value = value + pick_y[side, rows, :] * line[side][0]
                if yt == 0:
                    value = value + jnp.where(sub == 4, line[0][1], jnp.where(sub == 5, line[0][2], 0.0))
                if yt == YT - 1:
                    value = value + jnp.where(sub == 6, line[1][1], jnp.where(sub == 5, line[1][2], 0.0))
                far[x, half, rows, :] = value

    def distant(t, carry):
        at, x0, y0, z0 = tile_spot(t)
        w8 = w[0:8, at]
        _, _, along_y = tile_weights(w8, low)
        along_x = []
        for side in range(2):
            total = None
            for a in range(4):
                term = w8[a : a + 1] * pick_x[side, pl.ds(x0 + a, 1), :]
                total = term if a == 0 else total + term
            along_x.append(total)
        weight = jnp.where(low, along_x[0], along_x[1]) * along_y
        rows = [jnp.where(low, far[0, half, pl.ds(y0, 8), :], far[1, half, pl.ds(y0 - 4, 8), :]) for half in range(2)]
        sampled[pl.ds(t, 1), :] += gather([rows], [weight], at, z0)
        return carry

    lax.fori_loop(0, TILES, distant, 0, unroll=16)

    value = live[...] * (sampled[...] + noise[...] * live_dir[...])
    image[...] = value
    pairs = (
        (live_res[...], live_res[...]),
        (live_dir[...], value),
        (live_res[...], value),
        (value, value),
    )
    place = iota((1, LANES), 1)
    total = jnp.zeros((1, LANES), F32)
    for i, (a, b) in enumerate(pairs):
        part = jnp.sum(jnp.sum(a * b, axis=0, keepdims=True), axis=1, keepdims=True)
        total = jnp.where(place == i, part, total)
    sum_out[...] = total
    copies = [send(sum_out, sum_in_x.at[k - 1], sx_sem, k - 1, at_x(k)) for k in range(1, n_gx)]
    for k in range(1, n_gx):
        copies[k - 1].wait_recv()
        total = total + sum_in_x[k - 1]
    sum_mid[...] = total
    copies = [send(sum_mid, sum_in_yz.at[k - 1], syz_sem, k - 1, around_yz(k)) for k in range(1, n_yz)]
    for k in range(1, n_yz):
        copies[k - 1].wait_recv()
        total = total + sum_in_yz[k - 1]
    sums[...] = total
    for wait in sent:
        wait()

    @pl.when(px < OWNERS)
    def _():
        for q in range(n_gx):
            pl.when(px != q)(back(q).wait_send)


def update_kernel(sums, iterate, live, live_dir, live_res, image, new_iterate, new_residual, new_direction):
    place = iota((1, LANES), 1)

    def total(which):
        return jnp.sum(jnp.where(place == which, sums[...], 0.0), axis=1, keepdims=True)

    norm_old, curvature, cross, square = total(0), total(1), total(2), total(3)
    step = norm_old / curvature
    norm_new = norm_old + step * (step * square - 2.0 * cross)
    held = live_res[...] - step * image[...]
    new_iterate[...] = live[...] * iterate[...] + step * live_dir[...]
    new_residual[...] = held
    new_direction[...] = held + norm_new / norm_old * live_dir[...]


def body(sizes, iterate, residual, direction, noise, stencil_base, interp_weights, tile_counts, reach):
    n_gx, n_gy, n_gz = sizes
    n_yz = n_gy * n_gz
    square = (TILES, LANES)
    in_vmem = pl.BlockSpec(memory_space=pltpu.VMEM)
    in_hbm = pl.BlockSpec(memory_space=pltpu.HBM)
    dma = pltpu.SemaphoreType.DMA

    def away(x):
        return pltpu.with_memory_space_constraint(x, pltpu.HBM)

    def keep(x):
        return pltpu.with_memory_space_constraint(x, pltpu.VMEM)

    grid, live_dir, live_res, live, lengths = pl.pallas_call(
        spread_kernel,
        out_shape=[pltpu.VMEM((WX, 2, ROWS, LANES), F32)] + [pltpu.VMEM(square, F32)] * 3 + [pltpu.VMEM((8, LANES), F32)],
        in_specs=[in_hbm] * 6,
        out_specs=[in_vmem] * 5,
        scratch_shapes=[
            pltpu.VMEM((2, 136, LANES), F32),
            pltpu.SMEM((TILES,), jnp.int32),
            pltpu.SMEM((3, TILES), jnp.int32),
            pltpu.SMEM((3,), F32),
            pltpu.VMEM((12, TILES * LANES), F32),
            pltpu.VMEM(square, F32),
            pltpu.VMEM(square, F32),
            dma((6,)),
        ],
        compiler_params=pltpu.CompilerParams(vmem_limit_bytes=16 << 20),
        name="spread",
    )(
        away(tile_counts),
        away(stencil_base),
        away(reach),
        away(interp_weights),
        away(direction.reshape(square)),
        away(residual.reshape(square)),
    )

    image, sums, kept = pl.pallas_call(
        functools.partial(solve_kernel, sizes),
        out_shape=[pltpu.VMEM(square, F32), pltpu.VMEM((1, LANES), F32), pltpu.VMEM(square, F32)],
        in_specs=[in_hbm] * 4 + [in_vmem] * 5,
        out_specs=[in_vmem] * 3,
        scratch_shapes=[
            pltpu.SMEM((3, TILES), jnp.int32),
            pltpu.SMEM((3, TILES), jnp.int32),
            pltpu.VMEM(square, F32),
            pltpu.VMEM((12, TILES * LANES), F32),
            pltpu.VMEM((WX, 2, ROWS, LANES), F32),
            pltpu.VMEM((96, 3 * ROWS), BF16),
            pltpu.VMEM((2, 136, LANES), F32),
            pltpu.VMEM((2, XROWS, LANES), F32),
            pltpu.VMEM((2, ROWS, LANES), F32),
            pltpu.VMEM((6, LIVE, LANES), F32),
            pltpu.VMEM((6, ROWS, LANES), F32),
            pltpu.VMEM((n_gx, 2, 8, LANES), F32),
            pltpu.VMEM((n_gx, 2, 8, LANES), F32),
            pltpu.VMEM((2, ROWS, LANES), F32),
            pltpu.VMEM((2, 2, ROWS, LANES), F32),
            pltpu.VMEM((2, YMSG, LANES), F32),
            pltpu.VMEM((2, 3, XROWS, LANES), F32),
            pltpu.VMEM((2, 8, LANES), F32),
            pltpu.VMEM((2, PAIRS, 8, LANES), F32),
            pltpu.VMEM((3, PAIRS, 8, LANES), F32),
            pltpu.VMEM((3, FIX, LANES), F32),
            pltpu.VMEM((2, 2 * XROWS, LANES), F32),
            pltpu.VMEM((9, 8, LANES), F32),
            pltpu.VMEM((STACKS, 8, LANES), F32),
            pltpu.VMEM((2, 3, 2, XROWS, LANES), F32),
            pltpu.VMEM((2, 2, ROWS, LANES), F32),
            pltpu.VMEM((8, LANES), F32),
            pltpu.VMEM((2, 2, 8, LANES), F32),
            pltpu.VMEM((3, 8, LANES), F32),
            pltpu.VMEM((12, 2, 8, LANES), F32),
            pltpu.VMEM(square, F32),
            pltpu.VMEM((1, LANES), F32),
            pltpu.VMEM((15, 1, LANES), F32),
            pltpu.VMEM((1, LANES), F32),
            pltpu.VMEM((15, 1, LANES), F32),
            dma((4,)),
            dma((2, n_gx)),
            dma((2, n_gx)),
            dma((2, 2)),
            dma((2, 3)),
            dma((2, 3)),
            dma((2, 2)),
            dma((2, 9)),
            dma((2, 3)),
            dma((2, 12)),
            dma((2, 15)),
            dma((2, 15)),
        ],
        compiler_params=pltpu.CompilerParams(
            collective_id=0, has_side_effects=True, vmem_limit_bytes=24 << 20
        ),
        name="solve",
    )(
        away(stencil_base),
        away(iterate.reshape(square)),
        away(noise.reshape(square)),
        away(interp_weights),
        keep(lengths),
        keep(grid),
        keep(live_dir),
        keep(live_res),
        keep(live),
    )

    outs = pl.pallas_call(
        update_kernel,
        out_shape=[jax.ShapeDtypeStruct(square, F32)] * 3,
        in_specs=[in_vmem] * 6,
        out_specs=[in_vmem] * 3,
        name="update",
    )(keep(sums), keep(kept), keep(live), keep(live_dir), keep(live_res), keep(image))
    return tuple(out.reshape(-1) for out in outs)


def solution(mesh):
    sizes = tuple(mesh.shape[axis] for axis in ("gx", "gy", "gz"))
    lines = P(("gx", "gy", "gz"))
    return jax.shard_map(
        functools.partial(body, sizes),
        mesh=mesh,
        in_specs=(lines, lines, lines, lines, P(None, ("gx", "gy", "gz")), P(None, ("gx", "gy", "gz")), lines, P()),
        out_specs=(lines, lines, lines),
        check_vma=False,
    )
```

```python
import functools

import jax
import jax.numpy as jnp
from jax import lax
from jax.experimental import pallas as pl
from jax.experimental.pallas import tpu as pltpu
from jax.sharding import PartitionSpec as P

F32 = jnp.float32
BF16 = jnp.bfloat16
LANES = 128
TILES = 128
NX, NY, NZ = 32, 64, 128
WX = NX + 3
TOP = 4
ROWS = 80
LIVE = 72
YT = LIVE // 8
OWN, SPARE, CHANNELS, COPIES = 5, 8, 6, 20
STACKS = -(-WX * YT // COPIES)
PAIRS = STACKS // 2
XROWS = 40
SIDE, FIX = XROWS, XROWS + 8
SPLIT = 24
PACK = SPARE + CHANNELS - OWN
OWNERS = ROWS // 8
MESH = pl.DeviceIdType.MESH


def iota(shape, dim):
    return lax.broadcasted_iota(jnp.int32, shape, dim)


def full(value):
    return jnp.full((1, LANES), value, F32)


def decay(distance, length):
    return jnp.exp(-distance.astype(F32) / length)


def outgoing(kind, source, size, length):
    one = decay(full(1), length) - jnp.exp(full(1.0) / length)
    two = decay(full(2), length) - jnp.exp(full(2.0) / length)
    one, two = one[:, :1], two[:, :1]
    zero = jnp.zeros(source.shape, F32)
    if kind == 0:
        return decay(size + 1 - source, length)
    if kind == 1:
        return jnp.where(source == size, one, jnp.where(source == size + 1, two, zero))
    if kind == 2:
        return jnp.where(source == size + 1, one, zero)
    if kind == 3:
        return decay(source + 1, length)
    if kind == 4:
        return jnp.where(source == -1, two, jnp.where(source == 0, one, zero))
    return jnp.where(source == -1, one, zero)


def incoming(kind, cell, size, length):
    if kind == 0:
        return decay(cell - 1, length)
    if kind == 3:
        return decay(size - 1 - cell, length)
    target = {1: -1, 2: 0, 4: size + 1, 5: size}[kind]
    return jnp.where(cell == target, 1.0, 0.0).astype(F32)


def lane_roles(lane):
    spare = lane >= SPARE
    place = jnp.maximum(lane - SPARE, 0)
    copy = place // CHANNELS
    return jnp.where(spare, place - copy * CHANNELS, -1), jnp.where(spare, copy, -1)


def line_row(x):
    return (x + XROWS - 8) % XROWS


def pair_place(pair):
    return {0: PAIRS - 2, PAIRS - 1: PAIRS - 1}.get(pair, pair - 1)


def tile_weights(w8, low):
    along_y = jnp.where(low, pltpu.roll(w8, 4, 0), w8)
    first = jnp.where(low, w8[0:1], w8[1:2]) * along_y
    second = jnp.where(low, w8[2:3], w8[3:4]) * along_y
    return first, second, along_y


def fetch(pairs, sem):
    copies = [pltpu.make_async_copy(src, dst, sem.at[i]) for i, (src, dst) in enumerate(pairs)]
    for copy in copies:
        copy.start()
    return copies


def spread_kernel(
    count_hbm,
    base_hbm,
    reach_hbm,
    w_hbm,
    direction_hbm,
    residual_hbm,
    grid,
    live_dir,
    live_res,
    live,
    lengths,
    table,
    count,
    base,
    reach,
    w,
    direction,
    residual,
    sem,
):
    copies = fetch(
        (
            (reach_hbm, reach),
            (w_hbm, w),
            (count_hbm, count),
            (base_hbm, base),
            (direction_hbm, direction),
            (residual_hbm, residual),
        ),
        sem,
    )

    def clear(x, carry):
        for half in range(2):
            grid[x, half] = jnp.zeros((ROWS, LANES), F32)
        return carry

    lax.fori_loop(0, WX, clear, 0)
    copies[0].wait()
    anchor_x = lax.axis_index("gx") * NX
    anchor_y = lax.axis_index("gy") * NY
    anchor_z = lax.axis_index("gz") * NZ
    length = reach[2] * float(NZ)
    scale = 1.0 / (
        jnp.sqrt(full(reach[0] * float(NX))) * jnp.sqrt(full(reach[1] * float(NY))) * jnp.sqrt(full(length))
    )
    source = iota((136, LANES), 0) - 1
    lane = iota((136, LANES), 1)
    for i, size in enumerate((NX, NY, NZ)):
        lengths[i : i + 1, :] = full(reach[i] * float(size))
    table[0] = decay(jnp.abs(lane - 1 - source), length) * scale
    own = (lane >= OWN) & (lane < SPARE)
    second = jnp.where(own, decay(jnp.abs(lane - OWN + NZ - 1 - source), length), 0.0)
    channel, _ = lane_roles(lane)
    for kind in range(CHANNELS):
        second = jnp.where(channel == kind, outgoing(kind, source, NZ, length), second)
    table[1] = second * scale
    for copy in copies[1:]:
        copy.wait()
    low = iota((8, LANES), 0) < 4
    slot = iota((1, LANES), 1)

    def tile(t, carry):
        at = pl.ds(pl.multiple_of(t * LANES, LANES), LANES)
        w8 = w[0:8, at]
        mask = slot < count[t]
        values = jnp.where(mask, direction[pl.ds(t, 1), :], 0.0)
        live_dir[pl.ds(t, 1), :] = values
        live_res[pl.ds(t, 1), :] = jnp.where(mask, residual[pl.ds(t, 1), :], 0.0)
        live[pl.ds(t, 1), :] = jnp.where(mask, 1.0, 0.0)
        first, second, _ = tile_weights(w8, low)
        x0 = base[0, t] - anchor_x + 1
        y0 = base[1, t] - anchor_y + 1 + TOP
        z0 = base[2, t] - anchor_z + 1
        parts = [[None, None], [None, None]]
        for e in range(4):
            along_z = w[8 + e : 9 + e, at] * values
            row = [table[half, pl.ds(z0 + e, 1), :] for half in range(2)]
            for pair, product in enumerate((first, second)):
                taps = jnp.sum(product * along_z, axis=1, keepdims=True)
                for half in range(2):
                    term = taps * row[half]
                    parts[pair][half] = term if e == 0 else parts[pair][half] + term
        for a in range(4):
            start = y0 if a % 2 == 0 else y0 - 4
            keep = low if a % 2 == 0 else jnp.logical_not(low)
            for half in range(2):
                spot = (x0 + a, half, pl.ds(start, 8), slice(None))
                grid[spot] = grid[spot] + jnp.where(keep, parts[a // 2][half], 0.0)
        return carry

    lax.fori_loop(0, TILES, tile, 0, unroll=32)


def solve_kernel(
    sizes,
    base_hbm,
    iterate_hbm,
    noise_hbm,
    w_hbm,
    lengths,
    grid,
    live_dir,
    live_res,
    live,
    image,
    sums,
    iterate,
    base,
    spot,
    noise,
    w,
    smooth,
    basis,
    pick_z,
    pick_x,
    pick_y,
    x_side,
    x_out,
    x_in,
    x_prefix,
    x_far,
    x_fix_in,
    y_msg,
    y_fix,
    y_side,
    diagonal,
    z_out,
    z_in,
    y_in,
    y_fix_in,
    diagonal_in,
    z_mixed,
    y_mixed,
    far,
    far_z,
    far_y,
    far_z_in,
    far_y_in,
    near_weight,
    far_weight,
    sampled,
    sum_out,
    sum_in_x,
    sum_mid,
    sum_in_yz,
    in_sem,
    x_sem,
    x_back_sem,
    x_fix_sem,
    z_sem,
    y_sem,
    y_fix_sem,
    d_sem,
    fz_sem,
    fy_sem,
    sx_sem,
    syz_sem,
):
    n_gx, n_gy, n_gz = sizes
    n_yz = n_gy * n_gz
    px, py, pz = lax.axis_index("gx"), lax.axis_index("gy"), lax.axis_index("gz")
    pyz = py * n_gz + pz

    def at_x(k):
        return {"gx": lax.rem(px + k, n_gx)}

    def at_yz(ky, kz):
        return {"gy": lax.rem(py + ky, n_gy), "gz": lax.rem(pz + kz, n_gz)}

    def around_yz(k):
        other = lax.rem(pyz + k, n_yz)
        return {"gy": other // n_gz, "gz": lax.rem(other, n_gz)}

    barrier = pltpu.get_barrier_semaphore()
    for k in range(1, n_gx):
        pl.semaphore_signal(barrier, inc=1, device_id=at_x(k), device_id_type=MESH)
    for k in range(1, n_yz):
        pl.semaphore_signal(barrier, inc=1, device_id=around_yz(k), device_id_type=MESH)
    copies_in = fetch(((base_hbm, base), (noise_hbm, noise), (w_hbm, w), (iterate_hbm, iterate)), in_sem)
    length_x, length_y, length_z = (lengths[i : i + 1, 0:1] for i in range(3))
    sent = []

    def chunk(c):
        return pl.ds(pl.multiple_of(c * 8, 8), 8)

    def send(src, dst, sems, index, device, when=None, slot=None):
        copy = pltpu.make_async_remote_copy(
            src_ref=src,
            dst_ref=dst,
            send_sem=sems.at[0, index],
            recv_sem=sems.at[1, index if slot is None else slot],
            device_id=device,
            device_id_type=MESH,
        )
        if when is None:
            copy.start()
            sent.append(copy.wait_send)
        else:
            pl.when(when)(copy.start)
            sent.append(lambda: pl.when(when)(copy.wait_send))
        return copy

    def way(pos, k, count):
        return jnp.where(pos + k < count, 0, 1)

    def mix(pos, count, size, length, k):
        from_left = pos >= k
        left = jnp.where(from_left, jnp.exp(full(-float(size * (k - 1))) / length), 0.0)
        right = jnp.where(from_left, 0.0, jnp.exp(full(-float(size * (count - k - 1))) / length))
        next_left = jnp.where(from_left, full(1.0), 0.0) if k == 1 else full(0.0)
        next_right = jnp.where(from_left, 0.0, full(1.0)) if count - k == 1 else full(0.0)
        return (left, next_left), (right, next_right)

    sub = iota((8, LANES), 0)
    lane = iota((8, LANES), 1)
    low = sub < 4
    channel, copy_of = lane_roles(lane)
    first_kinds = (channel >= 0) & (channel < 3)
    is_moment = (channel == 0) | (channel == 3)

    step_x = jnp.exp(full(-1.0) / length_x)
    fix_one = step_x - jnp.exp(full(1.0) / length_x)
    fix_two = jnp.exp(full(-2.0) / length_x) - jnp.exp(full(2.0) / length_x)

    def moments(yt, carry):
        rows = pl.ds(pl.multiple_of(yt * 8, 8), 8)
        for half, out in enumerate((x_out, x_side)):
            edge = [grid[x, half, rows, :] for x in (0, 1, WX - 2, WX - 1)]
            up, down = edge[0], edge[3]
            for x in range(1, WX):
                up = grid[x, half, rows, :] + step_x * up
                down = grid[WX - 1 - x, half, rows, :] + step_x * down
            out[0, rows, :] = up
            out[1, rows, :] = down
            out[2, rows, :] = edge[2] * fix_one + edge[3] * fix_two
            out[3, rows, :] = edge[3] * fix_one
            out[4, rows, :] = edge[0] * fix_two + edge[1] * fix_one
            out[5, rows, :] = edge[0] * fix_one
        return carry

    lax.fori_loop(0, YT, moments, 0, unroll=3)
    for plane in range(6):
        total = jnp.zeros((8, LANES), F32)
        for yt in range(YT):
            moved = pltpu.roll(x_side[plane, 8 * yt : 8 * yt + 8, :], (PACK * yt - OWN) % LANES, 1)
            total = jnp.where((lane >= PACK * yt) & (lane < PACK * (yt + 1)), moved, total)
        x_out[plane, LIVE:ROWS, :] = total

    def unpack(packed, yt):
        place = PACK * yt + jnp.where(lane < SPARE, jnp.maximum(lane - OWN, 0), channel + SPARE - OWN)
        return jnp.where(lane < OWN, 0.0, jnp.take_along_axis(packed, place, axis=1))

    pl.semaphore_wait(barrier, n_gx - 1 + n_yz - 1)
    x_right = send(x_out.at[pl.ds(2, 2)], x_fix_in.at[0], x_fix_sem, 0, at_x(1), px + 1 < n_gx)
    x_left = send(x_out.at[pl.ds(4, 2)], x_fix_in.at[1], x_fix_sem, 1, at_x(n_gx - 1), px > 0)
    for c in range(OWNERS):
        send(x_out.at[pl.ds(0, 2), chunk(c), :], x_in.at[px], x_sem, c, {"gx": c}, px != c, px)

    def scan(yt, carry):
        rows = pl.ds(pl.multiple_of(yt * 8, 8), 8)
        for half in range(2):
            state = grid[0, half, rows, :]
            smooth[0, half, rows, :] = state
            for x in range(1, WX):
                state = grid[x, half, rows, :] + step_x * state
                smooth[x, half, rows, :] = state
            state = step_x * grid[WX - 1, half, rows, :]
            for x in reversed(range(WX - 1)):
                smooth[x, half, rows, :] = smooth[x, half, rows, :] + state
                if x > 0:
                    state = step_x * (state + grid[x, half, rows, :])
        return carry

    lax.fori_loop(0, YT, scan, 0, unroll=3)
    for x in range(WX):
        for half in range(2):
            smooth[x, half, LIVE:ROWS, :] = jnp.zeros((ROWS - LIVE, LANES), F32)

    row = iota((96, 3 * ROWS), 0)
    col = iota((96, 3 * ROWS), 1)
    part = col // ROWS
    source = col - part * ROWS - TOP - 1
    cell = row - TOP - 1
    entry = jnp.where((cell >= -1) & (cell <= NY + 1), decay(jnp.abs(cell - source), length_y), 0.0)
    for kind in range(CHANNELS):
        entry = jnp.where(row == ROWS + kind + kind // 3, outgoing(kind, source, NY, length_y), entry)
    entry = jnp.where((source >= -1) & (source <= NY + 1), entry, 0.0)
    entry_high = entry.astype(BF16).astype(F32)
    basis[...] = jnp.where(part == 1, entry - entry_high, entry_high).astype(BF16)

    def contract(planes):
        values = jnp.concatenate(planes, axis=1)
        high = values.astype(BF16)
        rest = (values - high.astype(F32)).astype(BF16)
        stacked = jnp.concatenate([high, high, rest], axis=0)
        return jnp.dot(basis[...], stacked, preferred_element_type=F32)

    def back(q):
        return pltpu.make_async_remote_copy(
            src_ref=x_prefix.at[q],
            dst_ref=x_far.at[:, chunk(px), :],
            send_sem=x_back_sem.at[0, q],
            recv_sem=x_back_sem.at[1, px],
            device_id={"gx": q},
            device_id_type=MESH,
        )

    def contract_own(x):
        result = contract([smooth[x, 0], smooth[x, 1]])
        for half in range(2):
            smooth[x, half] = result[:ROWS, LANES * half : LANES * (half + 1)]
        for side in range(2):
            for kind in range(3):
                line = result[ROWS + 4 * side + kind : ROWS + 4 * side + kind + 1]
                at = pl.ds(line_row(x), 1)
                if kind == 0:
                    y_msg[side, at, :] = line[:, :LANES]
                else:
                    y_fix[side, kind - 1, at, :] = line[:, :LANES]
                y_side[side, kind, at, :] = line[:, LANES:]

    def contract_step(x, carry):
        contract_own(x)
        return carry

    lax.fori_loop(2, WX - 3, contract_step, 0, unroll=5)

    contract_own(WX - 3)
    stacks = [jnp.zeros((8, LANES), F32) for _ in range(STACKS)]

    def stacked_planes(planes):
        for x in planes:
            for yt in range(YT):
                stack, copy = divmod(x * YT + yt, COPIES)
                stacks[stack] = jnp.where(copy_of == copy, smooth[x, 1, 8 * yt : 8 * yt + 8, :], stacks[stack])

    def pair_up(pair):
        one, two = stacks[2 * pair], stacks[2 * pair + 1]
        z_out[0, pair_place(pair)] = jnp.where(first_kinds, one, pltpu.roll(two, 3, 1))
        z_out[1, pair_place(pair)] = jnp.where(first_kinds, pltpu.roll(one, LANES - 3, 1), two)

    early, late = pl.ds(0, PAIRS - 2), pl.ds(PAIRS - 2, 2)
    full_rows, rest_rows, rest_fix = pl.ds(0, SPLIT), pl.ds(SPLIT, FIX - SPLIT), pl.ds(SPLIT, XROWS - SPLIT)
    stacked_planes(range(2, WX - 2))
    for pair in range(1, PAIRS - 1):
        pair_up(pair)
    z_copies = [
        send(z_out.at[way(pz, k, n_gz), early], z_in.at[k - 1, early], z_sem, k - 1, at_yz(0, k))
        for k in range(1, n_gz)
    ]

    y_copies = [
        send(y_msg.at[way(py, k, n_gy), full_rows], y_in.at[k - 1, full_rows], y_sem, k - 1, at_yz(k, 0))
        for k in range(1, n_gy)
    ]
    y_fixes = []

    def send_fixes(rows, index):
        if n_gy > 1:
            right = send(
                y_fix.at[0, :, rows], y_fix_in.at[0, :, rows], y_fix_sem, index, at_yz(1, 0), py + 1 < n_gy
            )
            left = send(
                y_fix.at[1, :, rows], y_fix_in.at[1, :, rows], y_fix_sem, index + 1, at_yz(n_gy - 1, 0), py > 0
            )
            y_fixes.append((right, left))

    send_fixes(full_rows, 0)

    def received(dst, sems, slot):
        pltpu.make_async_remote_copy(
            src_ref=dst,
            dst_ref=dst,
            send_sem=sems.at[0, slot],
            recv_sem=sems.at[1, slot],
            device_id={"gx": slot},
            device_id_type=MESH,
        ).wait_recv()

    ratio = jnp.exp(full(-float(NX)) / length_x)

    @pl.when(px < OWNERS)
    def _():
        x_in[px] = x_out[0:2, chunk(px), :]
        for p in range(n_gx):
            pl.when(px != p)(lambda: received(x_in.at[p], x_sem, p))
        for side, order in enumerate((range(n_gx), reversed(range(n_gx)))):
            total = jnp.zeros((8, LANES), F32)
            for q in order:
                x_prefix[q, side] = total
                total = total * ratio + x_in[q, side]
        x_far[:, chunk(px), :] = x_prefix[px]
        for q in range(n_gx):
            pl.when(px != q)(back(q).start)

    if n_gx > 1:
        pl.when(px > 0)(x_right.wait_recv)
        pl.when(px + 1 < n_gx)(x_left.wait_recv)
    for side, valid, places in ((0, px > 0, (0, 1)), (1, px + 1 < n_gx, (WX - 1, WX - 2))):
        for kind, x in enumerate(places):
            smooth[x, 0, 0:LIVE, :] += jnp.where(valid, x_fix_in[side, kind, 0:LIVE, :], 0.0)
            packed = jnp.where(valid, x_fix_in[side, kind, LIVE:ROWS, :], 0.0)
            for yt in range(YT):
                smooth[x, 1, 8 * yt : 8 * yt + 8, :] += unpack(packed, yt)
    for x in (0, 1, WX - 2, WX - 1):
        contract_own(x)

    stacked_planes((0, 1, WX - 2, WX - 1))
    pair_up(0)
    pair_up(PAIRS - 1)
    for side in range(2):
        beside = jnp.zeros((8, LANES), F32)
        both = jnp.zeros((8, LANES), F32)
        for j in range(15):
            kind, xt = divmod(j, 5)
            value = y_side[side, kind, 8 * xt : 8 * xt + 8, :]
            moved = pltpu.roll(value, 8 * j, 1) if j else value
            beside = jnp.where((lane >= 8 * j) & (lane < 8 * j + 8), moved, beside)
            both = jnp.where(copy_of == j, value, both)
        y_msg[side, SIDE : SIDE + 8, :] = beside
        diagonal[side] = both
    z_copies += [
        send(z_out.at[way(pz, k, n_gz), late], z_in.at[k - 1, late], z_sem, k + 2, at_yz(0, k))
        for k in range(1, n_gz)
    ]
    y_copies += [
        send(y_msg.at[way(py, k, n_gy), rest_rows], y_in.at[k - 1, rest_rows], y_sem, k + 2, at_yz(k, 0))
        for k in range(1, n_gy)
    ]
    send_fixes(rest_fix, 2)
    d_copies = {}
    for ky in range(1, n_gy):
        for kz in range(1, n_gz):
            index = (ky - 1) * (n_gz - 1) + kz - 1
            d_copies[ky, kz] = send(
                diagonal.at[way(py, ky, n_gy)], diagonal_in.at[index], d_sem, index, at_yz(ky, kz)
            )

    copies_in[0].wait()

    def locate(t, carry):
        spot[0, t] = jnp.clip(base[0, t] - px * NX + 1, 0, NX - 1)
        spot[1, t] = jnp.clip(base[1, t] - py * NY + 1, 0, NY - 1) + TOP
        spot[2, t] = jnp.clip(base[2, t] - pz * NZ + 1, 0, NZ - 1)
        return carry

    lax.fori_loop(0, TILES, locate, 0, unroll=8)

    cell = iota((136, LANES), 0) - 1
    wide = iota((136, LANES), 1)
    pick_z[0] = jnp.where(wide == cell + 1, 1.0, 0.0).astype(F32)
    picked = jnp.where((wide >= OWN) & (wide < SPARE) & (wide - OWN + NZ - 1 == cell), 1.0, 0.0).astype(F32)
    wide_channel, _ = lane_roles(wide)
    for kind in range(CHANNELS):
        picked = jnp.where(wide_channel == kind, incoming(kind, cell, NZ, length_z), picked)
    pick_z[1] = picked
    cell = iota((XROWS, LANES), 0) - 1
    for side in range(2):
        pick_x[side] = incoming(3 * side, cell, NX, length_x)
    cell = iota((ROWS, LANES), 0) - TOP - 1
    for side in range(2):
        pick_y[side] = incoming(3 * side, cell, NY, length_y)

    for copy in copies_in[1:]:
        copy.wait()

    def weigh(t, carry):
        w8 = w[0:8, pl.ds(pl.multiple_of(t * LANES, LANES), LANES)]
        first, second, along_y = tile_weights(w8, low)
        along_x = []
        for side in range(2):
            total = None
            for a in range(4):
                term = w8[a : a + 1] * pick_x[side, pl.ds(spot[0, t] + a, 1), :]
                total = term if a == 0 else total + term
            along_x.append(total)
        near_weight[t, 0:8, :] = first
        near_weight[t, 8:16, :] = second
        far_weight[t] = jnp.where(low, along_x[0], along_x[1]) * along_y
        return carry

    lax.fori_loop(0, TILES, weigh, 0, unroll=8)

    for c in range(OWNERS):
        pl.when(px != c)(lambda: received(x_far.at[:, chunk(c), :], x_back_sem, c))
    for side in range(2):
        far[side, 0, 0:LIVE, :] = x_far[side, 0:LIVE, :]
        for yt in range(YT):
            far[side, 1, 8 * yt : 8 * yt + 8, :] = unpack(x_far[side, LIVE:ROWS, :], yt)
        for half in range(2):
            far[side, half, LIVE:ROWS, :] = jnp.zeros((ROWS - LIVE, LANES), F32)
    total = jnp.zeros((8, LANES), F32)
    for side in range(2):
        result = contract([far[side, 0], far[side, 1]])
        for half in range(2):
            values = result[:, LANES * half : LANES * (half + 1)]
            far[side, half] = values[:ROWS]
            for to in range(2):
                far_y[to, half, 4 * side : 4 * side + 4, :] = values[ROWS + 4 * to : ROWS + 4 * to + 4]
        for yt in range(YT):
            j = side * YT + yt
            total = jnp.where(copy_of == j, result[8 * yt : 8 * yt + 8, LANES:], total)
    far_z[...] = total
    far_z_copies = [send(far_z, far_z_in.at[k - 1], fz_sem, k - 1, at_yz(0, k)) for k in range(1, n_gz)]
    far_y_copies = {}
    for ky in range(1, n_gy):
        for kz in range(n_gz):
            index = (ky - 1) * n_gz + kz
            far_y_copies[ky, kz] = send(
                far_y.at[way(py, ky, n_gy)], far_y_in.at[index], fy_sem, index, at_yz(ky, kz)
            )

    def channel_weights(k):
        (left, next_left), (right, next_right) = mix(pz, n_gz, NZ, length_z, k)
        return jnp.where(
            first_kinds,
            jnp.where(is_moment, left, next_left),
            jnp.where(channel >= 3, jnp.where(is_moment, right, next_right), 0.0),
        )

    from_z = [[jnp.zeros((8, LANES), F32) for _ in range(PAIRS)] for _ in range(2)]
    for k in range(1, n_gz):
        z_copies[k - 1].wait_recv()
        z_copies[k + n_gz - 2].wait_recv()
        weights = [jnp.where(is_moment, moment, fix) for moment, fix in mix(pz, n_gz, NZ, length_z, k)]
        for pair in range(PAIRS):
            got = z_in[k - 1, pair_place(pair)]
            for side in range(2):
                from_z[side][pair] = from_z[side][pair] + weights[side] * got
    for pair in range(PAIRS):
        one, two = from_z[0][pair], from_z[1][pair]
        z_mixed[2 * pair] = jnp.where(first_kinds, one, pltpu.roll(two, 3, 1))
        z_mixed[2 * pair + 1] = jnp.where(first_kinds, pltpu.roll(one, LANES - 3, 1), two)
    beside = [jnp.zeros((8, LANES), F32) for _ in range(2)]
    both = [jnp.zeros((8, LANES), F32) for _ in range(2)]
    lines = [[jnp.zeros((8, LANES), F32) for _ in range(XROWS // 8)] for _ in range(2)]
    for ky in range(1, n_gy):
        y_copies[ky - 1].wait_recv()
        y_copies[ky + n_gy - 2].wait_recv()
        weights = mix(py, n_gy, NY, length_y, ky)
        for side in range(2):
            moment, fix = weights[side]
            for tile in range(XROWS // 8):
                lines[side][tile] = lines[side][tile] + moment * y_in[ky - 1, 8 * tile : 8 * tile + 8, :]
            beside[side] = beside[side] + jnp.where(lane < 40, moment, fix) * y_in[ky - 1, SIDE : SIDE + 8, :]
        for kz in range(1, n_gz):
            d_copies[ky, kz].wait_recv()
            got = channel_weights(kz) * diagonal_in[(ky - 1) * (n_gz - 1) + kz - 1]
            for side in range(2):
                moment, fix = weights[side]
                both[side] = both[side] + jnp.where(copy_of < 5, moment, fix) * got
    for right, left in y_fixes:
        pl.when(py > 0)(right.wait_recv)
        pl.when(py + 1 < n_gy)(left.wait_recv)
    for side, valid in enumerate((py > 0, py + 1 < n_gy)):
        for tile in range(XROWS // 8):
            y_mixed[side, 0, 0, 8 * tile : 8 * tile + 8, :] = lines[side][tile]
        for kind in range(1, 3):
            y_mixed[side, kind, 0] = jnp.where(valid, y_fix_in[side, kind - 1], 0.0)
        for j in range(15):
            kind, xt = divmod(j, 5)
            moved = pltpu.roll(beside[side], LANES - 8 * j, 1) if j else beside[side]
            y_mixed[side, kind, 1, 8 * xt : 8 * xt + 8, :] = jnp.where(
                lane < SPARE, moved, jnp.where(copy_of == j, both[side], 0.0)
            )

    def expand(x, carry):
        for half in range(2):
            line = [
                [y_mixed[side, kind, half, pl.ds(line_row(x), 1), :] for kind in range(3)] for side in range(2)
            ]
            for yt in range(YT):
                rows = slice(8 * yt, 8 * yt + 8)
                value = smooth[x, half, rows, :]
                if half == 1:
                    j = x * YT + yt
                    stack = j // COPIES
                    value = jnp.where(
                        lane < SPARE, value, jnp.where(copy_of == j - stack * COPIES, z_mixed[stack], 0.0)
                    )
                for side in range(2):
                    value = value + pick_y[side, rows, :] * line[side][0]
                if yt == 0:
                    value = value + jnp.where(sub == 4, line[0][1], jnp.where(sub == 5, line[0][2], 0.0))
                if yt == YT - 1:
                    value = value + jnp.where(sub == 6, line[1][1], jnp.where(sub == 5, line[1][2], 0.0))
                smooth[x, half, rows, :] = value
        return carry

    lax.fori_loop(0, WX, expand, 0, unroll=5)

    def tile_spot(t):
        at = pl.ds(pl.multiple_of(t * LANES, LANES), LANES)
        return at, spot[0, t], spot[1, t], spot[2, t]

    def gather(rows, weights, at, z0):
        total = None
        for e in range(4):
            pick = [pick_z[half, pl.ds(z0 + e, 1), :] for half in range(2)]
            inner = None
            for cells, weight in zip(rows, weights):
                taps = jnp.sum(cells[0] * pick[0] + cells[1] * pick[1], axis=1, keepdims=True)
                inner = weight * taps if inner is None else inner + weight * taps
            inner = inner * w[8 + e : 9 + e, at]
            total = inner if e == 0 else total + inner
        return jnp.sum(total, axis=0, keepdims=True)

    def near(t, carry):
        at, x0, y0, z0 = tile_spot(t)
        rows = [
            [
                jnp.where(
                    low, smooth[x0 + a, half, pl.ds(y0, 8), :], smooth[x0 + a + 1, half, pl.ds(y0 - 4, 8), :]
                )
                for half in range(2)
            ]
            for a in (0, 2)
        ]
        sampled[pl.ds(t, 1), :] = gather(rows, (near_weight[t, 0:8, :], near_weight[t, 8:16, :]), at, z0)
        return carry

    lax.fori_loop(0, TILES, near, 0, unroll=32)

    from_z = jnp.zeros((8, LANES), F32)
    for k in range(1, n_gz):
        far_z_copies[k - 1].wait_recv()
        from_z = from_z + channel_weights(k) * far_z_in[k - 1]
    lines = [[jnp.zeros((8, LANES), F32) for _ in range(2)] for _ in range(2)]
    for ky in range(1, n_gy):
        weights = mix(py, n_gy, NY, length_y, ky)
        weights = [jnp.where((sub == 0) | (sub == 4), moment, fix) for moment, fix in weights]
        for kz in range(n_gz):
            far_y_copies[ky, kz].wait_recv()
            index = (ky - 1) * n_gz + kz
            got = [far_y_in[index, half] for half in range(2)]
            if kz == 0:
                got[1] = jnp.where(lane < SPARE, got[1], 0.0)
            else:
                got = [None, jnp.where(copy_of == 0, channel_weights(kz) * got[1], 0.0)]
            for side in range(2):
                for half in range(2):
                    if got[half] is not None:
                        lines[side][half] = lines[side][half] + weights[side] * got[half]
    for x in range(2):
        for half in range(2):
            line = [[lines[side][half][4 * x + kind : 4 * x + kind + 1] for kind in range(3)] for side in range(2)]
            for yt in range(YT):
                rows = slice(8 * yt, 8 * yt + 8)
                value = far[x, half, rows, :]
                if half == 1:
                    value = jnp.where(lane < SPARE, value, jnp.where(copy_of == x * YT + yt, from_z, 0.0))
                for side in range(2):
                    value = value + pick_y[side, rows, :] * line[side][0]
                if yt == 0:
                    value = value + jnp.where(sub == 4, line[0][1], jnp.where(sub == 5, line[0][2], 0.0))
                if yt == YT - 1:
                    value = value + jnp.where(sub == 6, line[1][1], jnp.where(sub == 5, line[1][2], 0.0))
                far[x, half, rows, :] = value

    def distant(t, carry):
        at, x0, y0, z0 = tile_spot(t)
        rows = [jnp.where(low, far[0, half, pl.ds(y0, 8), :], far[1, half, pl.ds(y0 - 4, 8), :]) for half in range(2)]
        sampled[pl.ds(t, 1), :] += gather([rows], [far_weight[t]], at, z0)
        return carry

    lax.fori_loop(0, TILES, distant, 0, unroll=32)

    value = live[...] * (sampled[...] + noise[...] * live_dir[...])
    image[...] = value
    pairs = (
        (live_res[...], live_res[...]),
        (live_dir[...], value),
        (live_res[...], value),
        (value, value),
    )
    place = iota((1, LANES), 1)
    total = jnp.zeros((1, LANES), F32)
    for i, (a, b) in enumerate(pairs):
        part = jnp.sum(jnp.sum(a * b, axis=0, keepdims=True), axis=1, keepdims=True)
        total = jnp.where(place == i, part, total)
    sum_out[...] = total
    copies = [send(sum_out, sum_in_x.at[k - 1], sx_sem, k - 1, at_x(k)) for k in range(1, n_gx)]
    for k in range(1, n_gx):
        copies[k - 1].wait_recv()
        total = total + sum_in_x[k - 1]
    sum_mid[...] = total
    copies = [send(sum_mid, sum_in_yz.at[k - 1], syz_sem, k - 1, around_yz(k)) for k in range(1, n_yz)]
    for k in range(1, n_yz):
        copies[k - 1].wait_recv()
        total = total + sum_in_yz[k - 1]
    sums[...] = total
    for wait in sent:
        wait()

    @pl.when(px < OWNERS)
    def _():
        for q in range(n_gx):
            pl.when(px != q)(back(q).wait_send)


def update_kernel(sums, iterate, live, live_dir, live_res, image, new_iterate, new_residual, new_direction):
    place = iota((1, LANES), 1)

    def total(which):
        return jnp.sum(jnp.where(place == which, sums[...], 0.0), axis=1, keepdims=True)

    norm_old, curvature, cross, square = total(0), total(1), total(2), total(3)
    step = norm_old / curvature
    norm_new = norm_old + step * (step * square - 2.0 * cross)
    held = live_res[...] - step * image[...]
    new_iterate[...] = live[...] * iterate[...] + step * live_dir[...]
    new_residual[...] = held
    new_direction[...] = held + norm_new / norm_old * live_dir[...]


def body(sizes, iterate, residual, direction, noise, stencil_base, interp_weights, tile_counts, reach):
    n_gx, n_gy, n_gz = sizes
    n_yz = n_gy * n_gz
    square = (TILES, LANES)
    in_vmem = pl.BlockSpec(memory_space=pltpu.VMEM)
    in_hbm = pl.BlockSpec(memory_space=pltpu.HBM)
    dma = pltpu.SemaphoreType.DMA

    def away(x):
        return pltpu.with_memory_space_constraint(x, pltpu.HBM)

    def keep(x):
        return pltpu.with_memory_space_constraint(x, pltpu.VMEM)

    grid, live_dir, live_res, live, lengths = pl.pallas_call(
        spread_kernel,
        out_shape=[pltpu.VMEM((WX, 2, ROWS, LANES), F32)] + [pltpu.VMEM(square, F32)] * 3 + [pltpu.VMEM((8, LANES), F32)],
        in_specs=[in_hbm] * 6,
        out_specs=[in_vmem] * 5,
        scratch_shapes=[
            pltpu.VMEM((2, 136, LANES), F32),
            pltpu.SMEM((TILES,), jnp.int32),
            pltpu.SMEM((3, TILES), jnp.int32),
            pltpu.SMEM((3,), F32),
            pltpu.VMEM((12, TILES * LANES), F32),
            pltpu.VMEM(square, F32),
            pltpu.VMEM(square, F32),
            dma((6,)),
        ],
        compiler_params=pltpu.CompilerParams(vmem_limit_bytes=16 << 20),
        name="spread",
    )(
        away(tile_counts),
        away(stencil_base),
        away(reach),
        away(interp_weights),
        away(direction.reshape(square)),
        away(residual.reshape(square)),
    )

    image, sums, kept = pl.pallas_call(
        functools.partial(solve_kernel, sizes),
        out_shape=[pltpu.VMEM(square, F32), pltpu.VMEM((1, LANES), F32), pltpu.VMEM(square, F32)],
        in_specs=[in_hbm] * 4 + [in_vmem] * 5,
        out_specs=[in_vmem] * 3,
        scratch_shapes=[
            pltpu.SMEM((3, TILES), jnp.int32),
            pltpu.SMEM((3, TILES), jnp.int32),
            pltpu.VMEM(square, F32),
            pltpu.VMEM((12, TILES * LANES), F32),
            pltpu.VMEM((WX, 2, ROWS, LANES), F32),
            pltpu.VMEM((96, 3 * ROWS), BF16),
            pltpu.VMEM((2, 136, LANES), F32),
            pltpu.VMEM((2, XROWS, LANES), F32),
            pltpu.VMEM((2, ROWS, LANES), F32),
            pltpu.VMEM((6, LIVE, LANES), F32),
            pltpu.VMEM((6, ROWS, LANES), F32),
            pltpu.VMEM((n_gx, 2, 8, LANES), F32),
            pltpu.VMEM((n_gx, 2, 8, LANES), F32),
            pltpu.VMEM((2, ROWS, LANES), F32),
            pltpu.VMEM((2, 2, ROWS, LANES), F32),
            pltpu.VMEM((2, FIX, LANES), F32),
            pltpu.VMEM((2, 2, XROWS, LANES), F32),
            pltpu.VMEM((2, 3, XROWS, LANES), F32),
            pltpu.VMEM((2, 8, LANES), F32),
            pltpu.VMEM((2, PAIRS, 8, LANES), F32),
            pltpu.VMEM((3, PAIRS, 8, LANES), F32),
            pltpu.VMEM((3, FIX, LANES), F32),
            pltpu.VMEM((2, 2, XROWS, LANES), F32),
            pltpu.VMEM((9, 8, LANES), F32),
            pltpu.VMEM((STACKS, 8, LANES), F32),
            pltpu.VMEM((2, 3, 2, XROWS, LANES), F32),
            pltpu.VMEM((2, 2, ROWS, LANES), F32),
            pltpu.VMEM((8, LANES), F32),
            pltpu.VMEM((2, 2, 8, LANES), F32),
            pltpu.VMEM((3, 8, LANES), F32),
            pltpu.VMEM((12, 2, 8, LANES), F32),
            pltpu.VMEM((TILES, 16, LANES), F32),
            pltpu.VMEM((TILES, 8, LANES), F32),
            pltpu.VMEM(square, F32),
            pltpu.VMEM((1, LANES), F32),
            pltpu.VMEM((15, 1, LANES), F32),
            pltpu.VMEM((1, LANES), F32),
            pltpu.VMEM((15, 1, LANES), F32),
            dma((4,)),
            dma((2, n_gx)),
            dma((2, n_gx)),
            dma((2, 2)),
            dma((2, 6)),
            dma((2, 6)),
            dma((2, 4)),
            dma((2, 9)),
            dma((2, 3)),
            dma((2, 12)),
            dma((2, 15)),
            dma((2, 15)),
        ],
        compiler_params=pltpu.CompilerParams(
            collective_id=0, has_side_effects=True, vmem_limit_bytes=24 << 20
        ),
        name="solve",
    )(
        away(stencil_base),
        away(iterate.reshape(square)),
        away(noise.reshape(square)),
        away(interp_weights),
        keep(lengths),
        keep(grid),
        keep(live_dir),
        keep(live_res),
        keep(live),
    )

    outs = pl.pallas_call(
        update_kernel,
        out_shape=[jax.ShapeDtypeStruct(square, F32)] * 3,
        in_specs=[in_vmem] * 6,
        out_specs=[in_vmem] * 3,
        name="update",
    )(keep(sums), keep(kept), keep(live), keep(live_dir), keep(live_res), keep(image))
    return tuple(out.reshape(-1) for out in outs)


def solution(mesh):
    sizes = tuple(mesh.shape[axis] for axis in ("gx", "gy", "gz"))
    lines = P(("gx", "gy", "gz"))
    return jax.shard_map(
        functools.partial(body, sizes),
        mesh=mesh,
        in_specs=(lines, lines, lines, lines, P(None, ("gx", "gy", "gz")), P(None, ("gx", "gy", "gz")), lines, P()),
        out_specs=(lines, lines, lines),
        check_vma=False,
    )
```

```python
import functools

import jax
import jax.numpy as jnp
from jax import lax
from jax.experimental import pallas as pl
from jax.experimental.pallas import tpu as pltpu
from jax.sharding import PartitionSpec as P

F32 = jnp.float32
BF16 = jnp.bfloat16
LANES = 128
TILES = 128
NX, NY, NZ = 32, 64, 128
WX = NX + 3
TOP = 4
ROWS = 80
LIVE = 72
YT = LIVE // 8
OWN, SPARE, CHANNELS, COPIES = 5, 8, 6, 20
STACKS = -(-WX * YT // COPIES)
PAIRS = STACKS // 2
XROWS = 40
SIDE, FIX = XROWS, XROWS + 8
SPLIT = 24
PACK = SPARE + CHANNELS - OWN
OWNERS = ROWS // 8
MESH = pl.DeviceIdType.MESH


def iota(shape, dim):
    return lax.broadcasted_iota(jnp.int32, shape, dim)


def full(value):
    return jnp.full((1, LANES), value, F32)


def decay(distance, length):
    return jnp.exp(-distance.astype(F32) / length)


def outgoing(kind, source, size, length):
    one = decay(full(1), length) - jnp.exp(full(1.0) / length)
    two = decay(full(2), length) - jnp.exp(full(2.0) / length)
    one, two = one[:, :1], two[:, :1]
    zero = jnp.zeros(source.shape, F32)
    if kind == 0:
        return decay(size + 1 - source, length)
    if kind == 1:
        return jnp.where(source == size, one, jnp.where(source == size + 1, two, zero))
    if kind == 2:
        return jnp.where(source == size + 1, one, zero)
    if kind == 3:
        return decay(source + 1, length)
    if kind == 4:
        return jnp.where(source == -1, two, jnp.where(source == 0, one, zero))
    return jnp.where(source == -1, one, zero)


def incoming(kind, cell, size, length):
    if kind == 0:
        return decay(cell - 1, length)
    if kind == 3:
        return decay(size - 1 - cell, length)
    target = {1: -1, 2: 0, 4: size + 1, 5: size}[kind]
    return jnp.where(cell == target, 1.0, 0.0).astype(F32)


def lane_roles(lane):
    spare = lane >= SPARE
    place = jnp.maximum(lane - SPARE, 0)
    copy = place // CHANNELS
    return jnp.where(spare, place - copy * CHANNELS, -1), jnp.where(spare, copy, -1)


def line_row(x):
    return (x + XROWS - 8) % XROWS


def pair_place(pair):
    return {0: PAIRS - 2, PAIRS - 1: PAIRS - 1}.get(pair, pair - 1)


def tile_weights(w8, low):
    along_y = jnp.where(low, pltpu.roll(w8, 4, 0), w8)
    first = jnp.where(low, w8[0:1], w8[1:2]) * along_y
    second = jnp.where(low, w8[2:3], w8[3:4]) * along_y
    return first, second, along_y


def fetch(pairs, sem):
    copies = [pltpu.make_async_copy(src, dst, sem.at[i]) for i, (src, dst) in enumerate(pairs)]
    for copy in copies:
        copy.start()
    return copies


def spread_kernel(
    count_hbm,
    base_hbm,
    reach_hbm,
    w_hbm,
    direction_hbm,
    residual_hbm,
    grid,
    live_dir,
    live_res,
    live,
    lengths,
    table,
    count,
    base,
    reach,
    w,
    direction,
    residual,
    sem,
):
    copies = fetch(
        (
            (reach_hbm, reach),
            (w_hbm, w),
            (count_hbm, count),
            (base_hbm, base),
            (direction_hbm, direction),
            (residual_hbm, residual),
        ),
        sem,
    )

    def clear(x, carry):
        for half in range(2):
            grid[x, half] = jnp.zeros((ROWS, LANES), F32)
        return carry

    lax.fori_loop(0, WX, clear, 0)
    copies[0].wait()
    anchor_x = lax.axis_index("gx") * NX
    anchor_y = lax.axis_index("gy") * NY
    anchor_z = lax.axis_index("gz") * NZ
    length = reach[2] * float(NZ)
    scale = 1.0 / (
        jnp.sqrt(full(reach[0] * float(NX))) * jnp.sqrt(full(reach[1] * float(NY))) * jnp.sqrt(full(length))
    )
    source = iota((136, LANES), 0) - 1
    lane = iota((136, LANES), 1)
    for i, size in enumerate((NX, NY, NZ)):
        lengths[i : i + 1, :] = full(reach[i] * float(size))
    table[0] = decay(jnp.abs(lane - 1 - source), length) * scale
    own = (lane >= OWN) & (lane < SPARE)
    second = jnp.where(own, decay(jnp.abs(lane - OWN + NZ - 1 - source), length), 0.0)
    channel, _ = lane_roles(lane)
    for kind in range(CHANNELS):
        second = jnp.where(channel == kind, outgoing(kind, source, NZ, length), second)
    table[1] = second * scale
    for copy in copies[1:]:
        copy.wait()
    low = iota((8, LANES), 0) < 4
    slot = iota((1, LANES), 1)

    def tile(t, carry):
        at = pl.ds(pl.multiple_of(t * LANES, LANES), LANES)
        w8 = w[0:8, at]
        mask = slot < count[t]
        values = jnp.where(mask, direction[pl.ds(t, 1), :], 0.0)
        live_dir[pl.ds(t, 1), :] = values
        live_res[pl.ds(t, 1), :] = jnp.where(mask, residual[pl.ds(t, 1), :], 0.0)
        live[pl.ds(t, 1), :] = jnp.where(mask, 1.0, 0.0)
        first, second, _ = tile_weights(w8, low)
        x0 = base[0, t] - anchor_x + 1
        y0 = base[1, t] - anchor_y + 1 + TOP
        z0 = base[2, t] - anchor_z + 1
        parts = [[None, None], [None, None]]
        for e in range(4):
            along_z = w[8 + e : 9 + e, at] * values
            row = [table[half, pl.ds(z0 + e, 1), :] for half in range(2)]
            for pair, product in enumerate((first, second)):
                taps = jnp.sum(product * along_z, axis=1, keepdims=True)
                for half in range(2):
                    term = taps * row[half]
                    parts[pair][half] = term if e == 0 else parts[pair][half] + term
        for a in range(4):
            start = y0 if a % 2 == 0 else y0 - 4
            keep = low if a % 2 == 0 else jnp.logical_not(low)
            for half in range(2):
                spot = (x0 + a, half, pl.ds(start, 8), slice(None))
                grid[spot] = grid[spot] + jnp.where(keep, parts[a // 2][half], 0.0)
        return carry

    lax.fori_loop(0, TILES, tile, 0, unroll=32)


def solve_kernel(
    sizes,
    base_hbm,
    iterate_hbm,
    noise_hbm,
    w_hbm,
    lengths,
    grid,
    live_dir,
    live_res,
    live,
    image,
    sums,
    iterate,
    base,
    spot,
    noise,
    w,
    smooth,
    basis,
    pick_z,
    pick_x,
    pick_y,
    x_side,
    x_out,
    x_in,
    x_prefix,
    x_far,
    x_fix_in,
    y_msg,
    y_fix,
    y_side,
    diagonal,
    z_out,
    z_in,
    y_in,
    y_fix_in,
    diagonal_in,
    z_mixed,
    y_mixed,
    far,
    far_z,
    far_y,
    far_z_in,
    far_y_in,
    near_weight,
    far_weight,
    sampled,
    sum_out,
    sum_in_x,
    sum_mid,
    sum_in_yz,
    in_sem,
    x_sem,
    x_back_sem,
    x_fix_sem,
    z_sem,
    y_sem,
    y_fix_sem,
    d_sem,
    fz_sem,
    fy_sem,
    sx_sem,
    syz_sem,
):
    n_gx, n_gy, n_gz = sizes
    n_yz = n_gy * n_gz
    px, py, pz = lax.axis_index("gx"), lax.axis_index("gy"), lax.axis_index("gz")
    pyz = py * n_gz + pz

    def at_x(k):
        return {"gx": lax.rem(px + k, n_gx)}

    def at_yz(ky, kz):
        return {"gy": lax.rem(py + ky, n_gy), "gz": lax.rem(pz + kz, n_gz)}

    def around_yz(k):
        other = lax.rem(pyz + k, n_yz)
        return {"gy": other // n_gz, "gz": lax.rem(other, n_gz)}

    barrier = pltpu.get_barrier_semaphore()
    for k in range(1, n_gx):
        pl.semaphore_signal(barrier, inc=1, device_id=at_x(k), device_id_type=MESH)
    for k in range(1, n_yz):
        pl.semaphore_signal(barrier, inc=1, device_id=around_yz(k), device_id_type=MESH)
    copies_in = fetch(((base_hbm, base), (noise_hbm, noise), (w_hbm, w), (iterate_hbm, iterate)), in_sem)
    length_x, length_y, length_z = (lengths[i : i + 1, 0:1] for i in range(3))
    sent = []

    def chunk(c):
        return pl.ds(pl.multiple_of(c * 8, 8), 8)

    def send(src, dst, sems, index, device, when=None, slot=None):
        copy = pltpu.make_async_remote_copy(
            src_ref=src,
            dst_ref=dst,
            send_sem=sems.at[0, index],
            recv_sem=sems.at[1, index if slot is None else slot],
            device_id=device,
            device_id_type=MESH,
        )
        if when is None:
            copy.start()
            sent.append(copy.wait_send)
        else:
            pl.when(when)(copy.start)
            sent.append(lambda: pl.when(when)(copy.wait_send))
        return copy

    def way(pos, k, count):
        return jnp.where(pos + k < count, 0, 1)

    def mix(pos, count, size, length, k):
        from_left = pos >= k
        left = jnp.where(from_left, jnp.exp(full(-float(size * (k - 1))) / length), 0.0)
        right = jnp.where(from_left, 0.0, jnp.exp(full(-float(size * (count - k - 1))) / length))
        next_left = jnp.where(from_left, full(1.0), 0.0) if k == 1 else full(0.0)
        next_right = jnp.where(from_left, 0.0, full(1.0)) if count - k == 1 else full(0.0)
        return (left, next_left), (right, next_right)

    sub = iota((8, LANES), 0)
    lane = iota((8, LANES), 1)
    low = sub < 4
    channel, copy_of = lane_roles(lane)
    first_kinds = (channel >= 0) & (channel < 3)
    is_moment = (channel == 0) | (channel == 3)

    step_x = jnp.exp(full(-1.0) / length_x)
    fix_one = step_x - jnp.exp(full(1.0) / length_x)
    fix_two = jnp.exp(full(-2.0) / length_x) - jnp.exp(full(2.0) / length_x)

    def moments(yt, carry):
        rows = pl.ds(pl.multiple_of(yt * 8, 8), 8)
        for half, out in enumerate((x_out, x_side)):
            edge = [grid[x, half, rows, :] for x in (0, 1, WX - 2, WX - 1)]
            up, down = edge[0], edge[3]
            for x in range(1, WX):
                up = grid[x, half, rows, :] + step_x * up
                down = grid[WX - 1 - x, half, rows, :] + step_x * down
            out[0, rows, :] = up
            out[1, rows, :] = down
            out[2, rows, :] = edge[2] * fix_one + edge[3] * fix_two
            out[3, rows, :] = edge[3] * fix_one
            out[4, rows, :] = edge[0] * fix_two + edge[1] * fix_one
            out[5, rows, :] = edge[0] * fix_one
        return carry

    lax.fori_loop(0, YT, moments, 0, unroll=3)
    for plane in range(6):
        total = jnp.zeros((8, LANES), F32)
        for yt in range(YT):
            moved = pltpu.roll(x_side[plane, 8 * yt : 8 * yt + 8, :], (PACK * yt - OWN) % LANES, 1)
            total = jnp.where((lane >= PACK * yt) & (lane < PACK * (yt + 1)), moved, total)
        x_out[plane, LIVE:ROWS, :] = total

    def unpack(packed, yt):
        place = PACK * yt + jnp.where(lane < SPARE, jnp.maximum(lane - OWN, 0), channel + SPARE - OWN)
        return jnp.where(lane < OWN, 0.0, jnp.take_along_axis(packed, place, axis=1))

    pl.semaphore_wait(barrier, n_gx - 1 + n_yz - 1)
    x_right = send(x_out.at[pl.ds(2, 2)], x_fix_in.at[0], x_fix_sem, 0, at_x(1), px + 1 < n_gx)
    x_left = send(x_out.at[pl.ds(4, 2)], x_fix_in.at[1], x_fix_sem, 1, at_x(n_gx - 1), px > 0)
    for c in range(OWNERS):
        send(x_out.at[pl.ds(0, 2), chunk(c), :], x_in.at[px], x_sem, c, {"gx": c}, px != c, px)

    def scan(yt, carry):
        rows = pl.ds(pl.multiple_of(yt * 8, 8), 8)
        for half in range(2):
            state = grid[0, half, rows, :]
            smooth[0, half, rows, :] = state
            for x in range(1, WX):
                state = grid[x, half, rows, :] + step_x * state
                smooth[x, half, rows, :] = state
            state = step_x * grid[WX - 1, half, rows, :]
            for x in reversed(range(WX - 1)):
                smooth[x, half, rows, :] = smooth[x, half, rows, :] + state
                if x > 0:
                    state = step_x * (state + grid[x, half, rows, :])
        return carry

    lax.fori_loop(0, YT, scan, 0, unroll=3)
    for x in range(WX):
        for half in range(2):
            smooth[x, half, LIVE:ROWS, :] = jnp.zeros((ROWS - LIVE, LANES), F32)

    row = iota((96, 3 * ROWS), 0)
    col = iota((96, 3 * ROWS), 1)
    part = col // ROWS
    source = col - part * ROWS - TOP - 1
    cell = row - TOP - 1
    entry = jnp.where((cell >= -1) & (cell <= NY + 1), decay(jnp.abs(cell - source), length_y), 0.0)
    for kind in range(CHANNELS):
        entry = jnp.where(row == ROWS + kind + kind // 3, outgoing(kind, source, NY, length_y), entry)
    entry = jnp.where((source >= -1) & (source <= NY + 1), entry, 0.0)
    entry_high = entry.astype(BF16).astype(F32)
    basis[...] = jnp.where(part == 1, entry - entry_high, entry_high).astype(BF16)

    def contract(planes):
        values = jnp.concatenate(planes, axis=1)
        high = values.astype(BF16)
        rest = (values - high.astype(F32)).astype(BF16)
        stacked = jnp.concatenate([high, high, rest], axis=0)
        return jnp.dot(basis[...], stacked, preferred_element_type=F32)

    def back(q):
        return pltpu.make_async_remote_copy(
            src_ref=x_prefix.at[q],
            dst_ref=x_far.at[:, chunk(px), :],
            send_sem=x_back_sem.at[0, q],
            recv_sem=x_back_sem.at[1, px],
            device_id={"gx": q},
            device_id_type=MESH,
        )

    def contract_own(x):
        result = contract([smooth[x, 0], smooth[x, 1]])
        for half in range(2):
            smooth[x, half] = result[:ROWS, LANES * half : LANES * (half + 1)]
        for side in range(2):
            for kind in range(3):
                line = result[ROWS + 4 * side + kind : ROWS + 4 * side + kind + 1]
                at = pl.ds(line_row(x), 1)
                if kind == 0:
                    y_msg[side, at, :] = line[:, :LANES]
                else:
                    y_fix[side, kind - 1, at, :] = line[:, :LANES]
                y_side[side, kind, at, :] = line[:, LANES:]

    def contract_step(x, carry):
        contract_own(x)
        return carry

    lax.fori_loop(2, WX - 3, contract_step, 0, unroll=5)

    contract_own(WX - 3)
    stacks = [jnp.zeros((8, LANES), F32) for _ in range(STACKS)]

    def stacked_planes(planes):
        for x in planes:
            for yt in range(YT):
                stack, copy = divmod(x * YT + yt, COPIES)
                stacks[stack] = jnp.where(copy_of == copy, smooth[x, 1, 8 * yt : 8 * yt + 8, :], stacks[stack])

    def pair_up(pair):
        one, two = stacks[2 * pair], stacks[2 * pair + 1]
        z_out[0, pair_place(pair)] = jnp.where(first_kinds, one, pltpu.roll(two, 3, 1))
        z_out[1, pair_place(pair)] = jnp.where(first_kinds, pltpu.roll(one, LANES - 3, 1), two)

    early, late = pl.ds(0, PAIRS - 2), pl.ds(PAIRS - 2, 2)
    full_rows, rest_rows, rest_fix = pl.ds(0, SPLIT), pl.ds(SPLIT, FIX - SPLIT), pl.ds(SPLIT, XROWS - SPLIT)
    stacked_planes(range(2, WX - 2))
    for pair in range(1, PAIRS - 1):
        pair_up(pair)
    z_copies = [
        send(z_out.at[way(pz, k, n_gz), early], z_in.at[k - 1, early], z_sem, k - 1, at_yz(0, k))
        for k in range(1, n_gz)
    ]

    y_copies = [
        send(y_msg.at[way(py, k, n_gy), full_rows], y_in.at[k - 1, full_rows], y_sem, k - 1, at_yz(k, 0))
        for k in range(1, n_gy)
    ]
    y_fixes = []

    def send_fixes(rows, index):
        if n_gy > 1:
            right = send(
                y_fix.at[0, :, rows], y_fix_in.at[0, :, rows], y_fix_sem, index, at_yz(1, 0), py + 1 < n_gy
            )
            left = send(
                y_fix.at[1, :, rows], y_fix_in.at[1, :, rows], y_fix_sem, index + 1, at_yz(n_gy - 1, 0), py > 0
            )
            y_fixes.append((right, left))

    send_fixes(full_rows, 0)

    def received(dst, sems, slot):
        pltpu.make_async_remote_copy(
            src_ref=dst,
            dst_ref=dst,
            send_sem=sems.at[0, slot],
            recv_sem=sems.at[1, slot],
            device_id={"gx": slot},
            device_id_type=MESH,
        ).wait_recv()

    ratio = jnp.exp(full(-float(NX)) / length_x)

    @pl.when(px < OWNERS)
    def _():
        x_in[px] = x_out[0:2, chunk(px), :]
        for p in range(n_gx):
            pl.when(px != p)(lambda: received(x_in.at[p], x_sem, p))
        for side, order in enumerate((range(n_gx), reversed(range(n_gx)))):
            total = jnp.zeros((8, LANES), F32)
            for q in order:
                x_prefix[q, side] = total
                total = total * ratio + x_in[q, side]
        x_far[:, chunk(px), :] = x_prefix[px]
        for q in range(n_gx):
            pl.when(px != q)(back(q).start)

    if n_gx > 1:
        pl.when(px > 0)(x_right.wait_recv)
        pl.when(px + 1 < n_gx)(x_left.wait_recv)
    for side, valid, places in ((0, px > 0, (0, 1)), (1, px + 1 < n_gx, (WX - 1, WX - 2))):
        for kind, x in enumerate(places):
            smooth[x, 0, 0:LIVE, :] += jnp.where(valid, x_fix_in[side, kind, 0:LIVE, :], 0.0)
            packed = jnp.where(valid, x_fix_in[side, kind, LIVE:ROWS, :], 0.0)
            for yt in range(YT):
                smooth[x, 1, 8 * yt : 8 * yt + 8, :] += unpack(packed, yt)
    for x in (0, 1, WX - 2, WX - 1):
        contract_own(x)

    stacked_planes((0, 1, WX - 2, WX - 1))
    pair_up(0)
    pair_up(PAIRS - 1)
    for side in range(2):
        beside = jnp.zeros((8, LANES), F32)
        both = jnp.zeros((8, LANES), F32)
        for j in range(15):
            kind, xt = divmod(j, 5)
            value = y_side[side, kind, 8 * xt : 8 * xt + 8, :]
            moved = pltpu.roll(value, 8 * j, 1) if j else value
            beside = jnp.where((lane >= 8 * j) & (lane < 8 * j + 8), moved, beside)
            both = jnp.where(copy_of == j, value, both)
        y_msg[side, SIDE : SIDE + 8, :] = beside
        diagonal[side] = both
    z_copies += [
        send(z_out.at[way(pz, k, n_gz), late], z_in.at[k - 1, late], z_sem, k + 2, at_yz(0, k))
        for k in range(1, n_gz)
    ]
    y_copies += [
        send(y_msg.at[way(py, k, n_gy), rest_rows], y_in.at[k - 1, rest_rows], y_sem, k + 2, at_yz(k, 0))
        for k in range(1, n_gy)
    ]
    send_fixes(rest_fix, 2)
    d_copies = {}
    for ky in range(1, n_gy):
        for kz in range(1, n_gz):
            index = (ky - 1) * (n_gz - 1) + kz - 1
            d_copies[ky, kz] = send(
                diagonal.at[way(py, ky, n_gy)], diagonal_in.at[index], d_sem, index, at_yz(ky, kz)
            )

    copies_in[0].wait()

    def locate(t, carry):
        spot[0, t] = jnp.clip(base[0, t] - px * NX + 1, 0, NX - 1)
        spot[1, t] = jnp.clip(base[1, t] - py * NY + 1, 0, NY - 1) + TOP
        spot[2, t] = jnp.clip(base[2, t] - pz * NZ + 1, 0, NZ - 1)
        return carry

    lax.fori_loop(0, TILES, locate, 0, unroll=8)

    cell = iota((136, LANES), 0) - 1
    wide = iota((136, LANES), 1)
    pick_z[0] = jnp.where(wide == cell + 1, 1.0, 0.0).astype(F32)
    picked = jnp.where((wide >= OWN) & (wide < SPARE) & (wide - OWN + NZ - 1 == cell), 1.0, 0.0).astype(F32)
    wide_channel, _ = lane_roles(wide)
    for kind in range(CHANNELS):
        picked = jnp.where(wide_channel == kind, incoming(kind, cell, NZ, length_z), picked)
    pick_z[1] = picked
    cell = iota((XROWS, LANES), 0) - 1
    for side in range(2):
        pick_x[side] = incoming(3 * side, cell, NX, length_x)
    cell = iota((ROWS, LANES), 0) - TOP - 1
    for side in range(2):
        pick_y[side] = incoming(3 * side, cell, NY, length_y)

    for copy in copies_in[1:]:
        copy.wait()

    def weigh(t, carry):
        w8 = w[0:8, pl.ds(pl.multiple_of(t * LANES, LANES), LANES)]
        first, second, along_y = tile_weights(w8, low)
        along_x = []
        for side in range(2):
            total = None
            for a in range(4):
                term = w8[a : a + 1] * pick_x[side, pl.ds(spot[0, t] + a, 1), :]
                total = term if a == 0 else total + term
            along_x.append(total)
        near_weight[t, 0:8, :] = first
        near_weight[t, 8:16, :] = second
        far_weight[t] = jnp.where(low, along_x[0], along_x[1]) * along_y
        return carry

    lax.fori_loop(0, TILES, weigh, 0, unroll=8)

    for c in range(OWNERS):
        pl.when(px != c)(lambda: received(x_far.at[:, chunk(c), :], x_back_sem, c))
    for side in range(2):
        far[side, 0, 0:LIVE, :] = x_far[side, 0:LIVE, :]
        for yt in range(YT):
            far[side, 1, 8 * yt : 8 * yt + 8, :] = unpack(x_far[side, LIVE:ROWS, :], yt)
        for half in range(2):
            far[side, half, LIVE:ROWS, :] = jnp.zeros((ROWS - LIVE, LANES), F32)
    total = jnp.zeros((8, LANES), F32)
    for side in range(2):
        result = contract([far[side, 0], far[side, 1]])
        for half in range(2):
            values = result[:, LANES * half : LANES * (half + 1)]
            far[side, half] = values[:ROWS]
            for to in range(2):
                far_y[to, half, 4 * side : 4 * side + 4, :] = values[ROWS + 4 * to : ROWS + 4 * to + 4]
        for yt in range(YT):
            j = side * YT + yt
            total = jnp.where(copy_of == j, result[8 * yt : 8 * yt + 8, LANES:], total)
    far_z[...] = total
    far_z_copies = [send(far_z, far_z_in.at[k - 1], fz_sem, k - 1, at_yz(0, k)) for k in range(1, n_gz)]
    far_y_copies = {}
    for ky in range(1, n_gy):
        for kz in range(n_gz):
            index = (ky - 1) * n_gz + kz
            far_y_copies[ky, kz] = send(
                far_y.at[way(py, ky, n_gy)], far_y_in.at[index], fy_sem, index, at_yz(ky, kz)
            )

    def channel_weights(k):
        (left, next_left), (right, next_right) = mix(pz, n_gz, NZ, length_z, k)
        return jnp.where(
            first_kinds,
            jnp.where(is_moment, left, next_left),
            jnp.where(channel >= 3, jnp.where(is_moment, right, next_right), 0.0),
        )

    from_z = [[jnp.zeros((8, LANES), F32) for _ in range(PAIRS)] for _ in range(2)]
    for k in range(1, n_gz):
        z_copies[k - 1].wait_recv()
        z_copies[k + n_gz - 2].wait_recv()
        weights = [jnp.where(is_moment, moment, fix) for moment, fix in mix(pz, n_gz, NZ, length_z, k)]
        for pair in range(PAIRS):
            got = z_in[k - 1, pair_place(pair)]
            for side in range(2):
                from_z[side][pair] = from_z[side][pair] + weights[side] * got
    for pair in range(PAIRS):
        one, two = from_z[0][pair], from_z[1][pair]
        z_mixed[2 * pair] = jnp.where(first_kinds, one, pltpu.roll(two, 3, 1))
        z_mixed[2 * pair + 1] = jnp.where(first_kinds, pltpu.roll(one, LANES - 3, 1), two)
    beside = [jnp.zeros((8, LANES), F32) for _ in range(2)]
    both = [jnp.zeros((8, LANES), F32) for _ in range(2)]
    lines = [[jnp.zeros((8, LANES), F32) for _ in range(XROWS // 8)] for _ in range(2)]
    for ky in range(1, n_gy):
        y_copies[ky - 1].wait_recv()
        y_copies[ky + n_gy - 2].wait_recv()
        weights = mix(py, n_gy, NY, length_y, ky)
        for side in range(2):
            moment, fix = weights[side]
            for tile in range(XROWS // 8):
                lines[side][tile] = lines[side][tile] + moment * y_in[ky - 1, 8 * tile : 8 * tile + 8, :]
            beside[side] = beside[side] + jnp.where(lane < 40, moment, fix) * y_in[ky - 1, SIDE : SIDE + 8, :]
        for kz in range(1, n_gz):
            d_copies[ky, kz].wait_recv()
            got = channel_weights(kz) * diagonal_in[(ky - 1) * (n_gz - 1) + kz - 1]
            for side in range(2):
                moment, fix = weights[side]
                both[side] = both[side] + jnp.where(copy_of < 5, moment, fix) * got
    for right, left in y_fixes:
        pl.when(py > 0)(right.wait_recv)
        pl.when(py + 1 < n_gy)(left.wait_recv)
    for side, valid in enumerate((py > 0, py + 1 < n_gy)):
        for tile in range(XROWS // 8):
            y_mixed[side, 0, 0, 8 * tile : 8 * tile + 8, :] = lines[side][tile]
        for kind in range(1, 3):
            y_mixed[side, kind, 0] = jnp.where(valid, y_fix_in[side, kind - 1], 0.0)
        for j in range(15):
            kind, xt = divmod(j, 5)
            moved = pltpu.roll(beside[side], LANES - 8 * j, 1) if j else beside[side]
            y_mixed[side, kind, 1, 8 * xt : 8 * xt + 8, :] = jnp.where(
                lane < SPARE, moved, jnp.where(copy_of == j, both[side], 0.0)
            )

    def expand(x, carry):
        for half in range(2):
            line = [
                [y_mixed[side, kind, half, pl.ds(line_row(x), 1), :] for kind in range(3)] for side in range(2)
            ]
            for yt in range(YT):
                rows = slice(8 * yt, 8 * yt + 8)
                value = smooth[x, half, rows, :]
                if half == 1:
                    j = x * YT + yt
                    stack = j // COPIES
                    value = jnp.where(
                        lane < SPARE, value, jnp.where(copy_of == j - stack * COPIES, z_mixed[stack], 0.0)
                    )
                for side in range(2):
                    value = value + pick_y[side, rows, :] * line[side][0]
                if yt == 0:
                    value = value + jnp.where(sub == 4, line[0][1], jnp.where(sub == 5, line[0][2], 0.0))
                if yt == YT - 1:
                    value = value + jnp.where(sub == 6, line[1][1], jnp.where(sub == 5, line[1][2], 0.0))
                smooth[x, half, rows, :] = value
        return carry

    lax.fori_loop(0, WX, expand, 0, unroll=5)

    def tile_spot(t):
        at = pl.ds(pl.multiple_of(t * LANES, LANES), LANES)
        return at, spot[0, t], spot[1, t], spot[2, t]

    def gather(rows, weights, at, z0):
        total = None
        for e in range(4):
            pick = [pick_z[half, pl.ds(z0 + e, 1), :] for half in range(2)]
            inner = None
            for cells, weight in zip(rows, weights):
                taps = jnp.sum(cells[0] * pick[0] + cells[1] * pick[1], axis=1, keepdims=True)
                inner = weight * taps if inner is None else inner + weight * taps
            inner = inner * w[8 + e : 9 + e, at]
            total = inner if e == 0 else total + inner
        return jnp.sum(total, axis=0, keepdims=True)

    def near(t, carry):
        at, x0, y0, z0 = tile_spot(t)
        rows = [
            [
                jnp.where(
                    low, smooth[x0 + a, half, pl.ds(y0, 8), :], smooth[x0 + a + 1, half, pl.ds(y0 - 4, 8), :]
                )
                for half in range(2)
            ]
            for a in (0, 2)
        ]
        sampled[pl.ds(t, 1), :] = gather(rows, (near_weight[t, 0:8, :], near_weight[t, 8:16, :]), at, z0)
        return carry

    lax.fori_loop(0, TILES, near, 0, unroll=32)

    from_z = jnp.zeros((8, LANES), F32)
    for k in range(1, n_gz):
        far_z_copies[k - 1].wait_recv()
        from_z = from_z + channel_weights(k) * far_z_in[k - 1]
    lines = [[jnp.zeros((8, LANES), F32) for _ in range(2)] for _ in range(2)]
    for ky in range(1, n_gy):
        weights = mix(py, n_gy, NY, length_y, ky)
        weights = [jnp.where((sub == 0) | (sub == 4), moment, fix) for moment, fix in weights]
        for kz in range(n_gz):
            far_y_copies[ky, kz].wait_recv()
            index = (ky - 1) * n_gz + kz
            got = [far_y_in[index, half] for half in range(2)]
            if kz == 0:
                got[1] = jnp.where(lane < SPARE, got[1], 0.0)
            else:
                got = [None, jnp.where(copy_of == 0, channel_weights(kz) * got[1], 0.0)]
            for side in range(2):
                for half in range(2):
                    if got[half] is not None:
                        lines[side][half] = lines[side][half] + weights[side] * got[half]
    for x in range(2):
        for half in range(2):
            line = [[lines[side][half][4 * x + kind : 4 * x + kind + 1] for kind in range(3)] for side in range(2)]
            for yt in range(YT):
                rows = slice(8 * yt, 8 * yt + 8)
                value = far[x, half, rows, :]
                if half == 1:
                    value = jnp.where(lane < SPARE, value, jnp.where(copy_of == x * YT + yt, from_z, 0.0))
                for side in range(2):
                    value = value + pick_y[side, rows, :] * line[side][0]
                if yt == 0:
                    value = value + jnp.where(sub == 4, line[0][1], jnp.where(sub == 5, line[0][2], 0.0))
                if yt == YT - 1:
                    value = value + jnp.where(sub == 6, line[1][1], jnp.where(sub == 5, line[1][2], 0.0))
                far[x, half, rows, :] = value

    def distant(t, carry):
        at, x0, y0, z0 = tile_spot(t)
        rows = [jnp.where(low, far[0, half, pl.ds(y0, 8), :], far[1, half, pl.ds(y0 - 4, 8), :]) for half in range(2)]
        sampled[pl.ds(t, 1), :] += gather([rows], [far_weight[t]], at, z0)
        return carry

    lax.fori_loop(0, TILES, distant, 0, unroll=32)

    value = live[...] * (sampled[...] + noise[...] * live_dir[...])
    image[...] = value
    pairs = (
        (live_res[...], live_res[...]),
        (live_dir[...], value),
        (live_res[...], value),
        (value, value),
    )
    place = iota((1, LANES), 1)
    total = jnp.zeros((1, LANES), F32)
    for i, (a, b) in enumerate(pairs):
        part = jnp.sum(jnp.sum(a * b, axis=0, keepdims=True), axis=1, keepdims=True)
        total = jnp.where(place == i, part, total)
    sum_out[...] = total
    copies = [send(sum_out, sum_in_yz.at[k - 1], syz_sem, k - 1, around_yz(k)) for k in range(1, n_yz)]
    for k in range(1, n_yz):
        copies[k - 1].wait_recv()
        total = total + sum_in_yz[k - 1]
    sum_mid[...] = total
    copies = [send(sum_mid, sum_in_x.at[k - 1], sx_sem, k - 1, at_x(k)) for k in range(1, n_gx)]
    for k in range(1, n_gx):
        copies[k - 1].wait_recv()
        total = total + sum_in_x[k - 1]
    sums[...] = total
    for wait in sent:
        wait()

    @pl.when(px < OWNERS)
    def _():
        for q in range(n_gx):
            pl.when(px != q)(back(q).wait_send)


def update_kernel(sums, iterate, live, live_dir, live_res, image, new_iterate, new_residual, new_direction):
    place = iota((1, LANES), 1)

    def total(which):
        return jnp.sum(jnp.where(place == which, sums[...], 0.0), axis=1, keepdims=True)

    norm_old, curvature, cross, square = total(0), total(1), total(2), total(3)
    step = norm_old / curvature
    norm_new = norm_old + step * (step * square - 2.0 * cross)
    held = live_res[...] - step * image[...]
    new_iterate[...] = live[...] * iterate[...] + step * live_dir[...]
    new_residual[...] = held
    new_direction[...] = held + norm_new / norm_old * live_dir[...]


def body(sizes, iterate, residual, direction, noise, stencil_base, interp_weights, tile_counts, reach):
    n_gx, n_gy, n_gz = sizes
    n_yz = n_gy * n_gz
    square = (TILES, LANES)
    in_vmem = pl.BlockSpec(memory_space=pltpu.VMEM)
    in_hbm = pl.BlockSpec(memory_space=pltpu.HBM)
    dma = pltpu.SemaphoreType.DMA

    def away(x):
        return pltpu.with_memory_space_constraint(x, pltpu.HBM)

    def keep(x):
        return pltpu.with_memory_space_constraint(x, pltpu.VMEM)

    grid, live_dir, live_res, live, lengths = pl.pallas_call(
        spread_kernel,
        out_shape=[pltpu.VMEM((WX, 2, ROWS, LANES), F32)] + [pltpu.VMEM(square, F32)] * 3 + [pltpu.VMEM((8, LANES), F32)],
        in_specs=[in_hbm] * 6,
        out_specs=[in_vmem] * 5,
        scratch_shapes=[
            pltpu.VMEM((2, 136, LANES), F32),
            pltpu.SMEM((TILES,), jnp.int32),
            pltpu.SMEM((3, TILES), jnp.int32),
            pltpu.SMEM((3,), F32),
            pltpu.VMEM((12, TILES * LANES), F32),
            pltpu.VMEM(square, F32),
            pltpu.VMEM(square, F32),
            dma((6,)),
        ],
        compiler_params=pltpu.CompilerParams(vmem_limit_bytes=16 << 20),
        name="spread",
    )(
        away(tile_counts),
        away(stencil_base),
        away(reach),
        away(interp_weights),
        away(direction.reshape(square)),
        away(residual.reshape(square)),
    )

    image, sums, kept = pl.pallas_call(
        functools.partial(solve_kernel, sizes),
        out_shape=[pltpu.VMEM(square, F32), pltpu.VMEM((1, LANES), F32), pltpu.VMEM(square, F32)],
        in_specs=[in_hbm] * 4 + [in_vmem] * 5,
        out_specs=[in_vmem] * 3,
        scratch_shapes=[
            pltpu.SMEM((3, TILES), jnp.int32),
            pltpu.SMEM((3, TILES), jnp.int32),
            pltpu.VMEM(square, F32),
            pltpu.VMEM((12, TILES * LANES), F32),
            pltpu.VMEM((WX, 2, ROWS, LANES), F32),
            pltpu.VMEM((96, 3 * ROWS), BF16),
            pltpu.VMEM((2, 136, LANES), F32),
            pltpu.VMEM((2, XROWS, LANES), F32),
            pltpu.VMEM((2, ROWS, LANES), F32),
            pltpu.VMEM((6, LIVE, LANES), F32),
            pltpu.VMEM((6, ROWS, LANES), F32),
            pltpu.VMEM((n_gx, 2, 8, LANES), F32),
            pltpu.VMEM((n_gx, 2, 8, LANES), F32),
            pltpu.VMEM((2, ROWS, LANES), F32),
            pltpu.VMEM((2, 2, ROWS, LANES), F32),
            pltpu.VMEM((2, FIX, LANES), F32),
            pltpu.VMEM((2, 2, XROWS, LANES), F32),
            pltpu.VMEM((2, 3, XROWS, LANES), F32),
            pltpu.VMEM((2, 8, LANES), F32),
            pltpu.VMEM((2, PAIRS, 8, LANES), F32),
            pltpu.VMEM((3, PAIRS, 8, LANES), F32),
            pltpu.VMEM((3, FIX, LANES), F32),
            pltpu.VMEM((2, 2, XROWS, LANES), F32),
            pltpu.VMEM((9, 8, LANES), F32),
            pltpu.VMEM((STACKS, 8, LANES), F32),
            pltpu.VMEM((2, 3, 2, XROWS, LANES), F32),
            pltpu.VMEM((2, 2, ROWS, LANES), F32),
            pltpu.VMEM((8, LANES), F32),
            pltpu.VMEM((2, 2, 8, LANES), F32),
            pltpu.VMEM((3, 8, LANES), F32),
            pltpu.VMEM((12, 2, 8, LANES), F32),
            pltpu.VMEM((TILES, 16, LANES), F32),
            pltpu.VMEM((TILES, 8, LANES), F32),
            pltpu.VMEM(square, F32),
            pltpu.VMEM((1, LANES), F32),
            pltpu.VMEM((15, 1, LANES), F32),
            pltpu.VMEM((1, LANES), F32),
            pltpu.VMEM((15, 1, LANES), F32),
            dma((4,)),
            dma((2, n_gx)),
            dma((2, n_gx)),
            dma((2, 2)),
            dma((2, 6)),
            dma((2, 6)),
            dma((2, 4)),
            dma((2, 9)),
            dma((2, 3)),
            dma((2, 12)),
            dma((2, 15)),
            dma((2, 15)),
        ],
        compiler_params=pltpu.CompilerParams(
            collective_id=0, has_side_effects=True, vmem_limit_bytes=24 << 20
        ),
        name="solve",
    )(
        away(stencil_base),
        away(iterate.reshape(square)),
        away(noise.reshape(square)),
        away(interp_weights),
        keep(lengths),
        keep(grid),
        keep(live_dir),
        keep(live_res),
        keep(live),
    )

    outs = pl.pallas_call(
        update_kernel,
        out_shape=[jax.ShapeDtypeStruct(square, F32)] * 3,
        in_specs=[in_vmem] * 6,
        out_specs=[in_vmem] * 3,
        name="update",
    )(keep(sums), keep(kept), keep(live), keep(live_dir), keep(live_res), keep(image))
    return tuple(out.reshape(-1) for out in outs)


def solution(mesh):
    sizes = tuple(mesh.shape[axis] for axis in ("gx", "gy", "gz"))
    lines = P(("gx", "gy", "gz"))
    return jax.shard_map(
        functools.partial(body, sizes),
        mesh=mesh,
        in_specs=(lines, lines, lines, lines, P(None, ("gx", "gy", "gz")), P(None, ("gx", "gy", "gz")), lines, P()),
        out_specs=(lines, lines, lines),
        check_vma=False,
    )
```

```python
import functools

import jax
import jax.numpy as jnp
from jax import lax
from jax.experimental import pallas as pl
from jax.experimental.pallas import tpu as pltpu
from jax.sharding import PartitionSpec as P

F32 = jnp.float32
BF16 = jnp.bfloat16
LANES = 128
TILES = 128
NX, NY, NZ = 32, 64, 128
WX = NX + 3
TOP = 4
ROWS = 80
LIVE = 72
YT = LIVE // 8
OWN, SPARE, CHANNELS, COPIES = 5, 8, 6, 20
STACKS = -(-WX * YT // COPIES)
PAIRS = STACKS // 2
XROWS = 40
SIDE, FIX = XROWS, XROWS + 8
SPLIT = 24
PACK = SPARE + CHANNELS - OWN
OWNERS = ROWS // 8
MESH = pl.DeviceIdType.MESH


def iota(shape, dim):
    return lax.broadcasted_iota(jnp.int32, shape, dim)


def full(value):
    return jnp.full((1, LANES), value, F32)


def decay(distance, length):
    return jnp.exp(-distance.astype(F32) / length)


def outgoing(kind, source, size, length):
    one = decay(full(1), length) - jnp.exp(full(1.0) / length)
    two = decay(full(2), length) - jnp.exp(full(2.0) / length)
    one, two = one[:, :1], two[:, :1]
    zero = jnp.zeros(source.shape, F32)
    if kind == 0:
        return decay(size + 1 - source, length)
    if kind == 1:
        return jnp.where(source == size, one, jnp.where(source == size + 1, two, zero))
    if kind == 2:
        return jnp.where(source == size + 1, one, zero)
    if kind == 3:
        return decay(source + 1, length)
    if kind == 4:
        return jnp.where(source == -1, two, jnp.where(source == 0, one, zero))
    return jnp.where(source == -1, one, zero)


def incoming(kind, cell, size, length):
    if kind == 0:
        return decay(cell - 1, length)
    if kind == 3:
        return decay(size - 1 - cell, length)
    target = {1: -1, 2: 0, 4: size + 1, 5: size}[kind]
    return jnp.where(cell == target, 1.0, 0.0).astype(F32)


def lane_roles(lane):
    spare = lane >= SPARE
    place = jnp.maximum(lane - SPARE, 0)
    copy = place // CHANNELS
    return jnp.where(spare, place - copy * CHANNELS, -1), jnp.where(spare, copy, -1)


def line_row(x):
    return (x + XROWS - 8) % XROWS


def pair_place(pair):
    return {0: PAIRS - 2, PAIRS - 1: PAIRS - 1}.get(pair, pair - 1)


def tile_weights(w8, low):
    along_y = jnp.where(low, pltpu.roll(w8, 4, 0), w8)
    first = jnp.where(low, w8[0:1], w8[1:2]) * along_y
    second = jnp.where(low, w8[2:3], w8[3:4]) * along_y
    return first, second, along_y


def fetch(pairs, sem):
    copies = [pltpu.make_async_copy(src, dst, sem.at[i]) for i, (src, dst) in enumerate(pairs)]
    for copy in copies:
        copy.start()
    return copies


def spread_kernel(
    count_hbm,
    base_hbm,
    reach_hbm,
    w_hbm,
    direction_hbm,
    residual_hbm,
    grid,
    live_dir,
    live_res,
    live,
    lengths,
    table,
    count,
    base,
    reach,
    w,
    direction,
    residual,
    sem,
):
    copies = fetch(
        (
            (reach_hbm, reach),
            (w_hbm, w),
            (count_hbm, count),
            (base_hbm, base),
            (direction_hbm, direction),
            (residual_hbm, residual),
        ),
        sem,
    )

    def clear(x, carry):
        for half in range(2):
            grid[x, half] = jnp.zeros((ROWS, LANES), F32)
        return carry

    lax.fori_loop(0, WX, clear, 0)
    copies[0].wait()
    anchor_x = lax.axis_index("gx") * NX
    anchor_y = lax.axis_index("gy") * NY
    anchor_z = lax.axis_index("gz") * NZ
    length = reach[2] * float(NZ)
    scale = 1.0 / (
        jnp.sqrt(full(reach[0] * float(NX))) * jnp.sqrt(full(reach[1] * float(NY))) * jnp.sqrt(full(length))
    )
    source = iota((136, LANES), 0) - 1
    lane = iota((136, LANES), 1)
    for i, size in enumerate((NX, NY, NZ)):
        lengths[i : i + 1, :] = full(reach[i] * float(size))
    table[0] = decay(jnp.abs(lane - 1 - source), length) * scale
    own = (lane >= OWN) & (lane < SPARE)
    second = jnp.where(own, decay(jnp.abs(lane - OWN + NZ - 1 - source), length), 0.0)
    channel, _ = lane_roles(lane)
    for kind in range(CHANNELS):
        second = jnp.where(channel == kind, outgoing(kind, source, NZ, length), second)
    table[1] = second * scale
    for copy in copies[1:]:
        copy.wait()
    low = iota((8, LANES), 0) < 4
    slot = iota((1, LANES), 1)

    def tile(t, carry):
        at = pl.ds(pl.multiple_of(t * LANES, LANES), LANES)
        w8 = w[0:8, at]
        mask = slot < count[t]
        values = jnp.where(mask, direction[pl.ds(t, 1), :], 0.0)
        live_dir[pl.ds(t, 1), :] = values
        live_res[pl.ds(t, 1), :] = jnp.where(mask, residual[pl.ds(t, 1), :], 0.0)
        live[pl.ds(t, 1), :] = jnp.where(mask, 1.0, 0.0)
        first, second, _ = tile_weights(w8, low)
        x0 = base[0, t] - anchor_x + 1
        y0 = base[1, t] - anchor_y + 1 + TOP
        z0 = base[2, t] - anchor_z + 1
        parts = [[None, None], [None, None]]
        for e in range(4):
            along_z = w[8 + e : 9 + e, at] * values
            row = [table[half, pl.ds(z0 + e, 1), :] for half in range(2)]
            for pair, product in enumerate((first, second)):
                taps = jnp.sum(product * along_z, axis=1, keepdims=True)
                for half in range(2):
                    term = taps * row[half]
                    parts[pair][half] = term if e == 0 else parts[pair][half] + term
        for a in range(4):
            start = y0 if a % 2 == 0 else y0 - 4
            keep = low if a % 2 == 0 else jnp.logical_not(low)
            for half in range(2):
                spot = (x0 + a, half, pl.ds(start, 8), slice(None))
                grid[spot] = grid[spot] + jnp.where(keep, parts[a // 2][half], 0.0)
        return carry

    lax.fori_loop(0, TILES, tile, 0, unroll=32)


def solve_kernel(
    sizes,
    base_hbm,
    iterate_hbm,
    noise_hbm,
    w_hbm,
    lengths,
    grid,
    live_dir,
    live_res,
    live,
    image,
    sums,
    iterate,
    base,
    spot,
    noise,
    w,
    smooth,
    basis,
    pick_z,
    pick_x,
    pick_y,
    x_side,
    x_out,
    x_in,
    x_prefix,
    x_far,
    x_fix_in,
    y_msg,
    y_fix,
    y_side,
    diagonal,
    z_out,
    z_in,
    y_in,
    y_fix_in,
    diagonal_in,
    z_mixed,
    y_mixed,
    far,
    far_z,
    far_y,
    far_z_in,
    far_y_in,
    near_weight,
    far_weight,
    sampled,
    sum_out,
    sum_in_x,
    sum_mid,
    sum_in_yz,
    in_sem,
    x_sem,
    x_back_sem,
    x_fix_sem,
    z_sem,
    y_sem,
    y_fix_sem,
    d_sem,
    fz_sem,
    fy_sem,
    sx_sem,
    syz_sem,
):
    n_gx, n_gy, n_gz = sizes
    n_yz = n_gy * n_gz
    px, py, pz = lax.axis_index("gx"), lax.axis_index("gy"), lax.axis_index("gz")
    pyz = py * n_gz + pz

    def at_x(k):
        return {"gx": lax.rem(px + k, n_gx)}

    def at_yz(ky, kz):
        return {"gy": lax.rem(py + ky, n_gy), "gz": lax.rem(pz + kz, n_gz)}

    def around_yz(k):
        other = lax.rem(pyz + k, n_yz)
        return {"gy": other // n_gz, "gz": lax.rem(other, n_gz)}

    barrier = pltpu.get_barrier_semaphore()
    for k in range(1, n_gx):
        pl.semaphore_signal(barrier, inc=1, device_id=at_x(k), device_id_type=MESH)
    for k in range(1, n_yz):
        pl.semaphore_signal(barrier, inc=1, device_id=around_yz(k), device_id_type=MESH)
    copies_in = fetch(((base_hbm, base), (noise_hbm, noise), (w_hbm, w), (iterate_hbm, iterate)), in_sem)
    length_x, length_y, length_z = (lengths[i : i + 1, 0:1] for i in range(3))
    sent = []

    def chunk(c):
        return pl.ds(pl.multiple_of(c * 8, 8), 8)

    def send(src, dst, sems, index, device, when=None, slot=None):
        copy = pltpu.make_async_remote_copy(
            src_ref=src,
            dst_ref=dst,
            send_sem=sems.at[0, index],
            recv_sem=sems.at[1, index if slot is None else slot],
            device_id=device,
            device_id_type=MESH,
        )
        if when is None:
            copy.start()
            sent.append(copy.wait_send)
        else:
            pl.when(when)(copy.start)
            sent.append(lambda: pl.when(when)(copy.wait_send))
        return copy

    def way(pos, k, count):
        return jnp.where(pos + k < count, 0, 1)

    def mix(pos, count, size, length, k):
        from_left = pos >= k
        left = jnp.where(from_left, jnp.exp(full(-float(size * (k - 1))) / length), 0.0)
        right = jnp.where(from_left, 0.0, jnp.exp(full(-float(size * (count - k - 1))) / length))
        next_left = jnp.where(from_left, full(1.0), 0.0) if k == 1 else full(0.0)
        next_right = jnp.where(from_left, 0.0, full(1.0)) if count - k == 1 else full(0.0)
        return (left, next_left), (right, next_right)

    sub = iota((8, LANES), 0)
    lane = iota((8, LANES), 1)
    low = sub < 4
    channel, copy_of = lane_roles(lane)
    first_kinds = (channel >= 0) & (channel < 3)
    is_moment = (channel == 0) | (channel == 3)

    step_x = jnp.exp(full(-1.0) / length_x)
    fix_one = step_x - jnp.exp(full(1.0) / length_x)
    fix_two = jnp.exp(full(-2.0) / length_x) - jnp.exp(full(2.0) / length_x)

    def moments(yt, carry):
        rows = pl.ds(pl.multiple_of(yt * 8, 8), 8)
        for half, out in enumerate((x_out, x_side)):
            edge = [grid[x, half, rows, :] for x in (0, 1, WX - 2, WX - 1)]
            up, down = edge[0], edge[3]
            for x in range(1, WX):
                up = grid[x, half, rows, :] + step_x * up
                down = grid[WX - 1 - x, half, rows, :] + step_x * down
            out[0, rows, :] = up
            out[1, rows, :] = down
            out[2, rows, :] = edge[2] * fix_one + edge[3] * fix_two
            out[3, rows, :] = edge[3] * fix_one
            out[4, rows, :] = edge[0] * fix_two + edge[1] * fix_one
            out[5, rows, :] = edge[0] * fix_one
        return carry

    lax.fori_loop(0, YT, moments, 0, unroll=3)
    for plane in range(6):
        total = jnp.zeros((8, LANES), F32)
        for yt in range(YT):
            moved = pltpu.roll(x_side[plane, 8 * yt : 8 * yt + 8, :], (PACK * yt - OWN) % LANES, 1)
            total = jnp.where((lane >= PACK * yt) & (lane < PACK * (yt + 1)), moved, total)
        x_out[plane, LIVE:ROWS, :] = total

    def unpack(packed, yt):
        place = PACK * yt + jnp.where(lane < SPARE, jnp.maximum(lane - OWN, 0), channel + SPARE - OWN)
        return jnp.where(lane < OWN, 0.0, jnp.take_along_axis(packed, place, axis=1))

    pl.semaphore_wait(barrier, n_gx - 1 + n_yz - 1)
    x_right = send(x_out.at[pl.ds(2, 2)], x_fix_in.at[0], x_fix_sem, 0, at_x(1), px + 1 < n_gx)
    x_left = send(x_out.at[pl.ds(4, 2)], x_fix_in.at[1], x_fix_sem, 1, at_x(n_gx - 1), px > 0)
    for c in range(OWNERS):
        send(x_out.at[pl.ds(0, 2), chunk(c), :], x_in.at[px], x_sem, c, {"gx": c}, px != c, px)

    def scan(yt, carry):
        rows = pl.ds(pl.multiple_of(yt * 8, 8), 8)
        for half in range(2):
            state = grid[0, half, rows, :]
            smooth[0, half, rows, :] = state
            for x in range(1, WX):
                state = grid[x, half, rows, :] + step_x * state
                smooth[x, half, rows, :] = state
            state = step_x * grid[WX - 1, half, rows, :]
            for x in reversed(range(WX - 1)):
                smooth[x, half, rows, :] = smooth[x, half, rows, :] + state
                if x > 0:
                    state = step_x * (state + grid[x, half, rows, :])
        return carry

    lax.fori_loop(0, YT, scan, 0, unroll=3)
    for x in range(WX):
        for half in range(2):
            smooth[x, half, LIVE:ROWS, :] = jnp.zeros((ROWS - LIVE, LANES), F32)

    row = iota((96, 3 * ROWS), 0)
    col = iota((96, 3 * ROWS), 1)
    part = col // ROWS
    source = col - part * ROWS - TOP - 1
    cell = row - TOP - 1
    entry = jnp.where((cell >= -1) & (cell <= NY + 1), decay(jnp.abs(cell - source), length_y), 0.0)
    for kind in range(CHANNELS):
        entry = jnp.where(row == ROWS + kind + kind // 3, outgoing(kind, source, NY, length_y), entry)
    entry = jnp.where((source >= -1) & (source <= NY + 1), entry, 0.0)
    entry_high = entry.astype(BF16).astype(F32)
    basis[...] = jnp.where(part == 1, entry - entry_high, entry_high).astype(BF16)

    def contract(planes):
        values = jnp.concatenate(planes, axis=1)
        high = values.astype(BF16)
        rest = (values - high.astype(F32)).astype(BF16)
        stacked = jnp.concatenate([high, high, rest], axis=0)
        return jnp.dot(basis[...], stacked, preferred_element_type=F32)

    def back(q):
        return pltpu.make_async_remote_copy(
            src_ref=x_prefix.at[q],
            dst_ref=x_far.at[:, chunk(px), :],
            send_sem=x_back_sem.at[0, q],
            recv_sem=x_back_sem.at[1, px],
            device_id={"gx": q},
            device_id_type=MESH,
        )

    def contract_own(x):
        result = contract([smooth[x, 0], smooth[x, 1]])
        for half in range(2):
            smooth[x, half] = result[:ROWS, LANES * half : LANES * (half + 1)]
        for side in range(2):
            for kind in range(3):
                line = result[ROWS + 4 * side + kind : ROWS + 4 * side + kind + 1]
                at = pl.ds(line_row(x), 1)
                if kind == 0:
                    y_msg[side, at, :] = line[:, :LANES]
                else:
                    y_fix[side, kind - 1, at, :] = line[:, :LANES]
                y_side[side, kind, at, :] = line[:, LANES:]

    def contract_step(x, carry):
        contract_own(x)
        return carry

    lax.fori_loop(2, WX - 3, contract_step, 0, unroll=5)

    contract_own(WX - 3)
    stacks = [jnp.zeros((8, LANES), F32) for _ in range(STACKS)]

    def stacked_planes(planes):
        for x in planes:
            for yt in range(YT):
                stack, copy = divmod(x * YT + yt, COPIES)
                stacks[stack] = jnp.where(copy_of == copy, smooth[x, 1, 8 * yt : 8 * yt + 8, :], stacks[stack])

    def pair_up(pair):
        one, two = stacks[2 * pair], stacks[2 * pair + 1]
        z_out[0, pair_place(pair)] = jnp.where(first_kinds, one, pltpu.roll(two, 3, 1))
        z_out[1, pair_place(pair)] = jnp.where(first_kinds, pltpu.roll(one, LANES - 3, 1), two)

    early, late = pl.ds(0, PAIRS - 2), pl.ds(PAIRS - 2, 2)
    full_rows, rest_rows, rest_fix = pl.ds(0, SPLIT), pl.ds(SPLIT, FIX - SPLIT), pl.ds(SPLIT, XROWS - SPLIT)
    stacked_planes(range(2, WX - 2))
    for pair in range(1, PAIRS - 1):
        pair_up(pair)
    z_copies = [
        send(z_out.at[way(pz, k, n_gz), early], z_in.at[k - 1, early], z_sem, k - 1, at_yz(0, k))
        for k in range(1, n_gz)
    ]

    y_copies = [
        send(y_msg.at[way(py, k, n_gy), full_rows], y_in.at[k - 1, full_rows], y_sem, k - 1, at_yz(k, 0))
        for k in range(1, n_gy)
    ]
    y_fixes = []

    def send_fixes(rows, index):
        if n_gy > 1:
            right = send(
                y_fix.at[0, :, rows], y_fix_in.at[0, :, rows], y_fix_sem, index, at_yz(1, 0), py + 1 < n_gy
            )
            left = send(
                y_fix.at[1, :, rows], y_fix_in.at[1, :, rows], y_fix_sem, index + 1, at_yz(n_gy - 1, 0), py > 0
            )
            y_fixes.append((right, left))

    send_fixes(full_rows, 0)

    def received(dst, sems, slot):
        pltpu.make_async_remote_copy(
            src_ref=dst,
            dst_ref=dst,
            send_sem=sems.at[0, slot],
            recv_sem=sems.at[1, slot],
            device_id={"gx": slot},
            device_id_type=MESH,
        ).wait_recv()

    ratio = jnp.exp(full(-float(NX)) / length_x)

    @pl.when(px < OWNERS)
    def _():
        x_in[px] = x_out[0:2, chunk(px), :]
        for p in range(n_gx):
            pl.when(px != p)(lambda: received(x_in.at[p], x_sem, p))
        for side, order in enumerate((range(n_gx), reversed(range(n_gx)))):
            total = jnp.zeros((8, LANES), F32)
            for q in order:
                x_prefix[q, side] = total
                total = total * ratio + x_in[q, side]
        x_far[:, chunk(px), :] = x_prefix[px]
        for q in range(n_gx):
            pl.when(px != q)(back(q).start)

    if n_gx > 1:
        pl.when(px > 0)(x_right.wait_recv)
        pl.when(px + 1 < n_gx)(x_left.wait_recv)
    for side, valid, places in ((0, px > 0, (0, 1)), (1, px + 1 < n_gx, (WX - 1, WX - 2))):
        for kind, x in enumerate(places):
            smooth[x, 0, 0:LIVE, :] += jnp.where(valid, x_fix_in[side, kind, 0:LIVE, :], 0.0)
            packed = jnp.where(valid, x_fix_in[side, kind, LIVE:ROWS, :], 0.0)
            for yt in range(YT):
                smooth[x, 1, 8 * yt : 8 * yt + 8, :] += unpack(packed, yt)
    for x in (0, 1, WX - 2, WX - 1):
        contract_own(x)

    stacked_planes((0, 1, WX - 2, WX - 1))
    pair_up(0)
    pair_up(PAIRS - 1)
    for side in range(2):
        beside = jnp.zeros((8, LANES), F32)
        both = jnp.zeros((8, LANES), F32)
        for j in range(15):
            kind, xt = divmod(j, 5)
            value = y_side[side, kind, 8 * xt : 8 * xt + 8, :]
            moved = pltpu.roll(value, 8 * j, 1) if j else value
            beside = jnp.where((lane >= 8 * j) & (lane < 8 * j + 8), moved, beside)
            both = jnp.where(copy_of == j, value, both)
        y_msg[side, SIDE : SIDE + 8, :] = beside
        diagonal[side] = both
    d_copies = {}
    for ky in range(1, n_gy):
        for kz in range(1, n_gz):
            index = (ky - 1) * (n_gz - 1) + kz - 1
            d_copies[ky, kz] = send(
                diagonal.at[way(py, ky, n_gy)], diagonal_in.at[index], d_sem, index, at_yz(ky, kz)
            )
    z_copies += [
        send(z_out.at[way(pz, k, n_gz), late], z_in.at[k - 1, late], z_sem, k + 2, at_yz(0, k))
        for k in range(1, n_gz)
    ]
    y_copies += [
        send(y_msg.at[way(py, k, n_gy), rest_rows], y_in.at[k - 1, rest_rows], y_sem, k + 2, at_yz(k, 0))
        for k in range(1, n_gy)
    ]
    send_fixes(rest_fix, 2)

    copies_in[0].wait()

    def locate(t, carry):
        spot[0, t] = jnp.clip(base[0, t] - px * NX + 1, 0, NX - 1)
        spot[1, t] = jnp.clip(base[1, t] - py * NY + 1, 0, NY - 1) + TOP
        spot[2, t] = jnp.clip(base[2, t] - pz * NZ + 1, 0, NZ - 1)
        return carry

    lax.fori_loop(0, TILES, locate, 0, unroll=8)

    cell = iota((136, LANES), 0) - 1
    wide = iota((136, LANES), 1)
    pick_z[0] = jnp.where(wide == cell + 1, 1.0, 0.0).astype(F32)
    picked = jnp.where((wide >= OWN) & (wide < SPARE) & (wide - OWN + NZ - 1 == cell), 1.0, 0.0).astype(F32)
    wide_channel, _ = lane_roles(wide)
    for kind in range(CHANNELS):
        picked = jnp.where(wide_channel == kind, incoming(kind, cell, NZ, length_z), picked)
    pick_z[1] = picked
    cell = iota((XROWS, LANES), 0) - 1
    for side in range(2):
        pick_x[side] = incoming(3 * side, cell, NX, length_x)
    cell = iota((ROWS, LANES), 0) - TOP - 1
    for side in range(2):
        pick_y[side] = incoming(3 * side, cell, NY, length_y)

    for copy in copies_in[1:]:
        copy.wait()

    def weigh(t, carry):
        w8 = w[0:8, pl.ds(pl.multiple_of(t * LANES, LANES), LANES)]
        first, second, along_y = tile_weights(w8, low)
        along_x = []
        for side in range(2):
            total = None
            for a in range(4):
                term = w8[a : a + 1] * pick_x[side, pl.ds(spot[0, t] + a, 1), :]
                total = term if a == 0 else total + term
            along_x.append(total)
        near_weight[t, 0:8, :] = first
        near_weight[t, 8:16, :] = second
        far_weight[t] = jnp.where(low, along_x[0], along_x[1]) * along_y
        return carry

    lax.fori_loop(0, TILES, weigh, 0, unroll=8)

    for c in range(OWNERS):
        pl.when(px != c)(lambda: received(x_far.at[:, chunk(c), :], x_back_sem, c))
    for side in range(2):
        far[side, 0, 0:LIVE, :] = x_far[side, 0:LIVE, :]
        for yt in range(YT):
            far[side, 1, 8 * yt : 8 * yt + 8, :] = unpack(x_far[side, LIVE:ROWS, :], yt)
        for half in range(2):
            far[side, half, LIVE:ROWS, :] = jnp.zeros((ROWS - LIVE, LANES), F32)
    total = jnp.zeros((8, LANES), F32)
    for side in range(2):
        result = contract([far[side, 0], far[side, 1]])
        for half in range(2):
            values = result[:, LANES * half : LANES * (half + 1)]
            far[side, half] = values[:ROWS]
            for to in range(2):
                far_y[to, half, 4 * side : 4 * side + 4, :] = values[ROWS + 4 * to : ROWS + 4 * to + 4]
        for yt in range(YT):
            j = side * YT + yt
            total = jnp.where(copy_of == j, result[8 * yt : 8 * yt + 8, LANES:], total)
    far_z[...] = total
    far_z_copies = [send(far_z, far_z_in.at[k - 1], fz_sem, k - 1, at_yz(0, k)) for k in range(1, n_gz)]
    far_y_copies = {}
    for ky in range(1, n_gy):
        for kz in range(n_gz):
            index = (ky - 1) * n_gz + kz
            far_y_copies[ky, kz] = send(
                far_y.at[way(py, ky, n_gy)], far_y_in.at[index], fy_sem, index, at_yz(ky, kz)
            )

    def channel_weights(k):
        (left, next_left), (right, next_right) = mix(pz, n_gz, NZ, length_z, k)
        return jnp.where(
            first_kinds,
            jnp.where(is_moment, left, next_left),
            jnp.where(channel >= 3, jnp.where(is_moment, right, next_right), 0.0),
        )

    beside = [jnp.zeros((8, LANES), F32) for _ in range(2)]
    both = [jnp.zeros((8, LANES), F32) for _ in range(2)]
    lines = [[jnp.zeros((8, LANES), F32) for _ in range(XROWS // 8)] for _ in range(2)]
    for ky in range(1, n_gy):
        y_copies[ky - 1].wait_recv()
        y_copies[ky + n_gy - 2].wait_recv()
        weights = mix(py, n_gy, NY, length_y, ky)
        for side in range(2):
            moment, fix = weights[side]
            for tile in range(XROWS // 8):
                lines[side][tile] = lines[side][tile] + moment * y_in[ky - 1, 8 * tile : 8 * tile + 8, :]
            beside[side] = beside[side] + jnp.where(lane < 40, moment, fix) * y_in[ky - 1, SIDE : SIDE + 8, :]
    for right, left in y_fixes:
        pl.when(py > 0)(right.wait_recv)
        pl.when(py + 1 < n_gy)(left.wait_recv)
    for side, valid in enumerate((py > 0, py + 1 < n_gy)):
        for tile in range(XROWS // 8):
            y_mixed[side, 0, 0, 8 * tile : 8 * tile + 8, :] = lines[side][tile]
        for kind in range(1, 3):
            y_mixed[side, kind, 0] = jnp.where(valid, y_fix_in[side, kind - 1], 0.0)
    def expand(half, x, carry):
        for half in (half,):
            line = [
                [y_mixed[side, kind, half, pl.ds(line_row(x), 1), :] for kind in range(3)] for side in range(2)
            ]
            for yt in range(YT):
                rows = slice(8 * yt, 8 * yt + 8)
                value = smooth[x, half, rows, :]
                if half == 1:
                    j = x * YT + yt
                    stack = j // COPIES
                    value = jnp.where(
                        lane < SPARE, value, jnp.where(copy_of == j - stack * COPIES, z_mixed[stack], 0.0)
                    )
                for side in range(2):
                    value = value + pick_y[side, rows, :] * line[side][0]
                if yt == 0:
                    value = value + jnp.where(sub == 4, line[0][1], jnp.where(sub == 5, line[0][2], 0.0))
                if yt == YT - 1:
                    value = value + jnp.where(sub == 6, line[1][1], jnp.where(sub == 5, line[1][2], 0.0))
                smooth[x, half, rows, :] = value
        return carry

    lax.fori_loop(0, WX, functools.partial(expand, 0), 0, unroll=5)
    from_z = [[jnp.zeros((8, LANES), F32) for _ in range(PAIRS)] for _ in range(2)]
    for k in range(1, n_gz):
        z_copies[k - 1].wait_recv()
        z_copies[k + n_gz - 2].wait_recv()
        weights = [jnp.where(is_moment, moment, fix) for moment, fix in mix(pz, n_gz, NZ, length_z, k)]
        for pair in range(PAIRS):
            got = z_in[k - 1, pair_place(pair)]
            for side in range(2):
                from_z[side][pair] = from_z[side][pair] + weights[side] * got
    for pair in range(PAIRS):
        one, two = from_z[0][pair], from_z[1][pair]
        z_mixed[2 * pair] = jnp.where(first_kinds, one, pltpu.roll(two, 3, 1))
        z_mixed[2 * pair + 1] = jnp.where(first_kinds, pltpu.roll(one, LANES - 3, 1), two)
    for ky in range(1, n_gy):
        weights = mix(py, n_gy, NY, length_y, ky)
        for kz in range(1, n_gz):
            d_copies[ky, kz].wait_recv()
            got = channel_weights(kz) * diagonal_in[(ky - 1) * (n_gz - 1) + kz - 1]
            for side in range(2):
                moment, fix = weights[side]
                both[side] = both[side] + jnp.where(copy_of < 5, moment, fix) * got
    for side in range(2):
        for j in range(15):
            kind, xt = divmod(j, 5)
            moved = pltpu.roll(beside[side], LANES - 8 * j, 1) if j else beside[side]
            y_mixed[side, kind, 1, 8 * xt : 8 * xt + 8, :] = jnp.where(
                lane < SPARE, moved, jnp.where(copy_of == j, both[side], 0.0)
            )

    lax.fori_loop(0, WX, functools.partial(expand, 1), 0, unroll=5)

    def tile_spot(t):
        at = pl.ds(pl.multiple_of(t * LANES, LANES), LANES)
        return at, spot[0, t], spot[1, t], spot[2, t]

    def gather(rows, weights, at, z0):
        total = None
        for e in range(4):
            pick = [pick_z[half, pl.ds(z0 + e, 1), :] for half in range(2)]
            inner = None
            for cells, weight in zip(rows, weights):
                taps = jnp.sum(cells[0] * pick[0] + cells[1] * pick[1], axis=1, keepdims=True)
                inner = weight * taps if inner is None else inner + weight * taps
            inner = inner * w[8 + e : 9 + e, at]
            total = inner if e == 0 else total + inner
        return jnp.sum(total, axis=0, keepdims=True)

    def near(t, carry):
        at, x0, y0, z0 = tile_spot(t)
        rows = [
            [
                jnp.where(
                    low, smooth[x0 + a, half, pl.ds(y0, 8), :], smooth[x0 + a + 1, half, pl.ds(y0 - 4, 8), :]
                )
                for half in range(2)
            ]
            for a in (0, 2)
        ]
        sampled[pl.ds(t, 1), :] = gather(rows, (near_weight[t, 0:8, :], near_weight[t, 8:16, :]), at, z0)
        return carry

    lax.fori_loop(0, TILES, near, 0, unroll=32)

    from_z = jnp.zeros((8, LANES), F32)
    for k in range(1, n_gz):
        far_z_copies[k - 1].wait_recv()
        from_z = from_z + channel_weights(k) * far_z_in[k - 1]
    lines = [[jnp.zeros((8, LANES), F32) for _ in range(2)] for _ in range(2)]
    for ky in range(1, n_gy):
        weights = mix(py, n_gy, NY, length_y, ky)
        weights = [jnp.where((sub == 0) | (sub == 4), moment, fix) for moment, fix in weights]
        for kz in range(n_gz):
            far_y_copies[ky, kz].wait_recv()
            index = (ky - 1) * n_gz + kz
            got = [far_y_in[index, half] for half in range(2)]
            if kz == 0:
                got[1] = jnp.where(lane < SPARE, got[1], 0.0)
            else:
                got = [None, jnp.where(copy_of == 0, channel_weights(kz) * got[1], 0.0)]
            for side in range(2):
                for half in range(2):
                    if got[half] is not None:
                        lines[side][half] = lines[side][half] + weights[side] * got[half]
    for x in range(2):
        for half in range(2):
            line = [[lines[side][half][4 * x + kind : 4 * x + kind + 1] for kind in range(3)] for side in range(2)]
            for yt in range(YT):
                rows = slice(8 * yt, 8 * yt + 8)
                value = far[x, half, rows, :]
                if half == 1:
                    value = jnp.where(lane < SPARE, value, jnp.where(copy_of == x * YT + yt, from_z, 0.0))
                for side in range(2):
                    value = value + pick_y[side, rows, :] * line[side][0]
                if yt == 0:
                    value = value + jnp.where(sub == 4, line[0][1], jnp.where(sub == 5, line[0][2], 0.0))
                if yt == YT - 1:
                    value = value + jnp.where(sub == 6, line[1][1], jnp.where(sub == 5, line[1][2], 0.0))
                far[x, half, rows, :] = value

    def distant(t, carry):
        at, x0, y0, z0 = tile_spot(t)
        rows = [jnp.where(low, far[0, half, pl.ds(y0, 8), :], far[1, half, pl.ds(y0 - 4, 8), :]) for half in range(2)]
        sampled[pl.ds(t, 1), :] += gather([rows], [far_weight[t]], at, z0)
        return carry

    lax.fori_loop(0, TILES, distant, 0, unroll=32)

    value = live[...] * (sampled[...] + noise[...] * live_dir[...])
    image[...] = value
    pairs = (
        (live_res[...], live_res[...]),
        (live_dir[...], value),
        (live_res[...], value),
        (value, value),
    )
    place = iota((1, LANES), 1)
    total = jnp.zeros((1, LANES), F32)
    for i, (a, b) in enumerate(pairs):
        part = jnp.sum(jnp.sum(a * b, axis=0, keepdims=True), axis=1, keepdims=True)
        total = jnp.where(place == i, part, total)
    sum_out[...] = total
    copies = [send(sum_out, sum_in_yz.at[k - 1], syz_sem, k - 1, around_yz(k)) for k in range(1, n_yz)]
    for k in range(1, n_yz):
        copies[k - 1].wait_recv()
        total = total + sum_in_yz[k - 1]
    sum_mid[...] = total
    copies = [send(sum_mid, sum_in_x.at[k - 1], sx_sem, k - 1, at_x(k)) for k in range(1, n_gx)]
    for k in range(1, n_gx):
        copies[k - 1].wait_recv()
        total = total + sum_in_x[k - 1]
    sums[...] = total
    for wait in sent:
        wait()

    @pl.when(px < OWNERS)
    def _():
        for q in range(n_gx):
            pl.when(px != q)(back(q).wait_send)


def update_kernel(sums, iterate, live, live_dir, live_res, image, new_iterate, new_residual, new_direction):
    place = iota((1, LANES), 1)

    def total(which):
        return jnp.sum(jnp.where(place == which, sums[...], 0.0), axis=1, keepdims=True)

    norm_old, curvature, cross, square = total(0), total(1), total(2), total(3)
    step = norm_old / curvature
    norm_new = norm_old + step * (step * square - 2.0 * cross)
    held = live_res[...] - step * image[...]
    new_iterate[...] = live[...] * iterate[...] + step * live_dir[...]
    new_residual[...] = held
    new_direction[...] = held + norm_new / norm_old * live_dir[...]


def body(sizes, iterate, residual, direction, noise, stencil_base, interp_weights, tile_counts, reach):
    n_gx, n_gy, n_gz = sizes
    n_yz = n_gy * n_gz
    square = (TILES, LANES)
    in_vmem = pl.BlockSpec(memory_space=pltpu.VMEM)
    in_hbm = pl.BlockSpec(memory_space=pltpu.HBM)
    dma = pltpu.SemaphoreType.DMA

    def away(x):
        return pltpu.with_memory_space_constraint(x, pltpu.HBM)

    def keep(x):
        return pltpu.with_memory_space_constraint(x, pltpu.VMEM)

    grid, live_dir, live_res, live, lengths = pl.pallas_call(
        spread_kernel,
        out_shape=[pltpu.VMEM((WX, 2, ROWS, LANES), F32)] + [pltpu.VMEM(square, F32)] * 3 + [pltpu.VMEM((8, LANES), F32)],
        in_specs=[in_hbm] * 6,
        out_specs=[in_vmem] * 5,
        scratch_shapes=[
            pltpu.VMEM((2, 136, LANES), F32),
            pltpu.SMEM((TILES,), jnp.int32),
            pltpu.SMEM((3, TILES), jnp.int32),
            pltpu.SMEM((3,), F32),
            pltpu.VMEM((12, TILES * LANES), F32),
            pltpu.VMEM(square, F32),
            pltpu.VMEM(square, F32),
            dma((6,)),
        ],
        compiler_params=pltpu.CompilerParams(vmem_limit_bytes=16 << 20),
        name="spread",
    )(
        away(tile_counts),
        away(stencil_base),
        away(reach),
        away(interp_weights),
        away(direction.reshape(square)),
        away(residual.reshape(square)),
    )

    image, sums, kept = pl.pallas_call(
        functools.partial(solve_kernel, sizes),
        out_shape=[pltpu.VMEM(square, F32), pltpu.VMEM((1, LANES), F32), pltpu.VMEM(square, F32)],
        in_specs=[in_hbm] * 4 + [in_vmem] * 5,
        out_specs=[in_vmem] * 3,
        scratch_shapes=[
            pltpu.SMEM((3, TILES), jnp.int32),
            pltpu.SMEM((3, TILES), jnp.int32),
            pltpu.VMEM(square, F32),
            pltpu.VMEM((12, TILES * LANES), F32),
            pltpu.VMEM((WX, 2, ROWS, LANES), F32),
            pltpu.VMEM((96, 3 * ROWS), BF16),
            pltpu.VMEM((2, 136, LANES), F32),
            pltpu.VMEM((2, XROWS, LANES), F32),
            pltpu.VMEM((2, ROWS, LANES), F32),
            pltpu.VMEM((6, LIVE, LANES), F32),
            pltpu.VMEM((6, ROWS, LANES), F32),
            pltpu.VMEM((n_gx, 2, 8, LANES), F32),
            pltpu.VMEM((n_gx, 2, 8, LANES), F32),
            pltpu.VMEM((2, ROWS, LANES), F32),
            pltpu.VMEM((2, 2, ROWS, LANES), F32),
            pltpu.VMEM((2, FIX, LANES), F32),
            pltpu.VMEM((2, 2, XROWS, LANES), F32),
            pltpu.VMEM((2, 3, XROWS, LANES), F32),
            pltpu.VMEM((2, 8, LANES), F32),
            pltpu.VMEM((2, PAIRS, 8, LANES), F32),
            pltpu.VMEM((3, PAIRS, 8, LANES), F32),
            pltpu.VMEM((3, FIX, LANES), F32),
            pltpu.VMEM((2, 2, XROWS, LANES), F32),
            pltpu.VMEM((9, 8, LANES), F32),
            pltpu.VMEM((STACKS, 8, LANES), F32),
            pltpu.VMEM((2, 3, 2, XROWS, LANES), F32),
            pltpu.VMEM((2, 2, ROWS, LANES), F32),
            pltpu.VMEM((8, LANES), F32),
            pltpu.VMEM((2, 2, 8, LANES), F32),
            pltpu.VMEM((3, 8, LANES), F32),
            pltpu.VMEM((12, 2, 8, LANES), F32),
            pltpu.VMEM((TILES, 16, LANES), F32),
            pltpu.VMEM((TILES, 8, LANES), F32),
            pltpu.VMEM(square, F32),
            pltpu.VMEM((1, LANES), F32),
            pltpu.VMEM((15, 1, LANES), F32),
            pltpu.VMEM((1, LANES), F32),
            pltpu.VMEM((15, 1, LANES), F32),
            dma((4,)),
            dma((2, n_gx)),
            dma((2, n_gx)),
            dma((2, 2)),
            dma((2, 6)),
            dma((2, 6)),
            dma((2, 4)),
            dma((2, 9)),
            dma((2, 3)),
            dma((2, 12)),
            dma((2, 15)),
            dma((2, 15)),
        ],
        compiler_params=pltpu.CompilerParams(
            collective_id=0, has_side_effects=True, vmem_limit_bytes=24 << 20
        ),
        name="solve",
    )(
        away(stencil_base),
        away(iterate.reshape(square)),
        away(noise.reshape(square)),
        away(interp_weights),
        keep(lengths),
        keep(grid),
        keep(live_dir),
        keep(live_res),
        keep(live),
    )

    outs = pl.pallas_call(
        update_kernel,
        out_shape=[jax.ShapeDtypeStruct(square, F32)] * 3,
        in_specs=[in_vmem] * 6,
        out_specs=[in_vmem] * 3,
        name="update",
    )(keep(sums), keep(kept), keep(live), keep(live_dir), keep(live_res), keep(image))
    return tuple(out.reshape(-1) for out in outs)


def solution(mesh):
    sizes = tuple(mesh.shape[axis] for axis in ("gx", "gy", "gz"))
    lines = P(("gx", "gy", "gz"))
    return jax.shard_map(
        functools.partial(body, sizes),
        mesh=mesh,
        in_specs=(lines, lines, lines, lines, P(None, ("gx", "gy", "gz")), P(None, ("gx", "gy", "gz")), lines, P()),
        out_specs=(lines, lines, lines),
        check_vma=False,
    )
```
